32 devices in a mesh: fsdp: 8 (over z, y), seq: 4 (over x, core).
Axes of the slice: x: 2, y: 2, z: 4, core: 2. Of those that a mesh axis runs over, the one named last changes fastest.
Arguments:
- block_in: float32 [16, 580, 768], P('fsdp', 'seq'), may hold values from -6 to 6
- teacher: float32 [16, 580, 768], P('fsdp', 'seq'), may hold values from -6 to 6
- image_counts: int32 [8], replicated, may hold values from 1 to 2, as said below
- expert_ids: int32 [4, 16, 145, 2], P('seq', 'fsdp'), may hold values from 0 to 3, all different within a row; in each aligned block of 290 rows (0 to 289, 290 to 579, ..., all dimensions but the last counted through in order) at most 164 rows name the same one
- pair_keep: int32 [4, 16, 145, 2], P('seq', 'fsdp'), may hold values 0 or 1
- norm1_gain: bfloat16 [768], P('fsdp'), may hold values from 0.25 to 1.75
- norm1_bias: bfloat16 [768], P('fsdp'), may hold values from -1.1953125 to 1.1953125
- qkv_weight: bfloat16 [768, 2304], P('fsdp'), may hold values from -0.3125 to 0.3125
- out_weight: bfloat16 [768, 768], P('fsdp'), may hold values from -0.5 to 0.5
- norm2_gain: bfloat16 [768], P('fsdp'), may hold values from 0.25 to 1.75
- norm2_bias: bfloat16 [768], P('fsdp'), may hold values from -1.1953125 to 1.1953125
- router_weight: bfloat16 [768, 4], P('fsdp'), may hold values from -0.15625 to 0.15625
- expert_in: bfloat16 [768, 4, 3072], P('fsdp'), may hold values from -0.21875 to 0.21875
- expert_out: bfloat16 [3072, 4, 768], P('fsdp'), may hold values from -0.625 to 0.625
Outputs:
- block_out: float32 [16, 580, 768], P('fsdp', 'seq')
- mean_loss: float32 [], replicated
- grad_block_in: float32 [16, 580, 768], P('fsdp', 'seq')
- grad_norm1_gain: float32 [768], P('fsdp')
- grad_norm1_bias: float32 [768], P('fsdp')
- grad_qkv_weight: float32 [768, 2304], P('fsdp')
- grad_out_weight: float32 [768, 768], P('fsdp')
- grad_norm2_gain: float32 [768], P('fsdp')
- grad_norm2_bias: float32 [768], P('fsdp')
- grad_router_weight: float32 [768, 4], P('fsdp')
- grad_expert_in: float32 [768, 4, 3072], P('fsdp')
- grad_expert_out: float32 [3072, 4, 768], P('fsdp')
The draws below stay inside these ranges and needn't reach their ends.
Inputs may be any that keep to these rules, and one draw needn't show every extreme that they name: `image_counts`: some group holds 2 images. `expert_ids`: the 2 experts of a slot differ; in the slots of one device (aligned blocks of 290 rows, leading dimensions taken together in order) no expert is named by more than 164 rows, a bound that some block reaches.
All inputs are finite; a program needn't handle non-finite values. No bound on the sum of `pair_keep` on one device may be relied on, other than what follows from the above.
Results may differ from the reference program's by a relative error of at most 0.013.
The reference program's roundings to bfloat16 on the way count: a program that leaves them out, or rounds other values in their place, can miss the bound.
Values may be sent and summed in bfloat16 or wider, within the bound.
A program may use at most 320 MiB of HBM per device.

```python
import math
import jax
import jax.numpy as jnp
import numpy as np
from jax import lax

D = 768
HEADS = 12
HD = 64
FF = 3072
SEQ_LEN = 577
EXPERTS = 4
TOPK = 2
IMG = 2
GROUPS = 8
SEQ_PIECES = 4
PIECE = 145
SEQ_SLOTS = 580
IMAGES = 16
CAP = 164


def draw_image_counts(key, part):
    key_short, key_full = jax.random.split(key)
    shorter = jax.random.randint(key_short, (GROUPS,), 0, 2)
    full_group = jax.random.randint(key_full, (), 0, GROUPS)
    counts = IMG - shorter
    counts = jnp.where(jnp.arange(GROUPS) == full_group, IMG, counts)
    return jnp.maximum(counts, 1).astype(jnp.int32)


def plant(values, stream_key, least, largest):
    extent = values.shape
    index_at = [jax.random.randint(jax.random.fold_in(stream_key, axis), (), 0, extent[axis]) for axis in range(len(extent))]
    values = values.at[tuple(index_at)].set(least)
    longest = extent.index(max(extent))
    index_at[longest] = (index_at[longest] + 1) % extent[longest]
    return values.at[tuple(index_at)].set(largest)


def strengthened(array, stream_key, source, target, shards_of, factor):
    owner, partner = [(jnp.arange(array.shape[position]) // (array.shape[position] // shards_of)).reshape([-1 if axis == position else 1 for axis in range(array.ndim)]) for position in (source, target)]
    chosen = jax.random.permutation(stream_key, shards_of)[partner]
    strong = (owner == chosen) | (owner == (partner + shards_of // 2) % shards_of)
    return jnp.where(strong, factor * array, array)


def shard_levels(stream_key, extent, cuts, low, top_value):
    gain, own = 1.0, jax.random.fold_in(stream_key, 6)
    for axis_at, blocks in cuts:
        heights = jnp.exp(jax.random.uniform(jax.random.fold_in(own, axis_at), (blocks,), jnp.float32, low / len(cuts), top_value / len(cuts)))
        gain = gain * jnp.repeat(heights, extent[axis_at] // blocks).reshape([-1 if axis == axis_at else 1 for axis in range(len(extent))])
    return gain


def deal_out(stream_key, own, number, rows, number_of, top, reach, skew):
    ranking = jax.random.permutation(stream_key, number_of)
    heavy_load, ordinary = load_shares(number_of, rows * top, reach, skew, True), load_shares(number_of, rows * top, reach, skew, False)
    places = jnp.arange(number_of)

    def named(sizes, rotation):
        used = int((sizes > 0).sum())
        fixed = max(1, used // 4)
        shifted = fixed + (places - fixed + rotation * (used - fixed)) % max(1, number_of - fixed)
        return jnp.zeros((number_of,), jnp.int32).at[ranking[jnp.where(places < fixed, places, shifted)]].set(jnp.asarray(sizes, jnp.int32))

    sizes = jnp.where(number % 4 == 0, named(heavy_load, number // 4), named(ordinary, number - number // 4 - 1))
    mixed = jax.random.permutation(jax.random.fold_in(own, 3), number_of)
    donor, taker = mixed[0:number_of // 2 * 2:2], mixed[1:number_of // 2 * 2:2]
    margin = jnp.minimum(sizes[donor] - 1, reach - sizes[taker]) // 2
    margin = jnp.where((donor == ranking[0]) | (taker == ranking[0]) | (sizes[taker] == 0), 0, jnp.maximum(margin, 0))
    shifted = jax.random.randint(jax.random.fold_in(own, 4), (number_of // 2,), 0, 1 << 20) % (margin + 1)
    sizes = sizes.at[donor].add(-shifted).at[taker].add(shifted)
    items = jnp.searchsorted(jnp.cumsum(sizes), jnp.arange(rows * top), side="right").astype(jnp.int32)
    table = items.reshape(top, rows).T
    table = table[jax.random.permutation(jax.random.fold_in(own, 1), rows)]
    rotation = jax.random.randint(jax.random.fold_in(own, 2), (rows, 1), 0, top)
    return jnp.take_along_axis(table, (jnp.arange(top)[None, :] + rotation) % top, axis=1)


def load_shares(amount, total, bound, skew, full):
    portions = [(1 << 20) // math.isqrt(grade ** skew) + 1 for grade in range(1, amount + 1)]
    largest = bound if full else min(bound, max(-(-total // amount), total * portions[0] // sum(portions)))
    least = 1 if total - largest >= amount - 1 else 0
    holding, surplus = [largest] + [least] * (amount - 1), total - largest - least * (amount - 1)
    while surplus > 0:
        movable = [i for i in range(1, amount) if holding[i] < largest] or [i for i in range(1, amount) if holding[i] < bound]
        pool, left = sum([portions[i] for i in movable]), surplus
        for i in movable:
            more = min(bound - holding[i], max(1, left * portions[i] // pool), surplus)
            holding[i] = holding[i] + more
            surplus = surplus - more
    return np.array(holding)


def gaussian(key, dims, spread, limit, cuts=(), held_as=jnp.bfloat16):
    drawn = jax.random.normal(key, dims, jnp.float32) * spread
    if len(cuts) > 0:
        drawn = shard_levels(key, dims, cuts, -0.22, 0.18) * drawn
    return jnp.clip(drawn, min=-limit, max=limit).astype(held_as)


def gaussian_with(key, dims, width, limit, cuts, heavy, kind=jnp.bfloat16):
    drawn = width * jax.random.normal(key, dims, jnp.float32)
    if cuts:
        drawn = drawn * shard_levels(key, dims, cuts, -0.22, 0.18)
    return jnp.clip(strengthened(drawn, jax.random.fold_in(key, 3), *heavy), -limit, limit).astype(kind)


def setup_inputs(seed: int = 0) -> dict:
    splits = jax.random.split(jax.random.key(seed), 15)
    block_in = gaussian_with(splits[0], (IMAGES, SEQ_SLOTS, D), 1.0, 6.0, ((0, 8), (1, 4)), (0, 2, 8, 2.0), jnp.float32)
    teacher = gaussian(splits[1], (IMAGES, SEQ_SLOTS, D), 1.0, 6.0, ((0, 8), (1, 4)), jnp.float32)
    image_counts = draw_image_counts(jax.random.fold_in(splits[14], 71), 0)
    expert_ids_keys = jax.random.split(jax.random.fold_in(splits[3], 1), SEQ_PIECES * IMAGES * PIECE // (IMG * PIECE))
    expert_ids_turns = jax.random.permutation(jax.random.fold_in(splits[3], 3), SEQ_PIECES * IMAGES * PIECE // (IMG * PIECE))
    expert_ids = jax.vmap(lambda own, number: deal_out(jax.random.fold_in(splits[3], 2), own, number, IMG * PIECE, EXPERTS, TOPK, CAP, 0))(expert_ids_keys, expert_ids_turns).reshape((SEQ_PIECES, IMAGES, PIECE, TOPK))
    pair_keep = plant((jax.random.randint(splits[4], (SEQ_PIECES, IMAGES, PIECE, TOPK), 0, 8) < 7).astype(jnp.int32), jax.random.fold_in(splits[4], 1), 0, 1)
    norm1_gain = jnp.clip(1.0 + 0.15 * jax.random.normal(splits[5], (D,), jnp.float32), 0.25, 1.75).astype(jnp.bfloat16)
    norm1_bias = gaussian(splits[6], (D,), 0.2, 1.1953125, ((0, 8),))
    qkv_weight = gaussian(splits[7], (D, 3 * D), (D // 2) ** -0.5, 0.3125, ((0, 8),))
    out_weight = gaussian(splits[8], (D, D), (D // 6) ** -0.5, 0.5, ((0, 8),))
    norm2_gain = jnp.clip(1.0 + 0.15 * jax.random.normal(splits[9], (D,), jnp.float32), 0.25, 1.75).astype(jnp.bfloat16)
    norm2_bias = gaussian(splits[10], (D,), 0.2, 1.1953125, ((0, 8),))
    router_weight = gaussian(splits[11], (D, EXPERTS), (2 * D) ** -0.5, 0.15625, ((0, 8),))
    expert_in = gaussian(splits[12], (D, EXPERTS, FF), D ** -0.5, 0.21875, ((0, 8),))
    expert_out = gaussian(splits[13], (FF, EXPERTS, D), (FF // 32) ** -0.5, 0.625, ((0, 8),))
    return dict(block_in=block_in, teacher=teacher, image_counts=image_counts, expert_ids=expert_ids, pair_keep=pair_keep, norm1_gain=norm1_gain, norm1_bias=norm1_bias, qkv_weight=qkv_weight, out_weight=out_weight, norm2_gain=norm2_gain, norm2_bias=norm2_bias, router_weight=router_weight, expert_in=expert_in, expert_out=expert_out)


@jax.custom_vjp
def low(v):
    return lax.optimization_barrier(v.astype(jnp.bfloat16)).astype(jnp.float32)

@jax.custom_vjp
def low_back(v):
    return v

def low_keep(v):
    return (low(v), None)

def low_pass(kept, grad):
    return (grad,)

def back_keep(v):
    return (v, None)

def back_low(kept, grad):
    return (low(grad),)
low.defvjp(low_keep, low_pass)
low_back.defvjp(back_keep, back_low)
NORM_EPS = 1e-06
PRECISE = lax.Precision.HIGHEST

def layer_norm(values_in, gain_vec, bias_vec):
    centered = values_in - lax.optimization_barrier(jnp.mean(values_in, axis=-1, keepdims=True))
    variance = lax.optimization_barrier(jnp.mean(centered * centered, axis=-1, keepdims=True))
    return centered * lax.rsqrt(variance + NORM_EPS) * gain_vec + bias_vec

def slot_holds(piece_index, piece_len, seq_len, pieces):
    lengths = seq_len // pieces + (piece_index < seq_len % pieces).astype(jnp.int32)
    return jnp.arange(piece_len, dtype=jnp.int32)[None, :] < lengths[:, None]

def route_slots(expert_rows, usable, experts, capacity):
    expert_hits = ((expert_rows[:, :, None] == jnp.arange(experts, dtype=jnp.int32)[None, None, :]) & usable[:, :, None]).astype(jnp.int32)
    flat_hits = expert_hits.reshape(-1, experts)
    earlier = (jnp.cumsum(flat_hits, axis=0, dtype=jnp.int32) - flat_hits).reshape(expert_hits.shape)
    within = lax.optimization_barrier(jnp.sum(earlier * expert_hits, axis=2, dtype=jnp.int32))
    return jnp.where(usable, expert_rows * capacity + within, experts * capacity).astype(jnp.int32)

def slot_pairs(slot_index, experts, capacity):
    pair_total = slot_index.size
    slot_table = jnp.full((experts * capacity + 1,), pair_total, jnp.int32)
    return slot_table.at[slot_index.reshape(-1)].set(jnp.arange(pair_total, dtype=jnp.int32))[:experts * capacity]

def to_devices(array_in):
    last_dim = array_in.shape[-1]
    grouped = array_in.reshape(GROUPS, IMG, SEQ_PIECES, PIECE, last_dim).transpose(2, 0, 1, 3, 4)
    return grouped.reshape(SEQ_PIECES * GROUPS, IMG * PIECE, last_dim)

def from_devices(array_in):
    last_dim = array_in.shape[-1]
    grouped = array_in.reshape(SEQ_PIECES, GROUPS, IMG, PIECE, last_dim).transpose(1, 2, 0, 3, 4)
    return grouped.reshape(IMAGES, SEQ_SLOTS, last_dim)

def attend_group(queries, key_rows, value_rows, key_ok):
    scores = low_back(jnp.einsum('iqhd,ikhd->ihqk', queries, key_rows, precision=PRECISE) * HD ** (-0.5))
    scores = jnp.where(key_ok[None, None, None, :], scores, -1e+30)
    shares = low(jax.nn.softmax(scores, axis=-1))
    return jnp.einsum('ihqk,ikhd->iqhd', shares, value_rows, precision=PRECISE)

def expert_device(normed_rows, prob_rows, expert_rows, usable, expert_in, expert_out):
    slot_index = route_slots(expert_rows, usable, EXPERTS, CAP)
    pair_of_slot = slot_pairs(slot_index, EXPERTS, CAP)
    padded_rows = jnp.concatenate([normed_rows, jnp.zeros((1, D), jnp.float32)], axis=0)
    dispatched = padded_rows[pair_of_slot // TOPK].reshape(EXPERTS, CAP, D)
    hidden = low_back(jnp.einsum('ecd,def->ecf', dispatched, expert_in, precision=PRECISE))
    activated = low(jax.nn.gelu(hidden, approximate=False))
    returned = low_back(jnp.einsum('ecf,fed->ecd', activated, expert_out, precision=PRECISE))
    flat_back = jnp.concatenate([returned.reshape(EXPERTS * CAP, D), jnp.zeros((1, D), jnp.float32)], axis=0)
    picked = flat_back[slot_index]
    chosen = expert_rows[:, :, None] == jnp.arange(EXPERTS, dtype=jnp.int32)[None, None, :]
    gate_values = lax.optimization_barrier(jnp.sum(jnp.where(chosen, prob_rows[:, None, :], 0.0), axis=2))
    pair_weight = jnp.where(usable, gate_values, 0.0)
    return lax.optimization_barrier(jnp.sum(pair_weight[:, :, None] * picked, axis=1))

def forward(block_in, gain_one, bias_one, qkv_weight, out_weight, gain_two, bias_two, router_weight, expert_in, expert_out, key_ok, pair_ok, expert_rows):
    normed_one = low(layer_norm(block_in, gain_one, bias_one))
    projected = low_back(low(jnp.einsum('isd,dc->isc', normed_one, qkv_weight, precision=PRECISE)))
    split_heads = projected.reshape(GROUPS, IMG, SEQ_SLOTS, 3, HEADS, HD)

    def attend_one(group_block):
        return attend_group(group_block[:, :, 0], group_block[:, :, 1], group_block[:, :, 2], key_ok)
    context = lax.map(jax.checkpoint(attend_one), split_heads)
    context = low_back(low(context.reshape(IMAGES, SEQ_SLOTS, D)))
    attended = low_back(jnp.einsum('isd,de->ise', context, out_weight, precision=PRECISE))
    middle = block_in + attended
    normed_two = low(layer_norm(middle, gain_two, bias_two))
    routed = jax.nn.softmax(jnp.einsum('isd,de->ise', normed_two, router_weight, precision=PRECISE), axis=-1)

    def per_device(device_item):
        return jax.checkpoint(expert_device)(device_item[0], device_item[1], device_item[2], device_item[3], expert_in, expert_out)
    mixture = lax.map(per_device, (to_devices(normed_two), to_devices(routed), expert_rows, pair_ok))
    return middle + from_devices(mixture)

def reference(block_in, teacher, image_counts, expert_ids, pair_keep, norm1_gain, norm1_bias, qkv_weight, out_weight, norm2_gain, norm2_bias, router_weight, expert_in, expert_out):
    piece_ids = jnp.arange(SEQ_PIECES, dtype=jnp.int32)
    key_ok = slot_holds(piece_ids, PIECE, SEQ_LEN, SEQ_PIECES).reshape(SEQ_SLOTS)
    image_ok = jnp.arange(IMAGES, dtype=jnp.int32) % IMG < jnp.repeat(image_counts, IMG, total_repeat_length=IMAGES)
    token_ok = image_ok[:, None] & key_ok[None, :]
    expert_rows = expert_ids.reshape(SEQ_PIECES * GROUPS, IMG * PIECE, TOPK)
    pair_ok = (pair_keep.reshape(SEQ_PIECES * GROUPS, IMG * PIECE, TOPK) == 1) & to_devices(token_ok[:, :, None])
    gain_one = norm1_gain.astype(jnp.float32)
    bias_one = norm1_bias.astype(jnp.float32)
    qkv_f = qkv_weight.astype(jnp.float32)
    out_f = out_weight.astype(jnp.float32)
    gain_two = norm2_gain.astype(jnp.float32)
    bias_two = norm2_bias.astype(jnp.float32)
    router_f = router_weight.astype(jnp.float32)
    in_f = expert_in.astype(jnp.float32)
    down_f = expert_out.astype(jnp.float32)

    def whole_layer(input_rows, g_one, b_one, w_qkv_f, w_out_f, g_two, b_two, w_router_f, w_in_f, w_down_f):
        return forward(input_rows, g_one, b_one, w_qkv_f, w_out_f, g_two, b_two, w_router_f, w_in_f, w_down_f, key_ok, pair_ok, expert_rows)
    block_out, pullback = jax.vjp(whole_layer, block_in, gain_one, bias_one, qkv_f, out_f, gain_two, bias_two, router_f, in_f, down_f)
    token_weight = token_ok[:, :, None].astype(jnp.float32)
    misfit = (block_out - teacher) * token_weight
    gradients = pullback(misfit)
    mean_loss = jnp.sum(misfit * misfit) / ((jnp.sum(image_counts, dtype=jnp.int32) * SEQ_LEN).astype(jnp.float32) * D)
    return (block_out, mean_loss, gradients[0], gradients[1], gradients[2], gradients[3], gradients[4], gradients[5], gradients[6], gradients[7], gradients[8], gradients[9])
```

```python
import jax
import jax.numpy as jnp
from jax import lax
from jax.sharding import PartitionSpec as P

HEADS = 12
HD = 64
SEQ_LEN = 577
EXPERTS = 4
TOPK = 2
NORM_EPS = 1e-06
PRECISE = lax.Precision.HIGHEST
F32 = jnp.float32
BF16 = jnp.bfloat16


def layer_norm(values_in, gain_vec, bias_vec):
    centered = values_in - jnp.mean(values_in, axis=-1, keepdims=True)
    variance = jnp.mean(centered * centered, axis=-1, keepdims=True)
    root = lax.rsqrt(variance + NORM_EPS)
    unit = centered * root
    return unit * gain_vec + bias_vec, unit, root


def layer_norm_back(grad_out, unit, root, gain_vec):
    scaled = grad_out * gain_vec
    return root * (
        scaled
        - jnp.mean(scaled, axis=-1, keepdims=True)
        - unit * jnp.mean(scaled * unit, axis=-1, keepdims=True)
    )


def slot_holds(piece_index, piece_len, seq_len, pieces):
    lengths = seq_len // pieces + (piece_index < seq_len % pieces).astype(jnp.int32)
    return jnp.arange(piece_len, dtype=jnp.int32)[None, :] < lengths[:, None]


def dot32(left, right, dims):
    return lax.dot_general(left, right, (dims, ((), ())), preferred_element_type=F32)


def on_device(
    block_in,
    teacher,
    image_counts,
    expert_ids,
    pair_keep,
    norm1_gain,
    norm1_bias,
    qkv_weight,
    out_weight,
    norm2_gain,
    norm2_bias,
    router_weight,
    expert_in,
    expert_out,
):
    images, piece_len, features = block_in.shape
    pieces = lax.axis_size("seq")
    groups = lax.axis_size("fsdp")
    seq_place = lax.axis_index("seq")
    group_place = lax.axis_index("fsdp")
    rows = images * piece_len
    slots = pieces * piece_len
    heads_here = HEADS // pieces
    cols = heads_here * HD
    hidden_size = expert_in.shape[2]
    capacity = rows * TOPK * 9 // (EXPERTS * 8) + 1
    inv_root = HD ** (-0.5)
    in_rows = expert_in.shape[0]
    out_rows = expert_out.shape[0]

    small = jnp.concatenate(
        [
            jnp.stack([norm1_gain, norm1_bias, norm2_gain, norm2_bias], axis=1),
            router_weight,
            out_weight,
            lax.dynamic_index_in_dim(
                qkv_weight.reshape(-1, 3, pieces, cols), seq_place, 2, keepdims=False
            ).reshape(-1, 3 * cols),
        ],
        axis=1,
    )
    small_full = lax.all_gather(small, "fsdp", axis=0, tiled=True)
    gain_one, bias_one, gain_two, bias_two = [small_full[:, i].astype(F32) for i in range(4)]
    router_full = small_full[:, 4 : 4 + EXPERTS]
    out_full = small_full[:, 4 + EXPERTS : 4 + EXPERTS + features]
    qkv_here = small_full[:, 4 + EXPERTS + features :]
    up_here = lax.all_gather(
        lax.dynamic_index_in_dim(expert_in, seq_place, 1, keepdims=False), "fsdp", axis=0, tiled=True
    )
    down_here = lax.all_gather(
        lax.dynamic_index_in_dim(expert_out, seq_place, 1, keepdims=False), "fsdp", axis=0, tiled=True
    )

    own_slots = slot_holds(jnp.reshape(seq_place, (1,)), piece_len, SEQ_LEN, pieces).reshape(piece_len)
    key_ok = slot_holds(jnp.arange(pieces, dtype=jnp.int32), piece_len, SEQ_LEN, pieces).reshape(slots)
    group_count = jnp.sum(
        jnp.where(jnp.arange(image_counts.shape[0], dtype=jnp.int32) == group_place, image_counts, 0)
    )
    token_ok = (
        (jnp.arange(images, dtype=jnp.int32) < group_count)[:, None] & own_slots[None, :]
    ).reshape(rows)

    flat_in = block_in.reshape(rows, features)
    normed_one, unit_one, root_one = layer_norm(flat_in, gain_one, bias_one)
    low_one = normed_one.astype(BF16)
    low_all = lax.all_gather(low_one.reshape(images, piece_len, features), "seq", axis=1, tiled=True)
    projected = dot32(low_all, qkv_here, ((2,), (0,))).astype(BF16)
    by_heads = projected.reshape(images, slots, 3, heads_here, HD).transpose(2, 0, 3, 1, 4)
    queries, key_rows, value_rows = by_heads[0], by_heads[1], by_heads[2]
    scores = jnp.einsum("ihqd,ihkd->ihqk", queries, key_rows, preferred_element_type=F32) * inv_root
    scores = jnp.where(key_ok[None, None, None, :], scores, -1e30)
    raised = jnp.exp(scores - jnp.max(scores, axis=-1, keepdims=True))
    attn = raised / jnp.sum(raised, axis=-1, keepdims=True)
    attn_low = attn.astype(BF16)
    context = jnp.einsum("ihqk,ihkd->iqhd", attn_low, value_rows, preferred_element_type=F32).astype(BF16)
    context_rows = lax.all_to_all(
        context.reshape(images, slots, 1, cols), "seq", split_axis=1, concat_axis=2, tiled=True
    ).reshape(rows, features)
    middle = flat_in + dot32(context_rows, out_full, ((1,), (0,)))
    normed_two, unit_two, root_two = layer_norm(middle, gain_two, bias_two)
    low_two = normed_two.astype(BF16)
    probs = jax.nn.softmax(dot32(low_two, router_full, ((1,), (0,))), axis=-1)

    expert_rows = expert_ids.reshape(rows, TOPK)
    usable = (pair_keep.reshape(rows, TOPK) == 1) & token_ok[:, None]
    hit = jnp.any(
        (expert_rows[:, :, None] == jnp.arange(EXPERTS, dtype=jnp.int32)) & usable[:, :, None], axis=1
    )
    earlier = (jnp.arange(rows)[:, None] > jnp.arange(rows)[None, :]).astype(BF16)
    place = dot32(earlier, hit.astype(BF16), ((1,), (0,))).astype(jnp.int32)
    place = jnp.where(hit, place, -1)
    select = (place.T[:, None, :] == jnp.arange(capacity, dtype=jnp.int32)[None, :, None]).astype(BF16)
    weight = jnp.where(hit, probs, 0.0)

    dispatched = dot32(select, low_two, ((2,), (0,))).astype(BF16)
    arrived = lax.all_to_all(dispatched, "seq", split_axis=0, concat_axis=0, tiled=True)
    arrived = arrived.reshape(pieces * capacity, features)
    hidden = dot32(arrived, up_here, ((1,), (0,)))
    activated, gelu_back = jax.vjp(lambda u: jax.nn.gelu(u, approximate=False), hidden)
    low_act = activated.astype(BF16)
    returned = dot32(low_act, down_here, ((1,), (0,))).astype(BF16)
    returned = lax.all_to_all(
        returned.reshape(pieces, capacity, features), "seq", split_axis=0, concat_axis=0, tiled=True
    )
    picked = jnp.einsum("est,esd->etd", select, returned, preferred_element_type=F32)
    block_out = middle + jnp.sum(weight.T[:, :, None] * picked, axis=0)
    misfit = (block_out - teacher.reshape(rows, features)) * token_ok.astype(F32)[:, None]
    loss_here = jnp.sum(misfit * misfit)

    pair_grad = (weight.T[:, :, None] * misfit[None]).astype(BF16)
    returned_grad = jnp.einsum("est,etd->esd", select, pair_grad, preferred_element_type=F32).astype(BF16)
    prob_grad = jnp.where(hit, jnp.sum(picked * misfit[None], axis=2).T, 0.0)
    grad_arrived = lax.all_to_all(returned_grad, "seq", split_axis=0, concat_axis=0, tiled=True).reshape(
        pieces * capacity, features
    )
    hidden_grad = gelu_back(dot32(grad_arrived, down_here, ((1,), (1,))))[0].astype(BF16)
    grad_down = dot32(low_act, grad_arrived, ((0,), (0,))).astype(BF16)
    grad_up = dot32(arrived, hidden_grad, ((0,), (0,))).astype(BF16)
    dispatch_grad = dot32(hidden_grad, up_here, ((1,), (1,))).astype(BF16)
    dispatch_grad = lax.all_to_all(
        dispatch_grad.reshape(pieces, capacity, features), "seq", split_axis=0, concat_axis=0, tiled=True
    )
    owned_down = lax.psum_scatter(grad_down, "fsdp", scatter_dimension=0, tiled=True)
    owned_up = lax.psum_scatter(grad_up, "fsdp", scatter_dimension=0, tiled=True)

    logit_grad = probs * (prob_grad - jnp.sum(probs * prob_grad, axis=1, keepdims=True))
    grad_router = lax.dot_general(
        low_two.astype(F32), logit_grad, (((0,), (0,)), ((), ())), precision=PRECISE
    )
    normed_two_grad = jnp.einsum("est,esd->td", select, dispatch_grad, preferred_element_type=F32)
    normed_two_grad = normed_two_grad + lax.dot_general(
        logit_grad, router_full.astype(F32), (((1,), (1,)), ((), ())), precision=PRECISE
    )
    grad_gain_two = jnp.sum(normed_two_grad * unit_two, axis=0)
    grad_bias_two = jnp.sum(normed_two_grad, axis=0)
    middle_grad = misfit + layer_norm_back(normed_two_grad, unit_two, root_two, gain_two)
    attended_grad = middle_grad.astype(BF16)
    grad_out_w = dot32(context_rows, attended_grad, ((0,), (0,))).astype(BF16)
    context_grad = dot32(attended_grad, out_full, ((1,), (1,))).astype(BF16)
    heads_grad = lax.all_to_all(
        context_grad.reshape(images, piece_len, pieces, cols), "seq", split_axis=2, concat_axis=1, tiled=True
    ).reshape(images, slots, heads_here, HD)
    value_grad = jnp.einsum("ihqk,iqhd->ikhd", attn_low, heads_grad, preferred_element_type=F32)
    share_grad = jnp.einsum("iqhd,ihkd->ihqk", heads_grad, value_rows, preferred_element_type=F32)
    score_grad = (attn * (share_grad - jnp.sum(attn * share_grad, axis=-1, keepdims=True))).astype(BF16)
    query_grad = jnp.einsum("ihqk,ihkd->iqhd", score_grad, key_rows, preferred_element_type=F32) * inv_root
    key_grad = jnp.einsum("ihqk,ihqd->ikhd", score_grad, queries, preferred_element_type=F32) * inv_root
    heads_back = jnp.stack([query_grad, key_grad, value_grad], axis=2).astype(BF16)
    heads_back = heads_back.reshape(images * slots, 3 * cols)
    grad_qkv = dot32(low_all.reshape(images * slots, features), heads_back, ((0,), (0,))).astype(BF16)
    normed_one_part = dot32(heads_back, qkv_here, ((1,), (1,))).astype(BF16)
    normed_one_grad = lax.psum_scatter(
        normed_one_part.reshape(images, slots, features), "seq", scatter_dimension=1, tiled=True
    ).astype(F32).reshape(rows, features)
    grad_gain_one = jnp.sum(normed_one_grad * unit_one, axis=0)
    grad_bias_one = jnp.sum(normed_one_grad, axis=0)
    input_grad = middle_grad + layer_norm_back(normed_one_grad, unit_one, root_one, gain_one)

    out_share = lax.psum_scatter(grad_out_w, "seq", scatter_dimension=1, tiled=True)
    attn_owned = lax.psum_scatter(
        jnp.concatenate([grad_qkv, out_share], axis=1), "fsdp", scatter_dimension=0, tiled=True
    )
    loss_row = jnp.zeros((features,), F32).at[0].set(loss_here)
    vectors = jnp.concatenate(
        [jnp.stack([grad_gain_one, grad_bias_one, grad_gain_two, grad_bias_two, loss_row]), grad_router.T], axis=0
    )
    vectors = lax.psum(vectors, ("fsdp", "seq"))
    mean_loss = vectors[4, 0] / (
        (jnp.sum(image_counts, dtype=jnp.int32) * SEQ_LEN).astype(F32) * features
    )
    owned_vectors = lax.dynamic_slice_in_dim(vectors, group_place * in_rows, in_rows, axis=1)
    attn_whole = lax.all_gather(attn_owned, "seq", axis=0)
    grad_qkv_w = (
        attn_whole[:, :, : 3 * cols].reshape(pieces, in_rows, 3, cols).transpose(1, 2, 0, 3)
        .reshape(in_rows, 3 * features).astype(F32)
    )
    grad_out_whole = attn_whole[:, :, 3 * cols :].transpose(1, 0, 2).reshape(in_rows, features).astype(F32)
    grad_up_w = lax.all_gather(owned_up, "seq", axis=0).transpose(1, 0, 2).astype(F32)
    grad_down_w = lax.all_gather(owned_down, "seq", axis=0).transpose(1, 0, 2).astype(F32)
    return (
        block_out.reshape(images, piece_len, features),
        mean_loss,
        input_grad.reshape(images, piece_len, features),
        owned_vectors[0],
        owned_vectors[1],
        grad_qkv_w,
        grad_out_whole,
        owned_vectors[2],
        owned_vectors[3],
        owned_vectors[5:].T,
        grad_up_w,
        grad_down_w,
    )


def solution(mesh):
    return jax.shard_map(
        on_device,
        mesh=mesh,
        in_specs=(
            P("fsdp", "seq", None),
            P("fsdp", "seq", None),
            P(),
            P("seq", "fsdp", None, None),
            P("seq", "fsdp", None, None),
            P("fsdp"),
            P("fsdp"),
            P("fsdp", None),
            P("fsdp", None),
            P("fsdp"),
            P("fsdp"),
            P("fsdp", None),
            P("fsdp", None, None),
            P("fsdp", None, None),
        ),
        out_specs=(
            P("fsdp", "seq", None),
            P(),
            P("fsdp", "seq", None),
            P("fsdp"),
            P("fsdp"),
            P("fsdp", None),
            P("fsdp", None),
            P("fsdp"),
            P("fsdp"),
            P("fsdp", None),
            P("fsdp", None, None),
            P("fsdp", None, None),
        ),
        check_vma=False,
    )
```

```python
import jax
import jax.numpy as jnp
from jax import lax
from jax.experimental import pallas as pl
from jax.experimental.pallas import tpu as pltpu
from jax.sharding import PartitionSpec as P

HEADS = 12
HD = 64
SEQ_LEN = 577
EXPERTS = 4
TOPK = 2
NORM_EPS = 1e-06
PRECISE = lax.Precision.HIGHEST
F32 = jnp.float32
BF16 = jnp.bfloat16


def layer_norm(values_in, gain_vec, bias_vec):
    centered = values_in - jnp.mean(values_in, axis=-1, keepdims=True)
    variance = jnp.mean(centered * centered, axis=-1, keepdims=True)
    root = lax.rsqrt(variance + NORM_EPS)
    unit = centered * root
    return unit * gain_vec + bias_vec, unit, root


def layer_norm_back(grad_out, unit, root, gain_vec):
    scaled = grad_out * gain_vec
    return root * (
        scaled
        - jnp.mean(scaled, axis=-1, keepdims=True)
        - unit * jnp.mean(scaled * unit, axis=-1, keepdims=True)
    )


def slot_holds(piece_index, piece_len, seq_len, pieces):
    lengths = seq_len // pieces + (piece_index < seq_len % pieces).astype(jnp.int32)
    return jnp.arange(piece_len, dtype=jnp.int32)[None, :] < lengths[:, None]


def dot32(left, right, dims):
    return lax.dot_general(left, right, (dims, ((), ())), preferred_element_type=F32)


def on_device_plain(
    block_in,
    teacher,
    image_counts,
    expert_ids,
    pair_keep,
    norm1_gain,
    norm1_bias,
    qkv_weight,
    out_weight,
    norm2_gain,
    norm2_bias,
    router_weight,
    expert_in,
    expert_out,
):
    images, piece_len, features = block_in.shape
    pieces = lax.axis_size("seq")
    groups = lax.axis_size("fsdp")
    seq_place = lax.axis_index("seq")
    group_place = lax.axis_index("fsdp")
    rows = images * piece_len
    slots = pieces * piece_len
    heads_here = HEADS // pieces
    cols = heads_here * HD
    hidden_size = expert_in.shape[2]
    capacity = rows * TOPK * 9 // (EXPERTS * 8) + 1
    inv_root = HD ** (-0.5)
    in_rows = expert_in.shape[0]
    out_rows = expert_out.shape[0]

    small = jnp.concatenate(
        [
            jnp.stack([norm1_gain, norm1_bias, norm2_gain, norm2_bias], axis=1),
            router_weight,
            out_weight,
            lax.dynamic_index_in_dim(
                qkv_weight.reshape(-1, 3, pieces, cols), seq_place, 2, keepdims=False
            ).reshape(-1, 3 * cols),
        ],
        axis=1,
    )
    small_full = lax.all_gather(small, "fsdp", axis=0, tiled=True)
    gain_one, bias_one, gain_two, bias_two = [small_full[:, i].astype(F32) for i in range(4)]
    router_full = small_full[:, 4 : 4 + EXPERTS]
    out_full = small_full[:, 4 + EXPERTS : 4 + EXPERTS + features]
    qkv_here = small_full[:, 4 + EXPERTS + features :]
    up_here = lax.all_gather(
        lax.dynamic_index_in_dim(expert_in, seq_place, 1, keepdims=False), "fsdp", axis=0, tiled=True
    )
    down_here = lax.all_gather(
        lax.dynamic_index_in_dim(expert_out, seq_place, 1, keepdims=False), "fsdp", axis=0, tiled=True
    )

    own_slots = slot_holds(jnp.reshape(seq_place, (1,)), piece_len, SEQ_LEN, pieces).reshape(piece_len)
    key_ok = slot_holds(jnp.arange(pieces, dtype=jnp.int32), piece_len, SEQ_LEN, pieces).reshape(slots)
    group_count = jnp.sum(
        jnp.where(jnp.arange(image_counts.shape[0], dtype=jnp.int32) == group_place, image_counts, 0)
    )
    token_ok = (
        (jnp.arange(images, dtype=jnp.int32) < group_count)[:, None] & own_slots[None, :]
    ).reshape(rows)

    flat_in = block_in.reshape(rows, features)
    normed_one, unit_one, root_one = layer_norm(flat_in, gain_one, bias_one)
    low_one = normed_one.astype(BF16)
    low_all = lax.all_gather(low_one.reshape(images, piece_len, features), "seq", axis=1, tiled=True)
    projected = dot32(low_all, qkv_here, ((2,), (0,))).astype(BF16)
    by_heads = projected.reshape(images, slots, 3, heads_here, HD).transpose(2, 0, 3, 1, 4)
    queries, key_rows, value_rows = by_heads[0], by_heads[1], by_heads[2]
    scores = jnp.einsum("ihqd,ihkd->ihqk", queries, key_rows, preferred_element_type=F32) * inv_root
    scores = jnp.where(key_ok[None, None, None, :], scores, -1e30)
    raised = jnp.exp(scores - jnp.max(scores, axis=-1, keepdims=True))
    attn = raised / jnp.sum(raised, axis=-1, keepdims=True)
    attn_low = attn.astype(BF16)
    context = jnp.einsum("ihqk,ihkd->iqhd", attn_low, value_rows, preferred_element_type=F32).astype(BF16)
    context_rows = lax.all_to_all(
        context.reshape(images, slots, 1, cols), "seq", split_axis=1, concat_axis=2, tiled=True
    ).reshape(rows, features)
    middle = flat_in + dot32(context_rows, out_full, ((1,), (0,)))
    normed_two, unit_two, root_two = layer_norm(middle, gain_two, bias_two)
    low_two = normed_two.astype(BF16)
    probs = jax.nn.softmax(dot32(low_two, router_full, ((1,), (0,))), axis=-1)

    expert_rows = expert_ids.reshape(rows, TOPK)
    usable = (pair_keep.reshape(rows, TOPK) == 1) & token_ok[:, None]
    hit = jnp.any(
        (expert_rows[:, :, None] == jnp.arange(EXPERTS, dtype=jnp.int32)) & usable[:, :, None], axis=1
    )
    earlier = (jnp.arange(rows)[:, None] > jnp.arange(rows)[None, :]).astype(BF16)
    place = dot32(earlier, hit.astype(BF16), ((1,), (0,))).astype(jnp.int32)
    place = jnp.where(hit, place, -1)
    select = (place.T[:, None, :] == jnp.arange(capacity, dtype=jnp.int32)[None, :, None]).astype(BF16)
    weight = jnp.where(hit, probs, 0.0)

    dispatched = dot32(select, low_two, ((2,), (0,))).astype(BF16)
    arrived = lax.all_to_all(dispatched, "seq", split_axis=0, concat_axis=0, tiled=True)
    arrived = arrived.reshape(pieces * capacity, features)
    hidden = dot32(arrived, up_here, ((1,), (0,)))
    activated, gelu_back = jax.vjp(lambda u: jax.nn.gelu(u, approximate=False), hidden)
    low_act = activated.astype(BF16)
    returned = dot32(low_act, down_here, ((1,), (0,))).astype(BF16)
    returned = lax.all_to_all(
        returned.reshape(pieces, capacity, features), "seq", split_axis=0, concat_axis=0, tiled=True
    )
    picked = jnp.einsum("est,esd->etd", select, returned, preferred_element_type=F32)
    block_out = middle + jnp.sum(weight.T[:, :, None] * picked, axis=0)
    misfit = (block_out - teacher.reshape(rows, features)) * token_ok.astype(F32)[:, None]
    loss_here = jnp.sum(misfit * misfit)

    pair_grad = (weight.T[:, :, None] * misfit[None]).astype(BF16)
    returned_grad = jnp.einsum("est,etd->esd", select, pair_grad, preferred_element_type=F32).astype(BF16)
    prob_grad = jnp.where(hit, jnp.sum(picked * misfit[None], axis=2).T, 0.0)
    grad_arrived = lax.all_to_all(returned_grad, "seq", split_axis=0, concat_axis=0, tiled=True).reshape(
        pieces * capacity, features
    )
    hidden_grad = gelu_back(dot32(grad_arrived, down_here, ((1,), (1,))))[0].astype(BF16)
    grad_down = dot32(low_act, grad_arrived, ((0,), (0,))).astype(BF16)
    grad_up = dot32(arrived, hidden_grad, ((0,), (0,))).astype(BF16)
    dispatch_grad = dot32(hidden_grad, up_here, ((1,), (1,))).astype(BF16)
    dispatch_grad = lax.all_to_all(
        dispatch_grad.reshape(pieces, capacity, features), "seq", split_axis=0, concat_axis=0, tiled=True
    )
    owned_down = lax.psum_scatter(grad_down, "fsdp", scatter_dimension=0, tiled=True)
    owned_up = lax.psum_scatter(grad_up, "fsdp", scatter_dimension=0, tiled=True)

    logit_grad = probs * (prob_grad - jnp.sum(probs * prob_grad, axis=1, keepdims=True))
    grad_router = lax.dot_general(
        low_two.astype(F32), logit_grad, (((0,), (0,)), ((), ())), precision=PRECISE
    )
    normed_two_grad = jnp.einsum("est,esd->td", select, dispatch_grad, preferred_element_type=F32)
    normed_two_grad = normed_two_grad + lax.dot_general(
        logit_grad, router_full.astype(F32), (((1,), (1,)), ((), ())), precision=PRECISE
    )
    grad_gain_two = jnp.sum(normed_two_grad * unit_two, axis=0)
    grad_bias_two = jnp.sum(normed_two_grad, axis=0)
    middle_grad = misfit + layer_norm_back(normed_two_grad, unit_two, root_two, gain_two)
    attended_grad = middle_grad.astype(BF16)
    grad_out_w = dot32(context_rows, attended_grad, ((0,), (0,))).astype(BF16)
    context_grad = dot32(attended_grad, out_full, ((1,), (1,))).astype(BF16)
    heads_grad = lax.all_to_all(
        context_grad.reshape(images, piece_len, pieces, cols), "seq", split_axis=2, concat_axis=1, tiled=True
    ).reshape(images, slots, heads_here, HD)
    value_grad = jnp.einsum("ihqk,iqhd->ikhd", attn_low, heads_grad, preferred_element_type=F32)
    share_grad = jnp.einsum("iqhd,ihkd->ihqk", heads_grad, value_rows, preferred_element_type=F32)
    score_grad = (attn * (share_grad - jnp.sum(attn * share_grad, axis=-1, keepdims=True))).astype(BF16)
    query_grad = jnp.einsum("ihqk,ihkd->iqhd", score_grad, key_rows, preferred_element_type=F32) * inv_root
    key_grad = jnp.einsum("ihqk,ihqd->ikhd", score_grad, queries, preferred_element_type=F32) * inv_root
    heads_back = jnp.stack([query_grad, key_grad, value_grad], axis=2).astype(BF16)
    heads_back = heads_back.reshape(images * slots, 3 * cols)
    grad_qkv = dot32(low_all.reshape(images * slots, features), heads_back, ((0,), (0,))).astype(BF16)
    normed_one_part = dot32(heads_back, qkv_here, ((1,), (1,))).astype(BF16)
    normed_one_grad = lax.psum_scatter(
        normed_one_part.reshape(images, slots, features), "seq", scatter_dimension=1, tiled=True
    ).astype(F32).reshape(rows, features)
    grad_gain_one = jnp.sum(normed_one_grad * unit_one, axis=0)
    grad_bias_one = jnp.sum(normed_one_grad, axis=0)
    input_grad = middle_grad + layer_norm_back(normed_one_grad, unit_one, root_one, gain_one)

    out_share = lax.psum_scatter(grad_out_w, "seq", scatter_dimension=1, tiled=True)
    attn_owned = lax.psum_scatter(
        jnp.concatenate([grad_qkv, out_share], axis=1), "fsdp", scatter_dimension=0, tiled=True
    )
    loss_row = jnp.zeros((features,), F32).at[0].set(loss_here)
    vectors = jnp.concatenate(
        [jnp.stack([grad_gain_one, grad_bias_one, grad_gain_two, grad_bias_two, loss_row]), grad_router.T], axis=0
    )
    vectors = lax.psum(vectors, ("fsdp", "seq"))
    mean_loss = vectors[4, 0] / (
        (jnp.sum(image_counts, dtype=jnp.int32) * SEQ_LEN).astype(F32) * features
    )
    owned_vectors = lax.dynamic_slice_in_dim(vectors, group_place * in_rows, in_rows, axis=1)
    attn_whole = lax.all_gather(attn_owned, "seq", axis=0)
    grad_qkv_w = (
        attn_whole[:, :, : 3 * cols].reshape(pieces, in_rows, 3, cols).transpose(1, 2, 0, 3)
        .reshape(in_rows, 3 * features).astype(F32)
    )
    grad_out_whole = attn_whole[:, :, 3 * cols :].transpose(1, 0, 2).reshape(in_rows, features).astype(F32)
    grad_up_w = lax.all_gather(owned_up, "seq", axis=0).transpose(1, 0, 2).astype(F32)
    grad_down_w = lax.all_gather(owned_down, "seq", axis=0).transpose(1, 0, 2).astype(F32)
    return (
        block_out.reshape(images, piece_len, features),
        mean_loss,
        input_grad.reshape(images, piece_len, features),
        owned_vectors[0],
        owned_vectors[1],
        grad_qkv_w,
        grad_out_whole,
        owned_vectors[2],
        owned_vectors[3],
        owned_vectors[5:].T,
        grad_up_w,
        grad_down_w,
    )


MESH = pl.DeviceIdType.MESH
LANES = 16
STATS = 16
GAIN_ONE, BIAS_ONE, GAIN_TWO, BIAS_TWO = 4, 5, 6, 7
LOSS_ROW = 8


def round_up(value, step):
    return (value + step - 1) // step * step


def flipped(place, bits):
    low, high = lax.rem(place, 2), place // 2
    if bits % 2:
        low = 1 - low
    if bits // 2:
        high = 1 - high
    return high * 2 + low


def unit_rows(values_in):
    centered = values_in - jnp.mean(values_in, axis=1, keepdims=True)
    variance = jnp.mean(centered * centered, axis=1, keepdims=True)
    root = lax.rsqrt(variance + NORM_EPS)
    return centered * root, root


def norm_back(grad_out, unit, root, gain_row):
    scaled = grad_out * gain_row
    return root * (
        scaled
        - jnp.mean(scaled, axis=1, keepdims=True)
        - unit * jnp.mean(scaled * unit, axis=1, keepdims=True)
    )


def hi_lo(values_in):
    high = values_in.astype(BF16)
    return high, (values_in - high.astype(F32)).astype(BF16)


def block_kernel(
    sizes,
    x_in,
    teacher_in,
    route_rows,
    route_cols,
    vec_in,
    attn_in,
    up_in,
    down_in,
    block_out,
    input_grad,
    stats_out,
    attn_all,
    up_all,
    down_all,
    zrecv_down,
    zrecv_up,
    zrecv_attn,
    vec_all,
    vecs,
    attn_w,
    out_w,
    up_w,
    down_w,
    low_all,
    qkv_s,
    lse_s,
    ctx_s,
    ctx_rows,
    middle,
    misfit,
    low_two,
    select,
    select_t,
    hits,
    weights,
    send_s,
    arrived,
    ret_r,
    back_r,
    dret_r,
    turned,
    act,
    slope,
    grad_down,
    yrecv_down,
    yrecv_up,
    dctx_s,
    half_recv,
    yrecv_attn,
    part_s,
    part_r,
    stats,
    stats_r,
    send_sem,
    recv_sem,
    local_sem,
):
    images, piece, padded, cap, features, cols, ffn, in_rows, out_rows = sizes
    rows = images * padded
    slots = 4 * padded
    half_cols = features // 2
    wide = ffn // 6
    f = lax.axis_index("fsdp")
    s = lax.axis_index("seq")
    z, y = f // 2, lax.rem(f, 2)
    inv_root = HD ** (-0.5)
    same = [flipped(z, k) * 2 + y for k in range(4)]
    other = [flipped(z, k) * 2 + (1 - y) for k in range(4)]
    near = [flipped(s, r) for r in range(4)]
    counter = [0, 0]
    pending = []

    def send(src, dst, group, seq):
        i = counter[0]
        counter[0] += 1
        copy = pltpu.make_async_remote_copy(
            src_ref=src,
            dst_ref=dst,
            send_sem=send_sem.at[i],
            recv_sem=recv_sem.at[i],
            device_id=(group, seq),
            device_id_type=MESH,
        )
        copy.start()
        pending.append(copy)
        return copy

    def done_sending(copy):
        pending[:] = [other_copy for other_copy in pending if other_copy is not copy]
        copy.wait_send()

    def local(src, dst):
        i = counter[1]
        counter[1] += 1
        copy = pltpu.make_async_copy(src, dst, local_sem.at[i])
        copy.start()
        return copy

    barrier = pltpu.get_barrier_semaphore()
    for g in same[1:] + other:
        pl.semaphore_signal(barrier, inc=1, device_id=(g, s), device_id_type=MESH)
    for q in near[1:]:
        pl.semaphore_signal(barrier, inc=1, device_id=(f, q), device_id_type=MESH)
    pl.semaphore_wait(barrier, 10)

    vec_copies = [send(vec_in, vec_all.at[f], g, s) for g in same[1:] + other]
    vec_all[f] = vec_in[...]

    def spot(ref, n, g):
        return ref.at[pl.ds(pl.multiple_of(g * n, n), n), :]

    def gather_start(src, dst, n):
        along_z = [None] + [send(src, spot(dst, n, f), same[k], s) for k in (1, 2, 3)]
        across = [send(src, spot(dst, n, f), other[0], s)]
        return along_z, across, local(src, spot(dst, n, f))

    def gather_pass(flow, dst, n, k):
        along_z, across, _ = flow
        along_z[k].wait_recv()
        across.append(send(spot(dst, n, same[k]), spot(dst, n, same[k]), other[0], s))

    def gather_end(flow):
        for copy in flow[1]:
            copy.wait_recv()
        flow[2].wait()

    attn_flow = gather_start(attn_in, attn_w, in_rows)

    own_near = near

    def near_of(shape, axis):
        at = lax.broadcasted_iota(jnp.int32, shape, axis)
        named = jnp.full(shape, -1, jnp.int32)
        for r in range(4):
            named = jnp.where(at == r, own_near[r], named)
        return named

    named = near_of((rows, LANES), 1)
    hit = ((route_rows[:, 0:1] == named) & (route_rows[:, 2:3] == 1)) | (
        (route_rows[:, 1:2] == named) & (route_rows[:, 3:4] == 1)
    )
    hit_f = jnp.where(hit, 1.0, 0.0)
    before = (
        lax.broadcasted_iota(jnp.int32, (rows, rows), 0) > lax.broadcasted_iota(jnp.int32, (rows, rows), 1)
    )
    before = jnp.where(before, 1.0, 0.0).astype(BF16)
    place = dot32(before, hit_f.astype(BF16), ((1,), (0,)))
    place = jnp.where(hit, place, -1.0)
    hits[...] = hit_f
    named_t = near_of((LANES, rows), 0)
    hit_t = ((route_cols[0:1, :] == named_t) & (route_cols[2:3, :] == 1)) | (
        (route_cols[1:2, :] == named_t) & (route_cols[3:4, :] == 1)
    )
    hit_tf = jnp.where(hit_t, 1.0, 0.0).astype(BF16)
    place_t = dot32(hit_tf, before, ((1,), (1,)))
    place_t = jnp.where(hit_t, place_t, -1.0)
    slot_down = lax.broadcasted_iota(jnp.int32, (cap, rows), 0).astype(F32)
    slot_along = lax.broadcasted_iota(jnp.int32, (rows, cap), 1).astype(F32)
    for r in range(4):
        select[r] = jnp.where(place_t[r : r + 1, :] == slot_down, 1.0, 0.0).astype(BF16)
        select_t[r] = jnp.where(place[:, r : r + 1] == slot_along, 1.0, 0.0).astype(BF16)

    for copy in vec_copies:
        copy.wait_recv()
    at_row = lax.broadcasted_iota(jnp.int32, (128, features), 0)
    at_col = lax.broadcasted_iota(jnp.int32, (128, features), 1)
    total = jnp.zeros((STATS, features), F32)
    for g in range(8):
        spread = jnp.where((at_col - g * in_rows == at_row) & (at_row < in_rows), 1.0, 0.0).astype(BF16)
        total = total + dot32(vec_all[g], spread, ((1,), (0,)))
    vecs[...] = total

    low_all[s] = jnp.zeros((rows, features), BF16)
    for i in range(images):
        unit, _ = unit_rows(x_in[i])
        low_all[s, i * padded : i * padded + piece, :] = (
            unit * vecs[GAIN_ONE : GAIN_ONE + 1, :] + vecs[BIAS_ONE : BIAS_ONE + 1, :]
        ).astype(BF16)
    low_x = send(low_all.at[s], low_all.at[s], f, near[2])
    low_c = send(low_all.at[s], low_all.at[s], f, near[1])

    for k in (1, 2, 3):
        gather_pass(attn_flow, attn_w, in_rows, k)
    up_flow = gather_start(up_in, up_w, in_rows)
    low_x.wait_recv()
    low_d = send(low_all.at[near[2]], low_all.at[near[2]], f, near[1])
    gather_end(attn_flow)
    mine = lax.rem(s, 2)
    here = pl.ds(pl.multiple_of(mine * half_cols, half_cols), half_cols)
    there = pl.ds(pl.multiple_of((1 - mine) * half_cols, half_cols), half_cols)
    out_half = send(attn_w.at[:, pl.ds(0, half_cols)], out_w.at[:, here], f, near[1])
    out_w[:, here] = attn_w[:, 0:half_cols]

    def project(j):
        found = dot32(low_all[j], attn_w[:, half_cols:], ((1,), (0,))).astype(BF16)
        for i in range(images):
            qkv_s[i, pl.ds(pl.multiple_of(j * padded, padded), padded), :] = found[
                i * padded : (i + 1) * padded, :
            ]

    project(s)
    low_c.wait_recv()
    project(near[1])
    project(near[2])
    low_d.wait_recv()
    project(near[3])

    key_at = lax.broadcasted_iota(jnp.int32, (slots, 1), 0)
    key_piece = jnp.zeros((slots, 1), jnp.int32)
    for j in range(1, 4):
        key_piece = key_piece + jnp.where(key_at >= j * padded, 1, 0)
    key_len = SEQ_LEN // 4 + jnp.where(key_piece < SEQ_LEN % 4, 1, 0)
    key_ok = key_at - key_piece * padded < key_len

    def heads_of(ref, i, kind, h):
        return ref[i, :, kind * cols + h * HD : kind * cols + (h + 1) * HD]

    def scores_of(i, h):
        found = dot32(heads_of(qkv_s, i, 1, h), heads_of(qkv_s, i, 0, h), ((1,), (1,))) * inv_root
        return jnp.where(key_ok, found, -1e30)

    gather_pass(up_flow, up_w, in_rows, 1)
    down_flow = gather_start(down_in, down_w, out_rows)

    @pl.loop(0, images)
    def _(i):
        found = []
        for h in range(cols // HD):
            scores = scores_of(i, h)
            highest = jnp.max(scores, axis=0, keepdims=True)
            raised = jnp.exp(scores - highest)
            total = jnp.sum(raised, axis=0, keepdims=True)
            shares = (raised * (1.0 / total)).astype(BF16)
            lse_s[i, h : h + 1, :] = highest + jnp.log(total)
            found.append(dot32(heads_of(qkv_s, i, 2, h), shares, ((0,), (0,))))
        ctx_s[i] = jnp.concatenate(found, axis=0).T.astype(BF16)

    def piece_rows(ref, j):
        return ref.at[:, pl.ds(pl.multiple_of(j * padded, padded), padded), :]

    ctx_copies = [send(piece_rows(ctx_s, near[r]), ctx_rows.at[s], f, near[r]) for r in (2, 3, 1)]
    ctx_rows[s] = ctx_s[:, pl.ds(pl.multiple_of(s * padded, padded), padded), :]
    for k in (2, 3):
        gather_pass(up_flow, up_w, in_rows, k)
    out_half.wait_recv()
    for copy in ctx_copies:
        copy.wait_recv()
        done_sending(copy)

    attended = jnp.zeros((rows, features), F32)
    for j in range(4):
        attended = attended + dot32(
            ctx_rows[j].reshape(rows, cols), out_w[j * cols : (j + 1) * cols, :], ((1,), (0,))
        )
    middle[...] = attended
    for i in range(images):
        at = slice(i * padded, i * padded + piece)
        middle[at, :] = middle[at, :] + x_in[i]
    unit, _ = unit_rows(middle[...])
    low_two[...] = (unit * vecs[GAIN_TWO : GAIN_TWO + 1, :] + vecs[BIAS_TWO : BIAS_TWO + 1, :]).astype(BF16)
    router = vecs[...].astype(BF16)

    def probs_of():
        logits = dot32(low_two[...], router, ((1,), (1,)))
        real = lax.broadcasted_iota(jnp.int32, (rows, LANES), 1) < EXPERTS
        logits = jnp.where(real, logits, -1e30)
        raised = jnp.exp(logits - jnp.max(logits, axis=1, keepdims=True))
        return raised / jnp.sum(raised, axis=1, keepdims=True)

    disp_copies = []
    for r in (2, 3, 1, 0):
        found = dot32(select[r], low_two[...], ((1,), (0,))).astype(BF16)
        if r:
            send_s[r - 1] = found
            disp_copies.append(send(send_s.at[r - 1], arrived.at[r], f, near[r]))
        else:
            arrived[0] = found
    probs = probs_of()
    lane = lax.broadcasted_iota(jnp.int32, (rows, LANES), 1)
    chosen = jnp.zeros((rows, LANES), F32)
    for r in range(4):
        value = jnp.sum(jnp.where(lane == near[r], probs, 0.0), axis=1, keepdims=True)
        chosen = jnp.where(lane == r, value, chosen)
    weights[...] = chosen * hits[...]

    gather_end(up_flow)
    gather_pass(down_flow, down_w, out_rows, 1)

    def expert_up(half):
        given = arrived[2 * half : 2 * half + 2].reshape(2 * cap, features)

        @pl.loop(0, 6)
        def _(t):
            tile = pl.ds(pl.multiple_of(t * wide, wide), wide)
            hidden = dot32(given, up_w[:, tile], ((1,), (0,)))
            phi = 0.5 * (1.0 + lax.erf(hidden * (2.0**-0.5)))
            at = slice(2 * half * cap, 2 * (half + 1) * cap)
            act[at, tile] = (hidden * phi).astype(BF16)
            slope[at, tile] = (phi + hidden * jnp.exp(-0.5 * hidden * hidden) * 0.3989422804014327).astype(BF16)

    disp_copies[2].wait_recv()
    expert_up(0)
    disp_copies[0].wait_recv()
    disp_copies[1].wait_recv()
    expert_up(1)
    for k in (2, 3):
        gather_pass(down_flow, down_w, out_rows, k)
    for copy in disp_copies:
        done_sending(copy)
    gather_end(down_flow)

    def to_rows(left, right, dims, half, dst):
        at = slice(2 * half * cap, 2 * (half + 1) * cap)
        found = dot32(left[at, :], right[...], dims).astype(BF16)
        out = []
        for r in (2 * half, 2 * half + 1):
            part = found[(r - 2 * half) * cap : (r - 2 * half + 1) * cap, :]
            if r:
                send_s[r - 1] = part
                out.append(send(send_s.at[r - 1], dst.at[r], f, near[r]))
            else:
                dst[0] = part
        return out

    ret_copies = to_rows(act, down_w, ((1,), (0,)), 1, ret_r)
    ret_copies += to_rows(act, down_w, ((1,), (0,)), 0, ret_r)
    for i in range(images):
        at = slice(i * padded, i * padded + piece)
        misfit[at, :] = teacher_in[i]
        misfit[i * padded + piece : (i + 1) * padded, :] = jnp.zeros((padded - piece, features), F32)
    for copy in ret_copies:
        copy.wait_recv()

    found = middle[...]
    for r in range(4):
        found = found + weights[:, r : r + 1] * dot32(select_t[r], ret_r[r], ((1,), (0,)))
    for i in range(images):
        block_out[i] = found[i * padded : i * padded + piece, :]
    token_ok = route_rows[:, 4:5].astype(F32)
    wrong = (found - misfit[...]) * token_ok
    misfit[...] = wrong
    for copy in ret_copies:
        done_sending(copy)
    dret_copies = []
    for r in (2, 3, 1, 0):
        pair = (weights[:, r : r + 1] * misfit[...]).astype(BF16)
        part = dot32(select[r], pair, ((1,), (0,))).astype(BF16)
        if r:
            send_s[r - 1] = part
            dret_copies.append(send(send_s.at[r - 1], dret_r.at[r], f, near[r]))
        else:
            dret_r[0] = part
    stats[...] = jnp.zeros_like(stats)
    stats[LOSS_ROW : LOSS_ROW + 1, :] = jnp.sum(wrong * wrong, axis=0, keepdims=True)
    probs = probs_of()
    prob_grad = jnp.zeros((rows, LANES), F32)
    for r in range(4):
        picked = dot32(select_t[r], ret_r[r], ((1,), (0,)))
        value = jnp.sum(picked * misfit[...], axis=1, keepdims=True) * hits[:, r : r + 1]
        prob_grad = jnp.where(lane == near[r], value, prob_grad)
    logit_grad = probs * (prob_grad - jnp.sum(probs * prob_grad, axis=1, keepdims=True))
    high, low = hi_lo(logit_grad)
    router_grad = dot32(high, low_two[...], ((0,), (0,))) + dot32(low, low_two[...], ((0,), (0,)))
    stats[0:EXPERTS, :] = router_grad[0:EXPERTS, :]
    for copy in dret_copies:
        copy.wait_recv()

    given = dret_r[...].reshape(4 * cap, features)
    turned[...] = given.T

    @pl.loop(0, 8)
    def _(g):
        grad_down[g] = dot32(
            turned[...], act[:, pl.ds(pl.multiple_of(g * out_rows, out_rows), out_rows)], ((1,), (0,))
        ).astype(BF16)

    def down_block(g):
        return grad_down.at[g]

    def up_block(g):
        return spot(up_w, in_rows, g)

    def attn_block(g):
        return spot(attn_w, in_rows, g)

    def sum_start(block, yrecv):
        return {k: send(block(other[k]), yrecv.at[k], other[0], s) for k in (3, 2, 1, 0)}

    def sum_pass(flow, block, yrecv, zrecv, k):
        flow[k].wait_recv()
        ref = block(same[k])
        ref[...] = (ref[...].astype(F32) + yrecv[k].astype(F32)).astype(BF16)
        if k:
            flow["z%d" % k] = send(ref, zrecv.at[k - 1], same[k], s)

    def sum_end(flow, block, yrecv, zrecv, dst):
        ref = block(f)
        loads = []
        for k in (1, 2, 3):
            flow["z%d" % k].wait_recv()
            loads.append(local(zrecv.at[k - 1], yrecv.at[k]))
        for copy in loads:
            copy.wait()
        total = ref[...].astype(F32)
        for k in (1, 2, 3):
            total = total + yrecv[k].astype(F32)
        ref[...] = total.astype(BF16)
        to_x = send(ref, dst.at[s], f, near[2])
        to_c = send(ref, dst.at[s], f, near[1])
        return to_x, to_c, local(ref, dst.at[s])

    def share_pass(flow, dst):
        flow[0].wait_recv()
        return send(dst.at[near[2]], dst.at[near[2]], f, near[1])

    down_sum = sum_start(down_block, yrecv_down)

    @pl.loop(0, 6)
    def _(t):
        tile = pl.ds(pl.multiple_of(t * wide, wide), wide)
        found = dot32(dret_r[...].reshape(4 * cap, features), down_w[tile, :], ((1,), (1,)))
        act[:, tile] = (found * slope[:, tile].astype(F32)).astype(BF16)

    for copy in dret_copies:
        done_sending(copy)
    back_copies = to_rows(act, up_w, ((1,), (1,)), 1, back_r)
    back_copies += to_rows(act, up_w, ((1,), (1,)), 0, back_r)
    sum_pass(down_sum, down_block, yrecv_down, zrecv_down, 3)
    for copy in up_flow[0][1:] + up_flow[1]:
        done_sending(copy)
    given = arrived[...].reshape(4 * cap, features)
    turned[...] = given.T

    @pl.loop(0, 6)
    def _(t):
        tile = pl.ds(pl.multiple_of(t * wide, wide), wide)
        up_w[:, tile] = dot32(turned[...], act[:, tile], ((1,), (0,))).astype(BF16)

    up_sum = sum_start(up_block, yrecv_up)
    sum_pass(down_sum, down_block, yrecv_down, zrecv_down, 2)

    normed_grad = dot32(high, router, ((1,), (0,))) + dot32(low, router, ((1,), (0,)))
    for copy in back_copies:
        copy.wait_recv()
    for r in range(4):
        normed_grad = normed_grad + dot32(select_t[r], back_r[r], ((1,), (0,)))
    unit, root = unit_rows(middle[...])
    stats[GAIN_TWO : GAIN_TWO + 1, :] = jnp.sum(normed_grad * unit, axis=0, keepdims=True)
    stats[BIAS_TWO : BIAS_TWO + 1, :] = jnp.sum(normed_grad, axis=0, keepdims=True)
    middle_grad = misfit[...] + norm_back(normed_grad, unit, root, vecs[GAIN_TWO : GAIN_TWO + 1, :])
    middle[...] = middle_grad
    low_two[...] = middle_grad.astype(BF16)

    dctx_copies = []
    for r in (2, 3, 1, 0):
        block = out_w[pl.ds(pl.multiple_of(near[r] * cols, cols), cols), :]
        found = dot32(low_two[...], block, ((1,), (1,))).astype(BF16).reshape(images, padded, cols)
        if r:
            dctx_s[r - 1] = found
            dctx_copies.append(send(dctx_s.at[r - 1], piece_rows(ctx_s, s), f, near[r]))
        else:
            ctx_s[:, pl.ds(pl.multiple_of(s * padded, padded), padded), :] = found
    done_sending(out_half)
    for j in range(4):
        out_w[j * cols : (j + 1) * cols, :] = dot32(
            ctx_rows[j].reshape(rows, cols), low_two[...], ((0,), (0,))
        ).astype(BF16)
    half_copy = send(out_w.at[:, there], half_recv, f, near[1])
    sum_pass(down_sum, down_block, yrecv_down, zrecv_down, 1)
    for copy in dctx_copies:
        copy.wait_recv()

    @pl.loop(0, images)
    def _(i):
        found = [[], [], []]
        for h in range(cols // HD):
            shares = jnp.exp(scores_of(i, h) - lse_s[i, h : h + 1, :])
            given = ctx_s[i, :, h * HD : (h + 1) * HD]
            found[2].append(dot32(shares.astype(BF16), given, ((1,), (0,))))
            share_grad = dot32(heads_of(qkv_s, i, 2, h), given, ((1,), (1,)))
            across = jnp.sum(shares * share_grad, axis=0, keepdims=True)
            score_grad = (shares * (share_grad - across)).astype(BF16)
            found[1].append(dot32(score_grad, heads_of(qkv_s, i, 0, h), ((1,), (0,))) * inv_root)
            query_t = dot32(heads_of(qkv_s, i, 1, h), score_grad, ((0,), (0,))) * inv_root
            found[0].append(query_t.T)
        for kind in range(3):
            whole = jnp.concatenate(found[kind], axis=1).astype(BF16)
            found[kind] = whole
        qkv_s[i] = jnp.concatenate(found, axis=1)

    sum_pass(down_sum, down_block, yrecv_down, zrecv_down, 0)

    def dqkv_rows(j):
        return qkv_s[:, pl.ds(pl.multiple_of(j * padded, padded), padded), :].reshape(rows, 3 * cols)

    def low_part(j):
        return dot32(dqkv_rows(j), attn_w[:, half_cols:], ((1,), (1,)))

    part_s[0] = low_part(near[3]).astype(BF16)
    part_c = send(part_s.at[0], part_r.at[0], f, near[1])
    part_s[1] = low_part(near[1]).astype(BF16)
    part_d = send(part_s.at[1], part_r.at[1], f, near[1])
    for_x = low_part(near[2])
    part_c.wait_recv()
    part_s[2] = (for_x + part_r[0].astype(F32)).astype(BF16)
    part_x = send(part_s.at[2], part_r.at[2], f, near[2])
    sum_pass(up_sum, up_block, yrecv_up, zrecv_up, 3)
    down_share = sum_end(down_sum, down_block, yrecv_down, zrecv_down, down_all)

    misfit[...] = low_part(s)

    for copy in attn_flow[1]:
        done_sending(copy)
    qkv_grad = jnp.zeros((features, 3 * cols), F32)
    for i in range(images):
        given = low_all[:, i * padded : (i + 1) * padded, :].reshape(4 * padded, features)
        qkv_grad = qkv_grad + dot32(given, qkv_s[i], ((0,), (0,)))
    attn_w[:, half_cols:] = qkv_grad.astype(BF16)
    half_copy.wait_recv()
    attn_w[:, 0:half_cols] = (out_w[:, here].astype(F32) + half_recv[...].astype(F32)).astype(BF16)
    attn_sum = sum_start(attn_block, yrecv_attn)
    sum_pass(up_sum, up_block, yrecv_up, zrecv_up, 2)

    part_d.wait_recv()
    low_grad = misfit[...] + part_r[1].astype(F32)
    part_x.wait_recv()
    low_grad = low_grad + part_r[2].astype(F32)
    misfit[...] = low_grad
    stats[BIAS_ONE : BIAS_ONE + 1, :] = jnp.sum(low_grad, axis=0, keepdims=True)
    gain_grad = jnp.zeros((1, features), F32)
    for i in range(images):
        at = slice(i * padded, i * padded + piece)
        unit, root = unit_rows(x_in[i])
        gain_grad = gain_grad + jnp.sum(misfit[at, :] * unit, axis=0, keepdims=True)
        input_grad[i] = middle[at, :] + norm_back(misfit[at, :], unit, root, vecs[GAIN_ONE : GAIN_ONE + 1, :])
    stats[GAIN_ONE : GAIN_ONE + 1, :] = gain_grad

    seq_copies = [send(stats, stats_r.at[r - 1], f, near[r]) for r in (1, 2, 3)]
    down_last = share_pass(down_share, down_all)
    for copy in seq_copies:
        copy.wait_recv()
        done_sending(copy)
    stats[...] = stats[...] + stats_r[0] + stats_r[1] + stats_r[2]
    y_copy = send(stats, stats_r.at[3], other[0], s)
    sum_pass(up_sum, up_block, yrecv_up, zrecv_up, 1)
    y_copy.wait_recv()
    done_sending(y_copy)
    stats[...] = stats[...] + stats_r[3]
    z_copies = [send(stats, stats_r.at[3 + k], same[k], s) for k in (1, 2, 3)]
    sum_pass(up_sum, up_block, yrecv_up, zrecv_up, 0)
    for copy in z_copies:
        copy.wait_recv()
    stats_out[...] = stats[...] + stats_r[4] + stats_r[5] + stats_r[6]

    up_share = sum_end(up_sum, up_block, yrecv_up, zrecv_up, up_all)
    for k in (3, 2, 1, 0):
        sum_pass(attn_sum, attn_block, yrecv_attn, zrecv_attn, k)
    up_last = share_pass(up_share, up_all)
    attn_share = sum_end(attn_sum, attn_block, yrecv_attn, zrecv_attn, attn_all)
    attn_last = share_pass(attn_share, attn_all)
    for share, last in ((down_share, down_last), (up_share, up_last), (attn_share, attn_last)):
        share[1].wait_recv()
        share[2].wait()
        last.wait_recv()
    for copy in list(pending):
        done_sending(copy)


def run_block(sizes, operands):
    images, piece, padded, cap, features, cols, ffn, in_rows, out_rows = sizes
    rows = images * padded
    half_cols = features // 2
    pack = half_cols + 3 * cols
    shape = jax.ShapeDtypeStruct
    vmem = pl.BlockSpec(memory_space=pltpu.VMEM)
    hbm = pl.BlockSpec(memory_space=pl.ANY)
    scratch = [
        pltpu.VMEM((8, STATS, 128), BF16),
        pltpu.VMEM((STATS, features), F32),
        pltpu.VMEM((8 * in_rows, pack), BF16),
        pltpu.VMEM((features, features), BF16),
        pltpu.VMEM((features, ffn), BF16),
        pltpu.VMEM((ffn, features), BF16),
        pltpu.VMEM((4, rows, features), BF16),
        pltpu.VMEM((images, 4 * padded, 3 * cols), BF16),
        pltpu.VMEM((images, 8, 4 * padded), F32),
        pltpu.VMEM((images, 4 * padded, cols), BF16),
        pltpu.VMEM((4, images, padded, cols), BF16),
        pltpu.VMEM((rows, features), F32),
        pltpu.VMEM((rows, features), F32),
        pltpu.VMEM((rows, features), BF16),
        pltpu.VMEM((4, cap, rows), BF16),
        pltpu.VMEM((4, rows, cap), BF16),
        pltpu.VMEM((rows, LANES), F32),
        pltpu.VMEM((rows, LANES), F32),
        pltpu.VMEM((3, cap, features), BF16),
        pltpu.VMEM((4, cap, features), BF16),
        pltpu.VMEM((4, cap, features), BF16),
        pltpu.VMEM((4, cap, features), BF16),
        pltpu.VMEM((4, cap, features), BF16),
        pltpu.VMEM((features, 4 * cap), BF16),
        pltpu.VMEM((4 * cap, ffn), BF16),
        pltpu.VMEM((4 * cap, ffn), BF16),
        pltpu.VMEM((8, features, out_rows), BF16),
        pltpu.VMEM((4, features, out_rows), BF16),
        pltpu.VMEM((4, in_rows, ffn), BF16),
        pltpu.VMEM((3, images, padded, cols), BF16),
        pltpu.VMEM((features, half_cols), BF16),
        pltpu.VMEM((4, in_rows, pack), BF16),
        pltpu.VMEM((3, rows, features), BF16),
        pltpu.VMEM((3, rows, features), BF16),
        pltpu.VMEM((STATS, features), F32),
        pltpu.VMEM((7, STATS, features), F32),
        pltpu.SemaphoreType.DMA((112,)),
        pltpu.SemaphoreType.DMA((112,)),
        pltpu.SemaphoreType.DMA((16,)),
    ]
    return pl.pallas_call(
        lambda *refs: block_kernel(sizes, *refs),
        out_shape=(
            shape((images, piece, features), F32),
            shape((images, piece, features), F32),
            shape((STATS, features), F32),
            shape((4, in_rows, pack), BF16),
            shape((4, in_rows, ffn), BF16),
            shape((4, features, out_rows), BF16),
            shape((3, features, out_rows), BF16),
            shape((3, in_rows, ffn), BF16),
            shape((3, in_rows, pack), BF16),
        ),
        in_specs=[vmem, vmem, vmem, vmem, vmem, hbm, hbm, hbm],
        out_specs=(vmem, vmem, vmem, hbm, hbm, hbm, hbm, hbm, hbm),
        scratch_shapes=scratch,
        compiler_params=pltpu.CompilerParams(
            collective_id=0, has_side_effects=True, vmem_limit_bytes=63_000_000
        ),
        name="block",
    )(*operands)


def on_device(
    block_in,
    teacher,
    image_counts,
    expert_ids,
    pair_keep,
    norm1_gain,
    norm1_bias,
    qkv_weight,
    out_weight,
    norm2_gain,
    norm2_bias,
    router_weight,
    expert_in,
    expert_out,
):
    arguments = (
        block_in, teacher, image_counts, expert_ids, pair_keep, norm1_gain, norm1_bias, qkv_weight,
        out_weight, norm2_gain, norm2_bias, router_weight, expert_in, expert_out,
    )
    images, piece_len, features = block_in.shape
    pieces = lax.axis_size("seq")
    groups = lax.axis_size("fsdp")
    in_rows, out_rows, ffn = expert_in.shape[0], expert_out.shape[0], expert_in.shape[2]
    if pieces != EXPERTS or groups != 8 or in_rows % 16 or in_rows > 128 or out_rows % 128:
        return on_device_plain(*arguments)
    s = lax.axis_index("seq")
    f = lax.axis_index("fsdp")
    rows = images * piece_len
    cols = HEADS // pieces * HD
    padded = round_up(piece_len, 16)
    cap = round_up(rows * TOPK * 9 // (EXPERTS * 8) + 1, 16)
    half_cols = features // 2

    own_len = SEQ_LEN // pieces + (s < SEQ_LEN % pieces).astype(jnp.int32)
    count = jnp.sum(
        jnp.where(jnp.arange(image_counts.shape[0], dtype=jnp.int32) == f, image_counts, 0)
    )
    token_ok = (jnp.arange(images)[:, None] < count) & (jnp.arange(piece_len)[None, :] < own_len)
    usable = ((pair_keep[0] == 1) & token_ok[:, :, None]).astype(jnp.int32)
    route = jnp.concatenate([expert_ids[0], usable, token_ok[:, :, None].astype(jnp.int32)], axis=2)
    route = jnp.pad(route, ((0, 0), (0, padded - piece_len), (0, 3))).reshape(images * padded, 8)

    vec = jnp.concatenate(
        [router_weight.T, jnp.stack([norm1_gain, norm1_bias, norm2_gain, norm2_bias], axis=0)], axis=0
    )
    vec = jnp.pad(vec, ((0, STATS - 8), (0, 128 - in_rows)))
    attn_shard = jnp.concatenate(
        [
            lax.dynamic_slice_in_dim(out_weight, lax.rem(s, 2) * half_cols, half_cols, axis=1),
            lax.dynamic_index_in_dim(
                qkv_weight.reshape(in_rows, 3, pieces, cols), s, 2, keepdims=False
            ).reshape(in_rows, 3 * cols),
        ],
        axis=1,
    )
    up_shard = lax.dynamic_index_in_dim(expert_in, s, 1, keepdims=False)
    down_shard = lax.dynamic_index_in_dim(expert_out, s, 1, keepdims=False)
    sizes = (images, piece_len, padded, cap, features, cols, ffn, in_rows, out_rows)
    block_out, input_grad, stats, attn_all, up_all, down_all, *_ = run_block(
        sizes, (block_in, teacher, route, route.T, vec, attn_shard, up_shard, down_shard)
    )
    mean_loss = jnp.sum(stats[LOSS_ROW]) / (
        (jnp.sum(image_counts, dtype=jnp.int32) * SEQ_LEN).astype(F32) * features
    )
    own = lax.dynamic_slice_in_dim(stats, f * in_rows, in_rows, axis=1)
    grad_qkv = (
        attn_all[:, :, half_cols:].reshape(pieces, in_rows, 3, cols).transpose(1, 2, 0, 3)
        .reshape(in_rows, 3 * features).astype(F32)
    )
    halves = attn_all[:, :, :half_cols].astype(F32)
    grad_out = jnp.concatenate([halves[0] + halves[2], halves[1] + halves[3]], axis=1)
    grad_up = up_all.transpose(1, 0, 2).astype(F32)
    grad_down = down_all.transpose(2, 0, 1).astype(F32)
    return (
        block_out,
        mean_loss,
        input_grad,
        own[GAIN_ONE],
        own[BIAS_ONE],
        grad_qkv,
        grad_out,
        own[GAIN_TWO],
        own[BIAS_TWO],
        own[:EXPERTS].T,
        grad_up,
        grad_down,
    )


def solution(mesh):
    return jax.shard_map(
        on_device,
        mesh=mesh,
        in_specs=(
            P("fsdp", "seq", None),
            P("fsdp", "seq", None),
            P(),
            P("seq", "fsdp", None, None),
            P("seq", "fsdp", None, None),
            P("fsdp"),
            P("fsdp"),
            P("fsdp", None),
            P("fsdp", None),
            P("fsdp"),
            P("fsdp"),
            P("fsdp", None),
            P("fsdp", None, None),
            P("fsdp", None, None),
        ),
        out_specs=(
            P("fsdp", "seq", None),
            P(),
            P("fsdp", "seq", None),
            P("fsdp"),
            P("fsdp"),
            P("fsdp", None),
            P("fsdp", None),
            P("fsdp"),
            P("fsdp"),
            P("fsdp", None),
            P("fsdp", None, None),
            P("fsdp", None, None),
        ),
        check_vma=False,
    )
```

```python
import jax
import jax.numpy as jnp
from jax import lax
from jax.experimental import pallas as pl
from jax.experimental.pallas import tpu as pltpu
from jax.sharding import PartitionSpec as P

HEADS = 12
HD = 64
SEQ_LEN = 577
EXPERTS = 4
TOPK = 2
NORM_EPS = 1e-06
PRECISE = lax.Precision.HIGHEST
F32 = jnp.float32
BF16 = jnp.bfloat16


def layer_norm(values_in, gain_vec, bias_vec):
    centered = values_in - jnp.mean(values_in, axis=-1, keepdims=True)
    variance = jnp.mean(centered * centered, axis=-1, keepdims=True)
    root = lax.rsqrt(variance + NORM_EPS)
    unit = centered * root
    return unit * gain_vec + bias_vec, unit, root


def layer_norm_back(grad_out, unit, root, gain_vec):
    scaled = grad_out * gain_vec
    return root * (
        scaled
        - jnp.mean(scaled, axis=-1, keepdims=True)
        - unit * jnp.mean(scaled * unit, axis=-1, keepdims=True)
    )


def slot_holds(piece_index, piece_len, seq_len, pieces):
    lengths = seq_len // pieces + (piece_index < seq_len % pieces).astype(jnp.int32)
    return jnp.arange(piece_len, dtype=jnp.int32)[None, :] < lengths[:, None]


def dot32(left, right, dims):
    return lax.dot_general(left, right, (dims, ((), ())), preferred_element_type=F32)


def on_device_plain(
    block_in,
    teacher,
    image_counts,
    expert_ids,
    pair_keep,
    norm1_gain,
    norm1_bias,
    qkv_weight,
    out_weight,
    norm2_gain,
    norm2_bias,
    router_weight,
    expert_in,
    expert_out,
):
    images, piece_len, features = block_in.shape
    pieces = lax.axis_size("seq")
    groups = lax.axis_size("fsdp")
    seq_place = lax.axis_index("seq")
    group_place = lax.axis_index("fsdp")
    rows = images * piece_len
    slots = pieces * piece_len
    heads_here = HEADS // pieces
    cols = heads_here * HD
    hidden_size = expert_in.shape[2]
    capacity = rows * TOPK * 9 // (EXPERTS * 8) + 1
    inv_root = HD ** (-0.5)
    in_rows = expert_in.shape[0]
    out_rows = expert_out.shape[0]

    small = jnp.concatenate(
        [
            jnp.stack([norm1_gain, norm1_bias, norm2_gain, norm2_bias], axis=1),
            router_weight,
            out_weight,
            lax.dynamic_index_in_dim(
                qkv_weight.reshape(-1, 3, pieces, cols), seq_place, 2, keepdims=False
            ).reshape(-1, 3 * cols),
        ],
        axis=1,
    )
    small_full = lax.all_gather(small, "fsdp", axis=0, tiled=True)
    gain_one, bias_one, gain_two, bias_two = [small_full[:, i].astype(F32) for i in range(4)]
    router_full = small_full[:, 4 : 4 + EXPERTS]
    out_full = small_full[:, 4 + EXPERTS : 4 + EXPERTS + features]
    qkv_here = small_full[:, 4 + EXPERTS + features :]
    up_here = lax.all_gather(
        lax.dynamic_index_in_dim(expert_in, seq_place, 1, keepdims=False), "fsdp", axis=0, tiled=True
    )
    down_here = lax.all_gather(
        lax.dynamic_index_in_dim(expert_out, seq_place, 1, keepdims=False), "fsdp", axis=0, tiled=True
    )

    own_slots = slot_holds(jnp.reshape(seq_place, (1,)), piece_len, SEQ_LEN, pieces).reshape(piece_len)
    key_ok = slot_holds(jnp.arange(pieces, dtype=jnp.int32), piece_len, SEQ_LEN, pieces).reshape(slots)
    group_count = jnp.sum(
        jnp.where(jnp.arange(image_counts.shape[0], dtype=jnp.int32) == group_place, image_counts, 0)
    )
    token_ok = (
        (jnp.arange(images, dtype=jnp.int32) < group_count)[:, None] & own_slots[None, :]
    ).reshape(rows)

    flat_in = block_in.reshape(rows, features)
    normed_one, unit_one, root_one = layer_norm(flat_in, gain_one, bias_one)
    low_one = normed_one.astype(BF16)
    low_all = lax.all_gather(low_one.reshape(images, piece_len, features), "seq", axis=1, tiled=True)
    projected = dot32(low_all, qkv_here, ((2,), (0,))).astype(BF16)
    by_heads = projected.reshape(images, slots, 3, heads_here, HD).transpose(2, 0, 3, 1, 4)
    queries, key_rows, value_rows = by_heads[0], by_heads[1], by_heads[2]
    scores = jnp.einsum("ihqd,ihkd->ihqk", queries, key_rows, preferred_element_type=F32) * inv_root
    scores = jnp.where(key_ok[None, None, None, :], scores, -1e30)
    raised = jnp.exp(scores - jnp.max(scores, axis=-1, keepdims=True))
    attn = raised / jnp.sum(raised, axis=-1, keepdims=True)
    attn_low = attn.astype(BF16)
    context = jnp.einsum("ihqk,ihkd->iqhd", attn_low, value_rows, preferred_element_type=F32).astype(BF16)
    context_rows = lax.all_to_all(
        context.reshape(images, slots, 1, cols), "seq", split_axis=1, concat_axis=2, tiled=True
    ).reshape(rows, features)
    middle = flat_in + dot32(context_rows, out_full, ((1,), (0,)))
    normed_two, unit_two, root_two = layer_norm(middle, gain_two, bias_two)
    low_two = normed_two.astype(BF16)
    probs = jax.nn.softmax(dot32(low_two, router_full, ((1,), (0,))), axis=-1)

    expert_rows = expert_ids.reshape(rows, TOPK)
    usable = (pair_keep.reshape(rows, TOPK) == 1) & token_ok[:, None]
    hit = jnp.any(
        (expert_rows[:, :, None] == jnp.arange(EXPERTS, dtype=jnp.int32)) & usable[:, :, None], axis=1
    )
    earlier = (jnp.arange(rows)[:, None] > jnp.arange(rows)[None, :]).astype(BF16)
    place = dot32(earlier, hit.astype(BF16), ((1,), (0,))).astype(jnp.int32)
    place = jnp.where(hit, place, -1)
    select = (place.T[:, None, :] == jnp.arange(capacity, dtype=jnp.int32)[None, :, None]).astype(BF16)
    weight = jnp.where(hit, probs, 0.0)

    dispatched = dot32(select, low_two, ((2,), (0,))).astype(BF16)
    arrived = lax.all_to_all(dispatched, "seq", split_axis=0, concat_axis=0, tiled=True)
    arrived = arrived.reshape(pieces * capacity, features)
    hidden = dot32(arrived, up_here, ((1,), (0,)))
    activated, gelu_back = jax.vjp(lambda u: jax.nn.gelu(u, approximate=False), hidden)
    low_act = activated.astype(BF16)
    returned = dot32(low_act, down_here, ((1,), (0,))).astype(BF16)
    returned = lax.all_to_all(
        returned.reshape(pieces, capacity, features), "seq", split_axis=0, concat_axis=0, tiled=True
    )
    picked = jnp.einsum("est,esd->etd", select, returned, preferred_element_type=F32)
    block_out = middle + jnp.sum(weight.T[:, :, None] * picked, axis=0)
    misfit = (block_out - teacher.reshape(rows, features)) * token_ok.astype(F32)[:, None]
    loss_here = jnp.sum(misfit * misfit)

    pair_grad = (weight.T[:, :, None] * misfit[None]).astype(BF16)
    returned_grad = jnp.einsum("est,etd->esd", select, pair_grad, preferred_element_type=F32).astype(BF16)
    prob_grad = jnp.where(hit, jnp.sum(picked * misfit[None], axis=2).T, 0.0)
    grad_arrived = lax.all_to_all(returned_grad, "seq", split_axis=0, concat_axis=0, tiled=True).reshape(
        pieces * capacity, features
    )
    hidden_grad = gelu_back(dot32(grad_arrived, down_here, ((1,), (1,))))[0].astype(BF16)
    grad_down = dot32(low_act, grad_arrived, ((0,), (0,))).astype(BF16)
    grad_up = dot32(arrived, hidden_grad, ((0,), (0,))).astype(BF16)
    dispatch_grad = dot32(hidden_grad, up_here, ((1,), (1,))).astype(BF16)
    dispatch_grad = lax.all_to_all(
        dispatch_grad.reshape(pieces, capacity, features), "seq", split_axis=0, concat_axis=0, tiled=True
    )
    owned_down = lax.psum_scatter(grad_down, "fsdp", scatter_dimension=0, tiled=True)
    owned_up = lax.psum_scatter(grad_up, "fsdp", scatter_dimension=0, tiled=True)

    logit_grad = probs * (prob_grad - jnp.sum(probs * prob_grad, axis=1, keepdims=True))
    grad_router = lax.dot_general(
        low_two.astype(F32), logit_grad, (((0,), (0,)), ((), ())), precision=PRECISE
    )
    normed_two_grad = jnp.einsum("est,esd->td", select, dispatch_grad, preferred_element_type=F32)
    normed_two_grad = normed_two_grad + lax.dot_general(
        logit_grad, router_full.astype(F32), (((1,), (1,)), ((), ())), precision=PRECISE
    )
    grad_gain_two = jnp.sum(normed_two_grad * unit_two, axis=0)
    grad_bias_two = jnp.sum(normed_two_grad, axis=0)
    middle_grad = misfit + layer_norm_back(normed_two_grad, unit_two, root_two, gain_two)
    attended_grad = middle_grad.astype(BF16)
    grad_out_w = dot32(context_rows, attended_grad, ((0,), (0,))).astype(BF16)
    context_grad = dot32(attended_grad, out_full, ((1,), (1,))).astype(BF16)
    heads_grad = lax.all_to_all(
        context_grad.reshape(images, piece_len, pieces, cols), "seq", split_axis=2, concat_axis=1, tiled=True
    ).reshape(images, slots, heads_here, HD)
    value_grad = jnp.einsum("ihqk,iqhd->ikhd", attn_low, heads_grad, preferred_element_type=F32)
    share_grad = jnp.einsum("iqhd,ihkd->ihqk", heads_grad, value_rows, preferred_element_type=F32)
    score_grad = (attn * (share_grad - jnp.sum(attn * share_grad, axis=-1, keepdims=True))).astype(BF16)
    query_grad = jnp.einsum("ihqk,ihkd->iqhd", score_grad, key_rows, preferred_element_type=F32) * inv_root
    key_grad = jnp.einsum("ihqk,ihqd->ikhd", score_grad, queries, preferred_element_type=F32) * inv_root
    heads_back = jnp.stack([query_grad, key_grad, value_grad], axis=2).astype(BF16)
    heads_back = heads_back.reshape(images * slots, 3 * cols)
    grad_qkv = dot32(low_all.reshape(images * slots, features), heads_back, ((0,), (0,))).astype(BF16)
    normed_one_part = dot32(heads_back, qkv_here, ((1,), (1,))).astype(BF16)
    normed_one_grad = lax.psum_scatter(
        normed_one_part.reshape(images, slots, features), "seq", scatter_dimension=1, tiled=True
    ).astype(F32).reshape(rows, features)
    grad_gain_one = jnp.sum(normed_one_grad * unit_one, axis=0)
    grad_bias_one = jnp.sum(normed_one_grad, axis=0)
    input_grad = middle_grad + layer_norm_back(normed_one_grad, unit_one, root_one, gain_one)

    out_share = lax.psum_scatter(grad_out_w, "seq", scatter_dimension=1, tiled=True)
    attn_owned = lax.psum_scatter(
        jnp.concatenate([grad_qkv, out_share], axis=1), "fsdp", scatter_dimension=0, tiled=True
    )
    loss_row = jnp.zeros((features,), F32).at[0].set(loss_here)
    vectors = jnp.concatenate(
        [jnp.stack([grad_gain_one, grad_bias_one, grad_gain_two, grad_bias_two, loss_row]), grad_router.T], axis=0
    )
    vectors = lax.psum(vectors, ("fsdp", "seq"))
    mean_loss = vectors[4, 0] / (
        (jnp.sum(image_counts, dtype=jnp.int32) * SEQ_LEN).astype(F32) * features
    )
    owned_vectors = lax.dynamic_slice_in_dim(vectors, group_place * in_rows, in_rows, axis=1)
    attn_whole = lax.all_gather(attn_owned, "seq", axis=0)
    grad_qkv_w = (
        attn_whole[:, :, : 3 * cols].reshape(pieces, in_rows, 3, cols).transpose(1, 2, 0, 3)
        .reshape(in_rows, 3 * features).astype(F32)
    )
    grad_out_whole = attn_whole[:, :, 3 * cols :].transpose(1, 0, 2).reshape(in_rows, features).astype(F32)
    grad_up_w = lax.all_gather(owned_up, "seq", axis=0).transpose(1, 0, 2).astype(F32)
    grad_down_w = lax.all_gather(owned_down, "seq", axis=0).transpose(1, 0, 2).astype(F32)
    return (
        block_out.reshape(images, piece_len, features),
        mean_loss,
        input_grad.reshape(images, piece_len, features),
        owned_vectors[0],
        owned_vectors[1],
        grad_qkv_w,
        grad_out_whole,
        owned_vectors[2],
        owned_vectors[3],
        owned_vectors[5:].T,
        grad_up_w,
        grad_down_w,
    )


MESH = pl.DeviceIdType.MESH
LANES = 16
STATS = 16
GAIN_ONE, BIAS_ONE, GAIN_TWO, BIAS_TWO = 4, 5, 6, 7
LOSS_ROW = 8


def round_up(value, step):
    return (value + step - 1) // step * step


def flipped(place, bits):
    low, high = lax.rem(place, 2), place // 2
    if bits % 2:
        low = 1 - low
    if bits // 2:
        high = 1 - high
    return high * 2 + low


def unit_rows(values_in):
    centered = values_in - jnp.mean(values_in, axis=1, keepdims=True)
    variance = jnp.mean(centered * centered, axis=1, keepdims=True)
    root = lax.rsqrt(variance + NORM_EPS)
    return centered * root, root


def norm_back(grad_out, unit, root, gain_row):
    scaled = grad_out * gain_row
    return root * (
        scaled
        - jnp.mean(scaled, axis=1, keepdims=True)
        - unit * jnp.mean(scaled * unit, axis=1, keepdims=True)
    )


def hi_lo(values_in):
    high = values_in.astype(BF16)
    return high, (values_in - high.astype(F32)).astype(BF16)


def block_kernel(
    sizes,
    x_in,
    teacher_in,
    counts,
    ids_in,
    keep_in,
    vec_in,
    attn_in,
    up_in,
    down_in,
    block_out,
    input_grad,
    stats_out,
    attn_all,
    up_all,
    down_all,
    vec_all,
    vecs,
    attn_w,
    out_w,
    up_w,
    down_w,
    low_all,
    qkv_s,
    lse_s,
    ctx_s,
    ctx_rows,
    middle,
    misfit,
    low_two,
    select,
    select_t,
    hits,
    weights,
    send_s,
    arrived,
    ret_r,
    back_r,
    dret_r,
    turned,
    act,
    slope,
    grad_down,
    core_down,
    yrecv_down,
    yrecv_up,
    zrecv_down,
    zrecv_up,
    dctx_s,
    half_recv,
    yrecv_attn,
    zrecv_attn,
    part_s,
    part_r,
    stats,
    stats_r,
    send_sem,
    recv_sem,
    local_sem,
    free_sem,
):
    images, piece, padded, cap, features, cols, ffn, in_rows, out_rows = sizes
    rows = images * padded
    slots = 4 * padded
    half_cols, half_ffn = features // 2, ffn // 2
    wide = ffn // 6
    f = lax.axis_index("fsdp")
    s = lax.axis_index("seq")
    z, y = f // 2, lax.rem(f, 2)
    inv_root = HD ** (-0.5)
    same = [flipped(z, k) * 2 + y for k in range(4)]
    other = [flipped(z, k) * 2 + (1 - y) for k in range(4)]
    near = [flipped(s, r) for r in range(4)]
    zb, xb, core = lax.rem(z, 2), s // 2, lax.rem(s, 2)
    named_by = [flipped(zb * 2 + xb, r) for r in range(4)]
    cluster = [(f, s), (f, near[2]), (same[1], s), (same[1], near[2])]
    counter = [0, 0]
    pending = []

    def send(src, dst, group, seq):
        i = counter[0]
        counter[0] += 1
        copy = pltpu.make_async_remote_copy(
            src_ref=src,
            dst_ref=dst,
            send_sem=send_sem.at[i],
            recv_sem=recv_sem.at[i],
            device_id=(group, seq),
            device_id_type=MESH,
        )
        copy.start()
        pending.append(copy)
        return copy

    def done_sending(copy):
        pending[:] = [other_copy for other_copy in pending if other_copy is not copy]
        copy.wait_send()

    def local(src, dst):
        i = counter[1]
        counter[1] += 1
        copy = pltpu.make_async_copy(src, dst, local_sem.at[i])
        copy.start()
        return copy

    barrier = pltpu.get_barrier_semaphore()
    for g in same[1:] + other:
        pl.semaphore_signal(barrier, inc=1, device_id=(g, s), device_id_type=MESH)
    for q in near[1:]:
        pl.semaphore_signal(barrier, inc=1, device_id=(f, q), device_id_type=MESH)
    pl.semaphore_signal(barrier, inc=1, device_id=cluster[3], device_id_type=MESH)
    pl.semaphore_wait(barrier, 11)

    vec_copies = [send(vec_in, vec_all.at[f], g, s) for g in same[1:] + other]
    vec_all[f] = vec_in[...]

    def spot(ref, n, g):
        return ref.at[pl.ds(pl.multiple_of(g * n, n), n), :]

    def gather_start(src, dst, n):
        along_z = [None] + [send(src, spot(dst, n, f), same[k], s) for k in (1, 2, 3)]
        across = [send(src, spot(dst, n, f), other[0], s)]
        return along_z, across, local(src, spot(dst, n, f))

    def gather_pass(flow, dst, n, k):
        along_z, across, _ = flow
        along_z[k].wait_recv()
        across.append(send(spot(dst, n, same[k]), spot(dst, n, same[k]), other[0], s))

    def gather_end(flow):
        for copy in flow[1]:
            copy.wait_recv()
        flow[2].wait()

    attn_flow = gather_start(attn_in, attn_w, in_rows)

    def up_spot(g):
        return up_w.at[
            pl.ds(pl.multiple_of(g * in_rows, in_rows), in_rows),
            pl.ds(pl.multiple_of(core * half_ffn, half_ffn), half_ffn),
        ]

    def down_spot(g):
        return down_w.at[
            pl.ds(pl.multiple_of(g * out_rows, out_rows), out_rows),
            pl.ds(pl.multiple_of(core * half_cols, half_cols), half_cols),
        ]

    def expert_start(src, at):
        own, odd = src.at[zb], src.at[1 - zb]
        along_z = [None] + [send(odd if k % 2 else own, at(f), same[k], s) for k in (1, 2, 3)]
        across = [send(own, at(f), other[0], s)]
        to_core = [send(own, at(f), f, near[1])]
        return along_z, across, to_core, local(own, at(f))

    def expert_pass(flow, at, k):
        flow[0][k].wait_recv()
        ref = at(same[k])
        flow[1].append(send(ref, ref, other[0], s))
        flow[2].append(send(ref, ref, f, near[1]))

    def expert_end(flow, at):
        for k in range(4):
            flow[1][k].wait_recv()
            ref = at(other[k])
            flow[2].append(send(ref, ref, f, near[1]))
        for copy in flow[2]:
            copy.wait_recv()
        flow[3].wait()

    def near_of(shape, axis):
        at = lax.broadcasted_iota(jnp.int32, shape, axis)
        named = jnp.full(shape, -1, jnp.int32)
        for r in range(4):
            named = jnp.where(at == r, named_by[r], named)
        return named

    own_len = SEQ_LEN // 4 + jnp.where(s < SEQ_LEN % 4, 1, 0)
    at_piece = lax.broadcasted_iota(jnp.int32, (1, piece), 1)
    route_rows = jnp.zeros((rows, LANES), F32)
    route_cols = jnp.zeros((LANES, rows), F32)
    for i in range(images):
        ok = jnp.where((at_piece < own_len) & (i < counts[f]), 1.0, 0.0)
        facts = jnp.concatenate(
            [
                ids_in[i].astype(F32),
                jnp.where(keep_in[i] == 1, 1.0, 0.0) * ok,
                ok,
                jnp.zeros((LANES - 5, piece), F32),
            ],
            axis=0,
        ).astype(BF16)
        spread = jnp.where(
            lax.broadcasted_iota(jnp.int32, (piece, rows), 0) + i * padded
            == lax.broadcasted_iota(jnp.int32, (piece, rows), 1),
            1.0,
            0.0,
        ).astype(BF16)
        route_cols = route_cols + dot32(facts, spread, ((1,), (0,)))
        route_rows = route_rows + dot32(spread, facts, ((0,), (1,)))
    token_ok = route_rows[:, 4:5]
    hits[:, LANES:] = token_ok
    route_rows = route_rows.astype(jnp.int32)
    route_cols = route_cols.astype(jnp.int32)
    named = near_of((rows, LANES), 1)
    hit = ((route_rows[:, 0:1] == named) & (route_rows[:, 2:3] == 1)) | (
        (route_rows[:, 1:2] == named) & (route_rows[:, 3:4] == 1)
    )
    hit_f = jnp.where(hit, 1.0, 0.0)
    before = (
        lax.broadcasted_iota(jnp.int32, (rows, rows), 0) > lax.broadcasted_iota(jnp.int32, (rows, rows), 1)
    )
    before = jnp.where(before, 1.0, 0.0).astype(BF16)
    place = dot32(before, hit_f.astype(BF16), ((1,), (0,)))
    place = jnp.where(hit, place, -1.0)
    hits[:, 0:LANES] = hit_f
    named_t = near_of((LANES, rows), 0)
    hit_t = ((route_cols[0:1, :] == named_t) & (route_cols[2:3, :] == 1)) | (
        (route_cols[1:2, :] == named_t) & (route_cols[3:4, :] == 1)
    )
    hit_tf = jnp.where(hit_t, 1.0, 0.0).astype(BF16)
    place_t = dot32(hit_tf, before, ((1,), (1,)))
    place_t = jnp.where(hit_t, place_t, -1.0)
    slot_down = lax.broadcasted_iota(jnp.int32, (cap, rows), 0).astype(F32)
    slot_along = lax.broadcasted_iota(jnp.int32, (rows, cap), 1).astype(F32)
    for r in range(4):
        select[r] = jnp.where(place_t[r : r + 1, :] == slot_down, 1.0, 0.0).astype(BF16)
        select_t[r] = jnp.where(place[:, r : r + 1] == slot_along, 1.0, 0.0).astype(BF16)

    for copy in vec_copies:
        copy.wait_recv()
    at_row = lax.broadcasted_iota(jnp.int32, (128, features), 0)
    at_col = lax.broadcasted_iota(jnp.int32, (128, features), 1)
    total = jnp.zeros((STATS, features), F32)
    for g in range(8):
        spread = jnp.where((at_col - g * in_rows == at_row) & (at_row < in_rows), 1.0, 0.0).astype(BF16)
        total = total + dot32(vec_all[g], spread, ((1,), (0,)))
    vecs[...] = total

    low_all[s] = jnp.zeros((rows, features), BF16)
    for i in range(images):
        unit, _ = unit_rows(x_in[:, i, :])
        low_all[s, i * padded : i * padded + piece, :] = (
            unit * vecs[GAIN_ONE : GAIN_ONE + 1, :] + vecs[BIAS_ONE : BIAS_ONE + 1, :]
        ).astype(BF16)
    low_x = send(low_all.at[s], low_all.at[s], f, near[2])
    low_c = send(low_all.at[s], low_all.at[s], f, near[1])

    for k in (1, 2, 3):
        gather_pass(attn_flow, attn_w, in_rows, k)
    up_flow = expert_start(up_in, up_spot)
    down_flow = expert_start(down_in, down_spot)
    low_x.wait_recv()
    low_d = send(low_all.at[near[2]], low_all.at[near[2]], f, near[1])
    gather_end(attn_flow)
    mine = lax.rem(s, 2)
    here = pl.ds(pl.multiple_of(mine * half_cols, half_cols), half_cols)
    there = pl.ds(pl.multiple_of((1 - mine) * half_cols, half_cols), half_cols)
    out_half = send(attn_w.at[:, pl.ds(0, half_cols)], out_w.at[:, here], f, near[1])
    out_w[:, here] = attn_w[:, 0:half_cols]

    def project(j):
        found = dot32(low_all[j], attn_w[:, half_cols:], ((1,), (0,))).astype(BF16)
        for i in range(images):
            qkv_s[i, pl.ds(pl.multiple_of(j * padded, padded), padded), :] = found[
                i * padded : (i + 1) * padded, :
            ]

    project(s)
    low_c.wait_recv()
    project(near[1])
    project(near[2])
    low_d.wait_recv()
    project(near[3])

    key_at = lax.broadcasted_iota(jnp.int32, (slots, 1), 0)
    key_piece = jnp.zeros((slots, 1), jnp.int32)
    for j in range(1, 4):
        key_piece = key_piece + jnp.where(key_at >= j * padded, 1, 0)
    key_len = SEQ_LEN // 4 + jnp.where(key_piece < SEQ_LEN % 4, 1, 0)
    key_ok = key_at - key_piece * padded < key_len

    def heads_of(ref, i, kind, h):
        return ref[i, :, kind * cols + h * HD : kind * cols + (h + 1) * HD]

    def scores_of(i, h):
        found = dot32(heads_of(qkv_s, i, 1, h), heads_of(qkv_s, i, 0, h), ((1,), (1,))) * inv_root
        return jnp.where(key_ok, found, -1e30)

    for k in (1, 2, 3):
        expert_pass(up_flow, up_spot, k)

    @pl.loop(0, images)
    def _(i):
        found = []
        for h in range(cols // HD):
            scores = scores_of(i, h)
            highest = jnp.max(scores, axis=0, keepdims=True)
            raised = jnp.exp(scores - highest)
            total = jnp.sum(raised, axis=0, keepdims=True)
            shares = (raised * (1.0 / total)).astype(BF16)
            lse_s[i, h : h + 1, :] = highest + jnp.log(total)
            found.append(dot32(heads_of(qkv_s, i, 2, h), shares, ((0,), (0,))))
        ctx_s[i] = jnp.concatenate(found, axis=0).T.astype(BF16)

    def piece_rows(ref, j):
        return ref.at[:, pl.ds(pl.multiple_of(j * padded, padded), padded), :]

    ctx_copies = [send(piece_rows(ctx_s, near[r]), ctx_rows.at[s], f, near[r]) for r in (2, 3, 1)]
    ctx_rows[s] = ctx_s[:, pl.ds(pl.multiple_of(s * padded, padded), padded), :]
    expert_pass(down_flow, down_spot, 1)
    out_half.wait_recv()
    for copy in ctx_copies:
        copy.wait_recv()
        done_sending(copy)

    attended = jnp.zeros((rows, features), F32)
    for j in range(4):
        attended = attended + dot32(
            ctx_rows[j].reshape(rows, cols), out_w[j * cols : (j + 1) * cols, :], ((1,), (0,))
        )
    middle[...] = attended
    for i in range(images):
        at = slice(i * padded, i * padded + piece)
        middle[at, :] = middle[at, :] + x_in[:, i, :]
    unit, _ = unit_rows(middle[...])
    low_two[...] = (unit * vecs[GAIN_TWO : GAIN_TWO + 1, :] + vecs[BIAS_TWO : BIAS_TWO + 1, :]).astype(BF16)
    router = vecs[...].astype(BF16)

    def probs_of():
        logits = dot32(low_two[...], router, ((1,), (1,)))
        real = lax.broadcasted_iota(jnp.int32, (rows, LANES), 1) < EXPERTS
        logits = jnp.where(real, logits, -1e30)
        raised = jnp.exp(logits - jnp.max(logits, axis=1, keepdims=True))
        return raised / jnp.sum(raised, axis=1, keepdims=True)

    disp_copies = []
    for r in (3, 2, 1, 0):
        found = dot32(select[r], low_two[...], ((1,), (0,))).astype(BF16)
        if r:
            send_s[r - 1] = found
            disp_copies.append(send(send_s.at[r - 1], arrived.at[r], *cluster[r]))
        else:
            arrived[0] = found
    probs = probs_of()
    lane = lax.broadcasted_iota(jnp.int32, (rows, LANES), 1)
    chosen = jnp.zeros((rows, LANES), F32)
    for r in range(4):
        value = jnp.sum(jnp.where(lane == named_by[r], probs, 0.0), axis=1, keepdims=True)
        chosen = jnp.where(lane == r, value, chosen)
    weights[...] = chosen * hits[:, 0:LANES]

    expert_end(up_flow, up_spot)
    for k in (2, 3):
        expert_pass(down_flow, down_spot, k)

    def expert_up(half):
        given = arrived[2 * half : 2 * half + 2].reshape(2 * cap, features)

        @pl.loop(0, 6)
        def _(t):
            tile = pl.ds(pl.multiple_of(t * wide, wide), wide)
            hidden = dot32(given, up_w[:, tile], ((1,), (0,)))
            phi = 0.5 * (1.0 + lax.erf(hidden * (2.0**-0.5)))
            at = slice(2 * half * cap, 2 * (half + 1) * cap)
            act[at, tile] = (hidden * phi).astype(BF16)
            slope[at, tile] = (phi + hidden * jnp.exp(-0.5 * hidden * hidden) * 0.3989422804014327).astype(BF16)

    disp_copies[2].wait_recv()
    expert_up(0)
    disp_copies[1].wait_recv()
    disp_copies[0].wait_recv()
    expert_up(1)
    for copy in disp_copies:
        done_sending(copy)
    expert_end(down_flow, down_spot)

    def to_rows(left, right, dims, half, dst):
        at = slice(2 * half * cap, 2 * (half + 1) * cap)
        found = dot32(left[at, :], right[...], dims).astype(BF16)
        out = []
        for r in (2 * half + 1, 2 * half):
            part = found[(r - 2 * half) * cap : (r - 2 * half + 1) * cap, :]
            if r:
                send_s[r - 1] = part
                out.append(send(send_s.at[r - 1], dst.at[r], *cluster[r]))
            else:
                dst[0] = part
        return out

    ret_copies = to_rows(act, down_w, ((1,), (0,)), 1, ret_r)
    ret_copies += to_rows(act, down_w, ((1,), (0,)), 0, ret_r)
    for i in range(images):
        at = slice(i * padded, i * padded + piece)
        misfit[at, :] = teacher_in[:, i, :]
        misfit[i * padded + piece : (i + 1) * padded, :] = jnp.zeros((padded - piece, features), F32)
    for copy in ret_copies:
        copy.wait_recv()

    found = middle[...]
    for r in range(4):
        found = found + weights[:, r : r + 1] * dot32(select_t[r], ret_r[r], ((1,), (0,)))
    for i in range(images):
        block_out[:, i, :] = found[i * padded : i * padded + piece, :]
    wrong = (found - misfit[...]) * hits[:, LANES:]
    misfit[...] = wrong
    for copy in ret_copies:
        done_sending(copy)
    dret_copies = []
    for r in (3, 2, 1, 0):
        pair = (weights[:, r : r + 1] * misfit[...]).astype(BF16)
        part = dot32(select[r], pair, ((1,), (0,))).astype(BF16)
        if r:
            send_s[r - 1] = part
            dret_copies.append(send(send_s.at[r - 1], dret_r.at[r], *cluster[r]))
        else:
            dret_r[0] = part
    stats[...] = jnp.zeros_like(stats)
    stats[LOSS_ROW : LOSS_ROW + 1, :] = jnp.sum(wrong * wrong, axis=0, keepdims=True)
    probs = probs_of()
    prob_grad = jnp.zeros((rows, LANES), F32)
    for r in range(4):
        picked = dot32(select_t[r], ret_r[r], ((1,), (0,)))
        value = jnp.sum(picked * misfit[...], axis=1, keepdims=True) * hits[:, r : r + 1]
        prob_grad = jnp.where(lane == named_by[r], value, prob_grad)
    logit_grad = probs * (prob_grad - jnp.sum(probs * prob_grad, axis=1, keepdims=True))
    high, low = hi_lo(logit_grad)
    router_grad = dot32(high, low_two[...], ((0,), (0,))) + dot32(low, low_two[...], ((0,), (0,)))
    stats[0:EXPERTS, :] = router_grad[0:EXPERTS, :]
    for copy in dret_copies:
        copy.wait_recv()

    given = dret_r[...].reshape(4 * cap, features)
    turned[...] = given.T

    @pl.loop(0, 8)
    def _(g):
        grad_down[g] = dot32(
            turned[...], act[:, pl.ds(pl.multiple_of(g * out_rows, out_rows), out_rows)], ((1,), (0,))
        ).astype(BF16)

    def half_at(ref, half, n):
        return ref.at[:, pl.ds(pl.multiple_of(half * n, n), n), :]

    core_copy = send(half_at(grad_down, 1 - core, half_cols), core_down, f, near[1])

    def down_block(g):
        return grad_down.at[g, pl.ds(pl.multiple_of(core * half_cols, half_cols), half_cols), :]

    def down_core(g):
        return core_down[g].astype(F32)

    def up_core(g):
        at = pl.ds(pl.multiple_of(lax.rem(g, 4) * in_rows, in_rows), in_rows)
        return slope[at, pl.ds(pl.multiple_of(g // 4 * half_ffn, half_ffn), half_ffn)].astype(F32)

    def attn_block(g):
        return spot(attn_w, in_rows, g)

    def sum_start(block, extra, yrecv):
        flow = {}
        for k in (3, 2, 1, 0):
            ref = block(other[k])
            if extra is not None:
                ref[...] = (ref[...].astype(F32) + extra(other[k])).astype(BF16)
            flow[k] = send(ref, yrecv.at[k], other[0], s)
        return flow

    def sum_pass(flow, block, extra, yrecv, zrecv, k):
        flow[k].wait_recv()
        ref = block(same[k])
        total = ref[...].astype(F32) + yrecv[k].astype(F32)
        if extra is not None:
            total = total + extra(same[k])
        ref[...] = total.astype(BF16)
        if k:
            flow["z%d" % k] = send(ref, zrecv.at[k - 1], same[k], s)

    def sum_end(flow, block, zrecv, dst):
        ref = block(f)
        for k in (1, 2, 3):
            flow["z%d" % k].wait_recv()
        total = ref[...].astype(F32)
        for k in (1, 2, 3):
            total = total + zrecv[k - 1].astype(F32)
        ref[...] = total.astype(BF16)
        return share(ref, dst.at[s], dst.at[near[2]])

    def share(ref, own, of_x):
        return send(ref, own, f, near[2]), send(ref, own, f, near[1]), local(ref, own), of_x

    def expert_sum_end(flow, block, yrecv, zrecv, own, of_x, turn):
        for k in (1, 2, 3):
            flow["z%d" % k].wait_recv()
        totals = (
            block(f)[...].astype(F32) + zrecv[1].astype(F32),
            zrecv[0].astype(F32) + zrecv[2].astype(F32),
        )
        for parity, total in zip((zb, 1 - zb), totals):
            yrecv[parity] = (total.T if turn else total).astype(BF16)
        return share(yrecv.at[pl.ds(0, 2)], own, of_x)

    def down_all_at(x):
        return down_all.at[:, x, :, pl.ds(pl.multiple_of(core * half_cols, half_cols), half_cols)]

    def up_all_at(x):
        return up_all.at[:, x, :, pl.ds(pl.multiple_of(core * half_ffn, half_ffn), half_ffn)]

    def share_pass(flow):
        flow[0].wait_recv()
        return send(flow[3], flow[3], f, near[1])

    @pl.loop(0, 6)
    def _(t):
        tile = pl.ds(pl.multiple_of(t * wide, wide), wide)
        found = dot32(dret_r[...].reshape(4 * cap, features), down_w[tile, :], ((1,), (1,)))
        act[:, tile] = (found * slope[:, tile].astype(F32)).astype(BF16)

    pl.semaphore_signal(free_sem, inc=1, device_id=(f, near[1]), device_id_type=MESH)
    for copy in dret_copies:
        done_sending(copy)
    core_copy.wait_recv()
    down_sum = sum_start(down_block, down_core, yrecv_down)
    back_copies = to_rows(act, up_w, ((1,), (1,)), 1, back_r)
    back_copies += to_rows(act, up_w, ((1,), (1,)), 0, back_r)
    sum_pass(down_sum, down_block, down_core, yrecv_down, zrecv_down, 3)
    for copy in up_flow[1] + up_flow[2]:
        done_sending(copy)
    given = arrived[...].reshape(4 * cap, features)
    turned[...] = given.T

    @pl.loop(0, 6)
    def _(t):
        tile = pl.ds(pl.multiple_of(t * wide, wide), wide)
        up_w[:, tile] = dot32(turned[...], act[:, tile], ((1,), (0,))).astype(BF16)

    pl.semaphore_wait(free_sem, 1)
    there_ffn = pl.ds(pl.multiple_of((1 - core) * half_ffn, half_ffn), half_ffn)
    up_copies = [
        send(
            up_w.at[pl.ds(h * 4 * in_rows, 4 * in_rows), there_ffn],
            slope.at[pl.ds(0, 4 * in_rows), pl.ds(h * half_ffn, half_ffn)],
            f,
            near[1],
        )
        for h in (0, 1)
    ]
    sum_pass(down_sum, down_block, down_core, yrecv_down, zrecv_down, 2)

    normed_grad = dot32(high, router, ((1,), (0,))) + dot32(low, router, ((1,), (0,)))
    for copy in up_copies:
        copy.wait_recv()
        done_sending(copy)
    up_sum = sum_start(up_spot, up_core, yrecv_up)
    for copy in back_copies:
        copy.wait_recv()
    for r in range(4):
        normed_grad = normed_grad + dot32(select_t[r], back_r[r], ((1,), (0,)))
    unit, root = unit_rows(middle[...])
    stats[GAIN_TWO : GAIN_TWO + 1, :] = jnp.sum(normed_grad * unit, axis=0, keepdims=True)
    stats[BIAS_TWO : BIAS_TWO + 1, :] = jnp.sum(normed_grad, axis=0, keepdims=True)
    middle_grad = misfit[...] + norm_back(normed_grad, unit, root, vecs[GAIN_TWO : GAIN_TWO + 1, :])
    middle[...] = middle_grad
    low_two[...] = middle_grad.astype(BF16)

    dctx_copies = []
    for r in (2, 3, 1, 0):
        block = out_w[pl.ds(pl.multiple_of(near[r] * cols, cols), cols), :]
        found = dot32(low_two[...], block, ((1,), (1,))).astype(BF16).reshape(images, padded, cols)
        if r:
            dctx_s[r - 1] = found
            dctx_copies.append(send(dctx_s.at[r - 1], piece_rows(ctx_s, s), f, near[r]))
        else:
            ctx_s[:, pl.ds(pl.multiple_of(s * padded, padded), padded), :] = found
    done_sending(out_half)
    for j in range(4):
        out_w[j * cols : (j + 1) * cols, :] = dot32(
            ctx_rows[j].reshape(rows, cols), low_two[...], ((0,), (0,))
        ).astype(BF16)
    half_copy = send(out_w.at[:, there], half_recv, f, near[1])
    sum_pass(down_sum, down_block, down_core, yrecv_down, zrecv_down, 1)
    for copy in dctx_copies:
        copy.wait_recv()

    @pl.loop(0, images)
    def _(i):
        found = [[], [], []]
        for h in range(cols // HD):
            shares = jnp.exp(scores_of(i, h) - lse_s[i, h : h + 1, :])
            given = ctx_s[i, :, h * HD : (h + 1) * HD]
            found[2].append(dot32(shares.astype(BF16), given, ((1,), (0,))))
            share_grad = dot32(heads_of(qkv_s, i, 2, h), given, ((1,), (1,)))
            across = jnp.sum(shares * share_grad, axis=0, keepdims=True)
            score_grad = (shares * (share_grad - across)).astype(BF16)
            found[1].append(dot32(score_grad, heads_of(qkv_s, i, 0, h), ((1,), (0,))) * inv_root)
            query_t = dot32(heads_of(qkv_s, i, 1, h), score_grad, ((0,), (0,))) * inv_root
            found[0].append(query_t.T)
        for kind in range(3):
            whole = jnp.concatenate(found[kind], axis=1).astype(BF16)
            found[kind] = whole
        qkv_s[i] = jnp.concatenate(found, axis=1)

    sum_pass(down_sum, down_block, down_core, yrecv_down, zrecv_down, 0)

    def dqkv_rows(j):
        return qkv_s[:, pl.ds(pl.multiple_of(j * padded, padded), padded), :].reshape(rows, 3 * cols)

    def low_part(j):
        return dot32(dqkv_rows(j), attn_w[:, half_cols:], ((1,), (1,)))

    part_s[0] = low_part(near[3]).astype(BF16)
    part_c = send(part_s.at[0], part_r.at[0], f, near[1])
    part_s[1] = low_part(near[1]).astype(BF16)
    part_d = send(part_s.at[1], part_r.at[1], f, near[1])
    for_x = low_part(near[2])
    part_c.wait_recv()
    part_s[2] = (for_x + part_r[0].astype(F32)).astype(BF16)
    part_x = send(part_s.at[2], part_r.at[2], f, near[2])
    sum_pass(up_sum, up_spot, up_core, yrecv_up, zrecv_up, 3)
    down_share = expert_sum_end(
        down_sum, down_block, yrecv_down, zrecv_down, down_all_at(xb), down_all_at(1 - xb), True
    )

    misfit[...] = low_part(s)

    for copy in attn_flow[1]:
        done_sending(copy)
    qkv_grad = jnp.zeros((features, 3 * cols), F32)
    for i in range(images):
        given = low_all[:, i * padded : (i + 1) * padded, :].reshape(4 * padded, features)
        qkv_grad = qkv_grad + dot32(given, qkv_s[i], ((0,), (0,)))
    attn_w[:, half_cols:] = qkv_grad.astype(BF16)
    half_copy.wait_recv()
    attn_w[:, 0:half_cols] = (out_w[:, here].astype(F32) + half_recv[...].astype(F32)).astype(BF16)
    attn_sum = sum_start(attn_block, None, yrecv_attn)
    sum_pass(up_sum, up_spot, up_core, yrecv_up, zrecv_up, 2)

    part_d.wait_recv()
    low_grad = misfit[...] + part_r[1].astype(F32)
    part_x.wait_recv()
    low_grad = low_grad + part_r[2].astype(F32)
    misfit[...] = low_grad
    stats[BIAS_ONE : BIAS_ONE + 1, :] = jnp.sum(low_grad, axis=0, keepdims=True)
    gain_grad = jnp.zeros((1, features), F32)
    for i in range(images):
        at = slice(i * padded, i * padded + piece)
        unit, root = unit_rows(x_in[:, i, :])
        gain_grad = gain_grad + jnp.sum(misfit[at, :] * unit, axis=0, keepdims=True)
        input_grad[:, i, :] = middle[at, :] + norm_back(misfit[at, :], unit, root, vecs[GAIN_ONE : GAIN_ONE + 1, :])
    stats[GAIN_ONE : GAIN_ONE + 1, :] = gain_grad

    seq_copies = [send(stats, stats_r.at[r - 1], f, near[r]) for r in (1, 2, 3)]
    down_last = share_pass(down_share)
    for copy in seq_copies:
        copy.wait_recv()
        done_sending(copy)
    stats[...] = stats[...] + stats_r[0] + stats_r[1] + stats_r[2]
    y_copy = send(stats, stats_r.at[3], other[0], s)
    sum_pass(up_sum, up_spot, up_core, yrecv_up, zrecv_up, 1)
    y_copy.wait_recv()
    done_sending(y_copy)
    stats[...] = stats[...] + stats_r[3]
    z_copies = [send(stats, stats_r.at[3 + k], same[k], s) for k in (1, 2, 3)]
    sum_pass(up_sum, up_spot, up_core, yrecv_up, zrecv_up, 0)
    for copy in z_copies:
        copy.wait_recv()
    stats_out[...] = stats[...] + stats_r[4] + stats_r[5] + stats_r[6]

    up_share = expert_sum_end(up_sum, up_spot, yrecv_up, zrecv_up, up_all_at(xb), up_all_at(1 - xb), False)
    for k in (3, 2, 1, 0):
        sum_pass(attn_sum, attn_block, None, yrecv_attn, zrecv_attn, k)
    up_last = share_pass(up_share)
    attn_share = sum_end(attn_sum, attn_block, zrecv_attn, attn_all)
    attn_last = share_pass(attn_share)
    for share, last in ((down_share, down_last), (up_share, up_last), (attn_share, attn_last)):
        share[1].wait_recv()
        share[2].wait()
        last.wait_recv()
    for copy in list(pending):
        done_sending(copy)


def run_block(sizes, operands):
    images, piece, padded, cap, features, cols, ffn, in_rows, out_rows = sizes
    rows = images * padded
    half_cols, half_ffn = features // 2, ffn // 2
    pack = half_cols + 3 * cols
    shape = jax.ShapeDtypeStruct
    vmem = pl.BlockSpec(memory_space=pltpu.VMEM)
    hbm = pl.BlockSpec(memory_space=pl.ANY)
    scratch = [
        pltpu.VMEM((8, STATS, 128), BF16),
        pltpu.VMEM((STATS, features), F32),
        pltpu.VMEM((8 * in_rows, pack), BF16),
        pltpu.VMEM((features, features), BF16),
        pltpu.VMEM((features, ffn), BF16),
        pltpu.VMEM((ffn, features), BF16),
        pltpu.VMEM((4, rows, features), BF16),
        pltpu.VMEM((images, 4 * padded, 3 * cols), BF16),
        pltpu.VMEM((images, 8, 4 * padded), F32),
        pltpu.VMEM((images, 4 * padded, cols), BF16),
        pltpu.VMEM((4, images, padded, cols), BF16),
        pltpu.VMEM((rows, features), F32),
        pltpu.VMEM((rows, features), F32),
        pltpu.VMEM((rows, features), BF16),
        pltpu.VMEM((4, cap, rows), BF16),
        pltpu.VMEM((4, rows, cap), BF16),
        pltpu.VMEM((rows, LANES + 1), F32),
        pltpu.VMEM((rows, LANES), F32),
        pltpu.VMEM((3, cap, features), BF16),
        pltpu.VMEM((4, cap, features), BF16),
        pltpu.VMEM((4, cap, features), BF16),
        pltpu.VMEM((4, cap, features), BF16),
        pltpu.VMEM((4, cap, features), BF16),
        pltpu.VMEM((features, 4 * cap), BF16),
        pltpu.VMEM((4 * cap, ffn), BF16),
        pltpu.VMEM((4 * cap, ffn), BF16),
        pltpu.VMEM((8, features, out_rows), BF16),
        pltpu.VMEM((8, half_cols, out_rows), BF16),
        pltpu.VMEM((4, half_cols, out_rows), BF16),
        pltpu.VMEM((4, in_rows, half_ffn), BF16),
        pltpu.VMEM((3, half_cols, out_rows), BF16),
        pltpu.VMEM((3, in_rows, half_ffn), BF16),
        pltpu.VMEM((3, images, padded, cols), BF16),
        pltpu.VMEM((features, half_cols), BF16),
        pltpu.VMEM((4, in_rows, pack), BF16),
        pltpu.VMEM((3, in_rows, pack), BF16),
        pltpu.VMEM((3, rows, features), BF16),
        pltpu.VMEM((3, rows, features), BF16),
        pltpu.VMEM((STATS, features), F32),
        pltpu.VMEM((7, STATS, features), F32),
        pltpu.SemaphoreType.DMA((144,)),
        pltpu.SemaphoreType.DMA((144,)),
        pltpu.SemaphoreType.DMA((16,)),
        pltpu.SemaphoreType.REGULAR,
    ]
    return pl.pallas_call(
        lambda *refs: block_kernel(sizes, *refs),
        out_shape=(
            shape((piece, images, features), F32),
            shape((piece, images, features), F32),
            shape((STATS, features), F32),
            shape((4, in_rows, pack), BF16),
            shape((2, 2, in_rows, ffn), BF16),
            shape((2, 2, out_rows, features), BF16),
        ),
        in_specs=[vmem, vmem, pl.BlockSpec(memory_space=pltpu.SMEM), vmem, vmem, vmem, hbm, hbm, hbm],
        out_specs=(vmem, vmem, vmem, hbm, hbm, hbm),
        scratch_shapes=scratch,
        compiler_params=pltpu.CompilerParams(
            collective_id=0, has_side_effects=True, vmem_limit_bytes=64_500_000
        ),
        name="block",
    )(*operands)


def finish_kernel(
    sizes,
    counts,
    stats,
    attn_all,
    up_all,
    down_all,
    loss,
    gain_one,
    bias_one,
    grad_qkv,
    grad_out,
    gain_two,
    bias_two,
    router,
    up,
    down,
):
    images, piece, padded, cap, features, cols, ffn, in_rows, out_rows = sizes
    half_cols = features // 2
    for e in range(EXPERTS):
        up[:, e, :] = up_all[e // 2, e % 2].astype(F32)
        down[:, e, :] = down_all[e // 2, e % 2].astype(F32)
    grad_out[:, 0:half_cols] = attn_all[0, :, 0:half_cols].astype(F32) + attn_all[2, :, 0:half_cols].astype(F32)
    grad_out[:, half_cols:] = attn_all[1, :, 0:half_cols].astype(F32) + attn_all[3, :, 0:half_cols].astype(F32)
    for kind in range(3):
        at = half_cols + kind * cols
        grad_qkv[:, kind * features : (kind + 1) * features] = jnp.concatenate(
            [attn_all[j, :, at : at + cols].astype(F32) for j in range(4)], axis=1
        )

    @pl.when(pl.program_id(0) == 0)
    def _():
        f = lax.axis_index("fsdp")
        own = jnp.zeros((STATS, in_rows), F32)
        for g in range(8):
            own = jnp.where(f == g, stats[:, g * in_rows : (g + 1) * in_rows], own)
        router[...] = own[0:EXPERTS, :]
        gain_one[...] = own[GAIN_ONE : GAIN_ONE + 1, :]
        bias_one[...] = own[BIAS_ONE : BIAS_ONE + 1, :]
        gain_two[...] = own[GAIN_TWO : GAIN_TWO + 1, :]
        bias_two[...] = own[BIAS_TWO : BIAS_TWO + 1, :]
        used = counts[0]
        for g in range(1, counts.shape[0]):
            used = used + counts[g]
        tokens = (used * SEQ_LEN).astype(F32) * features
        total = jnp.sum(stats[LOSS_ROW : LOSS_ROW + 1, :], axis=1, keepdims=True)
        loss[...] = total / tokens


def run_finish(sizes, image_counts, stats, attn_all, up_all, down_all):
    images, piece, padded, cap, features, cols, ffn, in_rows, out_rows = sizes
    half_cols = features // 2
    pack = half_cols + 3 * cols
    steps = in_rows // 16
    tall = out_rows // steps
    shape = jax.ShapeDtypeStruct

    def whole(*dims):
        return pl.BlockSpec(dims, lambda i: (0,) * len(dims))

    row = whole(1, in_rows)
    return pl.pallas_call(
        lambda *refs: finish_kernel(sizes, *refs),
        grid=(steps,),
        out_shape=(
            shape((1, 1), F32),
            shape((1, in_rows), F32),
            shape((1, in_rows), F32),
            shape((in_rows, 3 * features), F32),
            shape((in_rows, features), F32),
            shape((1, in_rows), F32),
            shape((1, in_rows), F32),
            shape((EXPERTS, in_rows), F32),
            shape((in_rows, EXPERTS, ffn), F32),
            shape((out_rows, EXPERTS, features), F32),
        ),
        in_specs=[
            pl.BlockSpec(memory_space=pltpu.SMEM),
            whole(STATS, features),
            pl.BlockSpec((4, 16, pack), lambda i: (0, i, 0)),
            pl.BlockSpec((2, 2, 16, ffn), lambda i: (0, 0, i, 0)),
            pl.BlockSpec((2, 2, tall, features), lambda i: (0, 0, i, 0)),
        ],
        out_specs=(
            whole(1, 1),
            row,
            row,
            pl.BlockSpec((16, 3 * features), lambda i: (i, 0)),
            pl.BlockSpec((16, features), lambda i: (i, 0)),
            row,
            row,
            whole(EXPERTS, in_rows),
            pl.BlockSpec((16, EXPERTS, ffn), lambda i: (i, 0, 0)),
            pl.BlockSpec((tall, EXPERTS, features), lambda i: (i, 0, 0)),
        ),
        name="finish",
    )(image_counts, stats, attn_all, up_all, down_all)


def on_device(
    block_in,
    teacher,
    image_counts,
    expert_ids,
    pair_keep,
    norm1_gain,
    norm1_bias,
    qkv_weight,
    out_weight,
    norm2_gain,
    norm2_bias,
    router_weight,
    expert_in,
    expert_out,
):
    arguments = (
        block_in, teacher, image_counts, expert_ids, pair_keep, norm1_gain, norm1_bias, qkv_weight,
        out_weight, norm2_gain, norm2_bias, router_weight, expert_in, expert_out,
    )
    images, piece_len, features = block_in.shape
    pieces = lax.axis_size("seq")
    groups = lax.axis_size("fsdp")
    in_rows, out_rows, ffn = expert_in.shape[0], expert_out.shape[0], expert_in.shape[2]
    if pieces != EXPERTS or groups != 8 or in_rows % 16 or in_rows > 128 or out_rows % 128:
        return on_device_plain(*arguments)
    s = lax.axis_index("seq")
    f = lax.axis_index("fsdp")
    rows = images * piece_len
    cols = HEADS // pieces * HD
    padded = round_up(piece_len, 16)
    cap = round_up(rows * TOPK * 9 // (EXPERTS * 8) + 1, 16)
    half_cols = features // 2

    vec = jnp.concatenate(
        [router_weight.T, jnp.stack([norm1_gain, norm1_bias, norm2_gain, norm2_bias], axis=0)], axis=0
    )
    vec = jnp.pad(vec, ((0, STATS - 8), (0, 128 - in_rows)))
    attn_shard = jnp.concatenate(
        [
            lax.dynamic_slice_in_dim(out_weight, lax.rem(s, 2) * half_cols, half_cols, axis=1),
            lax.dynamic_index_in_dim(
                qkv_weight.reshape(in_rows, 3, pieces, cols), s, 2, keepdims=False
            ).reshape(in_rows, 3 * cols),
        ],
        axis=1,
    )
    up_shard = lax.dynamic_slice(
        expert_in.reshape(in_rows, 2, 2, ffn), (0, 0, s // 2, lax.rem(s, 2) * (ffn // 2)), (in_rows, 2, 1, ffn // 2)
    ).transpose(1, 2, 0, 3).reshape(2, in_rows, ffn // 2)
    down_shard = lax.dynamic_slice(
        expert_out.reshape(out_rows, 2, 2, features),
        (0, 0, s // 2, lax.rem(s, 2) * half_cols),
        (out_rows, 2, 1, half_cols),
    ).transpose(1, 2, 0, 3).reshape(2, out_rows, half_cols)
    sizes = (images, piece_len, padded, cap, features, cols, ffn, in_rows, out_rows)
    block_out, input_grad, *sums = run_block(
        sizes,
        (
            block_in.transpose(1, 0, 2),
            teacher.transpose(1, 0, 2),
            image_counts,
            expert_ids[0].transpose(0, 2, 1),
            pair_keep[0].transpose(0, 2, 1),
            vec,
            attn_shard,
            up_shard,
            down_shard,
        ),
    )
    loss, gain_one, bias_one, grad_qkv, grad_out, gain_two, bias_two, router, up, down = run_finish(
        sizes, image_counts, *sums
    )
    return (
        block_out.transpose(1, 0, 2),
        loss.reshape(()),
        input_grad.transpose(1, 0, 2),
        gain_one.reshape(in_rows),
        bias_one.reshape(in_rows),
        grad_qkv,
        grad_out,
        gain_two.reshape(in_rows),
        bias_two.reshape(in_rows),
        router.T,
        up,
        down,
    )


def solution(mesh):
    return jax.shard_map(
        on_device,
        mesh=mesh,
        in_specs=(
            P("fsdp", "seq", None),
            P("fsdp", "seq", None),
            P(),
            P("seq", "fsdp", None, None),
            P("seq", "fsdp", None, None),
            P("fsdp"),
            P("fsdp"),
            P("fsdp", None),
            P("fsdp", None),
            P("fsdp"),
            P("fsdp"),
            P("fsdp", None),
            P("fsdp", None, None),
            P("fsdp", None, None),
        ),
        out_specs=(
            P("fsdp", "seq", None),
            P(),
            P("fsdp", "seq", None),
            P("fsdp"),
            P("fsdp"),
            P("fsdp", None),
            P("fsdp", None),
            P("fsdp"),
            P("fsdp"),
            P("fsdp", None),
            P("fsdp", None, None),
            P("fsdp", None, None),
        ),
        check_vma=False,
    )
```

```python
import jax
import jax.numpy as jnp
from jax import lax
from jax.experimental import pallas as pl
from jax.experimental.pallas import tpu as pltpu
from jax.sharding import PartitionSpec as P

HEADS = 12
HD = 64
SEQ_LEN = 577
EXPERTS = 4
TOPK = 2
NORM_EPS = 1e-06
PRECISE = lax.Precision.HIGHEST
F32 = jnp.float32
BF16 = jnp.bfloat16


def layer_norm(values_in, gain_vec, bias_vec):
    centered = values_in - jnp.mean(values_in, axis=-1, keepdims=True)
    variance = jnp.mean(centered * centered, axis=-1, keepdims=True)
    root = lax.rsqrt(variance + NORM_EPS)
    unit = centered * root
    return unit * gain_vec + bias_vec, unit, root


def layer_norm_back(grad_out, unit, root, gain_vec):
    scaled = grad_out * gain_vec
    return root * (
        scaled
        - jnp.mean(scaled, axis=-1, keepdims=True)
        - unit * jnp.mean(scaled * unit, axis=-1, keepdims=True)
    )


def slot_holds(piece_index, piece_len, seq_len, pieces):
    lengths = seq_len // pieces + (piece_index < seq_len % pieces).astype(jnp.int32)
    return jnp.arange(piece_len, dtype=jnp.int32)[None, :] < lengths[:, None]


def dot32(left, right, dims):
    return lax.dot_general(left, right, (dims, ((), ())), preferred_element_type=F32)


def on_device_plain(
    block_in,
    teacher,
    image_counts,
    expert_ids,
    pair_keep,
    norm1_gain,
    norm1_bias,
    qkv_weight,
    out_weight,
    norm2_gain,
    norm2_bias,
    router_weight,
    expert_in,
    expert_out,
):
    images, piece_len, features = block_in.shape
    pieces = lax.axis_size("seq")
    groups = lax.axis_size("fsdp")
    seq_place = lax.axis_index("seq")
    group_place = lax.axis_index("fsdp")
    rows = images * piece_len
    slots = pieces * piece_len
    heads_here = HEADS // pieces
    cols = heads_here * HD
    hidden_size = expert_in.shape[2]
    capacity = rows * TOPK * 9 // (EXPERTS * 8) + 1
    inv_root = HD ** (-0.5)
    in_rows = expert_in.shape[0]
    out_rows = expert_out.shape[0]

    small = jnp.concatenate(
        [
            jnp.stack([norm1_gain, norm1_bias, norm2_gain, norm2_bias], axis=1),
            router_weight,
            out_weight,
            lax.dynamic_index_in_dim(
                qkv_weight.reshape(-1, 3, pieces, cols), seq_place, 2, keepdims=False
            ).reshape(-1, 3 * cols),
        ],
        axis=1,
    )
    small_full = lax.all_gather(small, "fsdp", axis=0, tiled=True)
    gain_one, bias_one, gain_two, bias_two = [small_full[:, i].astype(F32) for i in range(4)]
    router_full = small_full[:, 4 : 4 + EXPERTS]
    out_full = small_full[:, 4 + EXPERTS : 4 + EXPERTS + features]
    qkv_here = small_full[:, 4 + EXPERTS + features :]
    up_here = lax.all_gather(
        lax.dynamic_index_in_dim(expert_in, seq_place, 1, keepdims=False), "fsdp", axis=0, tiled=True
    )
    down_here = lax.all_gather(
        lax.dynamic_index_in_dim(expert_out, seq_place, 1, keepdims=False), "fsdp", axis=0, tiled=True
    )

    own_slots = slot_holds(jnp.reshape(seq_place, (1,)), piece_len, SEQ_LEN, pieces).reshape(piece_len)
    key_ok = slot_holds(jnp.arange(pieces, dtype=jnp.int32), piece_len, SEQ_LEN, pieces).reshape(slots)
    group_count = jnp.sum(
        jnp.where(jnp.arange(image_counts.shape[0], dtype=jnp.int32) == group_place, image_counts, 0)
    )
    token_ok = (
        (jnp.arange(images, dtype=jnp.int32) < group_count)[:, None] & own_slots[None, :]
    ).reshape(rows)

    flat_in = block_in.reshape(rows, features)
    normed_one, unit_one, root_one = layer_norm(flat_in, gain_one, bias_one)
    low_one = normed_one.astype(BF16)
    low_all = lax.all_gather(low_one.reshape(images, piece_len, features), "seq", axis=1, tiled=True)
    projected = dot32(low_all, qkv_here, ((2,), (0,))).astype(BF16)
    by_heads = projected.reshape(images, slots, 3, heads_here, HD).transpose(2, 0, 3, 1, 4)
    queries, key_rows, value_rows = by_heads[0], by_heads[1], by_heads[2]
    scores = jnp.einsum("ihqd,ihkd->ihqk", queries, key_rows, preferred_element_type=F32) * inv_root
    scores = jnp.where(key_ok[None, None, None, :], scores, -1e30)
    raised = jnp.exp(scores - jnp.max(scores, axis=-1, keepdims=True))
    attn = raised / jnp.sum(raised, axis=-1, keepdims=True)
    attn_low = attn.astype(BF16)
    context = jnp.einsum("ihqk,ihkd->iqhd", attn_low, value_rows, preferred_element_type=F32).astype(BF16)
    context_rows = lax.all_to_all(
        context.reshape(images, slots, 1, cols), "seq", split_axis=1, concat_axis=2, tiled=True
    ).reshape(rows, features)
    middle = flat_in + dot32(context_rows, out_full, ((1,), (0,)))
    normed_two, unit_two, root_two = layer_norm(middle, gain_two, bias_two)
    low_two = normed_two.astype(BF16)
    probs = jax.nn.softmax(dot32(low_two, router_full, ((1,), (0,))), axis=-1)

    expert_rows = expert_ids.reshape(rows, TOPK)
    usable = (pair_keep.reshape(rows, TOPK) == 1) & token_ok[:, None]
    hit = jnp.any(
        (expert_rows[:, :, None] == jnp.arange(EXPERTS, dtype=jnp.int32)) & usable[:, :, None], axis=1
    )
    earlier = (jnp.arange(rows)[:, None] > jnp.arange(rows)[None, :]).astype(BF16)
    place = dot32(earlier, hit.astype(BF16), ((1,), (0,))).astype(jnp.int32)
    place = jnp.where(hit, place, -1)
    select = (place.T[:, None, :] == jnp.arange(capacity, dtype=jnp.int32)[None, :, None]).astype(BF16)
    weight = jnp.where(hit, probs, 0.0)

    dispatched = dot32(select, low_two, ((2,), (0,))).astype(BF16)
    arrived = lax.all_to_all(dispatched, "seq", split_axis=0, concat_axis=0, tiled=True)
    arrived = arrived.reshape(pieces * capacity, features)
    hidden = dot32(arrived, up_here, ((1,), (0,)))
    activated, gelu_back = jax.vjp(lambda u: jax.nn.gelu(u, approximate=False), hidden)
    low_act = activated.astype(BF16)
    returned = dot32(low_act, down_here, ((1,), (0,))).astype(BF16)
    returned = lax.all_to_all(
        returned.reshape(pieces, capacity, features), "seq", split_axis=0, concat_axis=0, tiled=True
    )
    picked = jnp.einsum("est,esd->etd", select, returned, preferred_element_type=F32)
    block_out = middle + jnp.sum(weight.T[:, :, None] * picked, axis=0)
    misfit = (block_out - teacher.reshape(rows, features)) * token_ok.astype(F32)[:, None]
    loss_here = jnp.sum(misfit * misfit)

    pair_grad = (weight.T[:, :, None] * misfit[None]).astype(BF16)
    returned_grad = jnp.einsum("est,etd->esd", select, pair_grad, preferred_element_type=F32).astype(BF16)
    prob_grad = jnp.where(hit, jnp.sum(picked * misfit[None], axis=2).T, 0.0)
    grad_arrived = lax.all_to_all(returned_grad, "seq", split_axis=0, concat_axis=0, tiled=True).reshape(
        pieces * capacity, features
    )
    hidden_grad = gelu_back(dot32(grad_arrived, down_here, ((1,), (1,))))[0].astype(BF16)
    grad_down = dot32(low_act, grad_arrived, ((0,), (0,))).astype(BF16)
    grad_up = dot32(arrived, hidden_grad, ((0,), (0,))).astype(BF16)
    dispatch_grad = dot32(hidden_grad, up_here, ((1,), (1,))).astype(BF16)
    dispatch_grad = lax.all_to_all(
        dispatch_grad.reshape(pieces, capacity, features), "seq", split_axis=0, concat_axis=0, tiled=True
    )
    owned_down = lax.psum_scatter(grad_down, "fsdp", scatter_dimension=0, tiled=True)
    owned_up = lax.psum_scatter(grad_up, "fsdp", scatter_dimension=0, tiled=True)

    logit_grad = probs * (prob_grad - jnp.sum(probs * prob_grad, axis=1, keepdims=True))
    grad_router = lax.dot_general(
        low_two.astype(F32), logit_grad, (((0,), (0,)), ((), ())), precision=PRECISE
    )
    normed_two_grad = jnp.einsum("est,esd->td", select, dispatch_grad, preferred_element_type=F32)
    normed_two_grad = normed_two_grad + lax.dot_general(
        logit_grad, router_full.astype(F32), (((1,), (1,)), ((), ())), precision=PRECISE
    )
    grad_gain_two = jnp.sum(normed_two_grad * unit_two, axis=0)
    grad_bias_two = jnp.sum(normed_two_grad, axis=0)
    middle_grad = misfit + layer_norm_back(normed_two_grad, unit_two, root_two, gain_two)
    attended_grad = middle_grad.astype(BF16)
    grad_out_w = dot32(context_rows, attended_grad, ((0,), (0,))).astype(BF16)
    context_grad = dot32(attended_grad, out_full, ((1,), (1,))).astype(BF16)
    heads_grad = lax.all_to_all(
        context_grad.reshape(images, piece_len, pieces, cols), "seq", split_axis=2, concat_axis=1, tiled=True
    ).reshape(images, slots, heads_here, HD)
    value_grad = jnp.einsum("ihqk,iqhd->ikhd", attn_low, heads_grad, preferred_element_type=F32)
    share_grad = jnp.einsum("iqhd,ihkd->ihqk", heads_grad, value_rows, preferred_element_type=F32)
    score_grad = (attn * (share_grad - jnp.sum(attn * share_grad, axis=-1, keepdims=True))).astype(BF16)
    query_grad = jnp.einsum("ihqk,ihkd->iqhd", score_grad, key_rows, preferred_element_type=F32) * inv_root
    key_grad = jnp.einsum("ihqk,ihqd->ikhd", score_grad, queries, preferred_element_type=F32) * inv_root
    heads_back = jnp.stack([query_grad, key_grad, value_grad], axis=2).astype(BF16)
    heads_back = heads_back.reshape(images * slots, 3 * cols)
    grad_qkv = dot32(low_all.reshape(images * slots, features), heads_back, ((0,), (0,))).astype(BF16)
    normed_one_part = dot32(heads_back, qkv_here, ((1,), (1,))).astype(BF16)
    normed_one_grad = lax.psum_scatter(
        normed_one_part.reshape(images, slots, features), "seq", scatter_dimension=1, tiled=True
    ).astype(F32).reshape(rows, features)
    grad_gain_one = jnp.sum(normed_one_grad * unit_one, axis=0)
    grad_bias_one = jnp.sum(normed_one_grad, axis=0)
    input_grad = middle_grad + layer_norm_back(normed_one_grad, unit_one, root_one, gain_one)

    out_share = lax.psum_scatter(grad_out_w, "seq", scatter_dimension=1, tiled=True)
    attn_owned = lax.psum_scatter(
        jnp.concatenate([grad_qkv, out_share], axis=1), "fsdp", scatter_dimension=0, tiled=True
    )
    loss_row = jnp.zeros((features,), F32).at[0].set(loss_here)
    vectors = jnp.concatenate(
        [jnp.stack([grad_gain_one, grad_bias_one, grad_gain_two, grad_bias_two, loss_row]), grad_router.T], axis=0
    )
    vectors = lax.psum(vectors, ("fsdp", "seq"))
    mean_loss = vectors[4, 0] / (
        (jnp.sum(image_counts, dtype=jnp.int32) * SEQ_LEN).astype(F32) * features
    )
    owned_vectors = lax.dynamic_slice_in_dim(vectors, group_place * in_rows, in_rows, axis=1)
    attn_whole = lax.all_gather(attn_owned, "seq", axis=0)
    grad_qkv_w = (
        attn_whole[:, :, : 3 * cols].reshape(pieces, in_rows, 3, cols).transpose(1, 2, 0, 3)
        .reshape(in_rows, 3 * features).astype(F32)
    )
    grad_out_whole = attn_whole[:, :, 3 * cols :].transpose(1, 0, 2).reshape(in_rows, features).astype(F32)
    grad_up_w = lax.all_gather(owned_up, "seq", axis=0).transpose(1, 0, 2).astype(F32)
    grad_down_w = lax.all_gather(owned_down, "seq", axis=0).transpose(1, 0, 2).astype(F32)
    return (
        block_out.reshape(images, piece_len, features),
        mean_loss,
        input_grad.reshape(images, piece_len, features),
        owned_vectors[0],
        owned_vectors[1],
        grad_qkv_w,
        grad_out_whole,
        owned_vectors[2],
        owned_vectors[3],
        owned_vectors[5:].T,
        grad_up_w,
        grad_down_w,
    )


MESH = pl.DeviceIdType.MESH
LANES = 16
STATS = 16
GAIN_ONE, BIAS_ONE, GAIN_TWO, BIAS_TWO = 4, 5, 6, 7
LOSS_ROW = 8


def round_up(value, step):
    return (value + step - 1) // step * step


def flipped(place, bits):
    low, high = lax.rem(place, 2), place // 2
    if bits % 2:
        low = 1 - low
    if bits // 2:
        high = 1 - high
    return high * 2 + low


def unit_rows(values_in):
    centered = values_in - jnp.mean(values_in, axis=1, keepdims=True)
    variance = jnp.mean(centered * centered, axis=1, keepdims=True)
    root = lax.rsqrt(variance + NORM_EPS)
    return centered * root, root


def norm_back(grad_out, unit, root, gain_row):
    scaled = grad_out * gain_row
    return root * (
        scaled
        - jnp.mean(scaled, axis=1, keepdims=True)
        - unit * jnp.mean(scaled * unit, axis=1, keepdims=True)
    )


def hi_lo(values_in):
    high = values_in.astype(BF16)
    return high, (values_in - high.astype(F32)).astype(BF16)


def block_kernel(
    sizes,
    x_in,
    teacher_in,
    counts,
    ids_in,
    keep_in,
    vec_in,
    qkv_in,
    out_in,
    up_in,
    down_in,
    block_out,
    input_grad,
    stats_out,
    qkv_all,
    out_all,
    up_all,
    down_all,
    vec_all,
    vecs,
    qkv_w,
    out_w,
    up_w,
    down_w,
    low_all,
    qkv_s,
    lse_s,
    ctx_s,
    ctx_rows,
    middle,
    misfit,
    low_two,
    select,
    select_t,
    hits,
    weights,
    send_s,
    arrived,
    ret_r,
    back_r,
    dret_r,
    turned,
    act,
    slope,
    grad_down,
    core_down,
    yrecv_down,
    yrecv_up,
    zrecv_down,
    zrecv_up,
    dctx_s,
    half_recv,
    yrecv_qkv,
    zrecv_qkv,
    yrecv_out,
    zrecv_out,
    part_s,
    part_r,
    stats,
    stats_r,
    send_sem,
    recv_sem,
    local_sem,
    free_sem,
):
    images, piece, padded, cap, features, cols, ffn, in_rows, out_rows = sizes
    rows = images * padded
    slots = 4 * padded
    half_cols, half_ffn = features // 2, ffn // 2
    wide = ffn // 6
    f = lax.axis_index("fsdp")
    s = lax.axis_index("seq")
    z, y = f // 2, lax.rem(f, 2)
    inv_root = HD ** (-0.5)
    same = [flipped(z, k) * 2 + y for k in range(4)]
    other = [flipped(z, k) * 2 + (1 - y) for k in range(4)]
    near = [flipped(s, r) for r in range(4)]
    zb, xb, core = lax.rem(z, 2), s // 2, lax.rem(s, 2)
    named_by = [flipped(zb * 2 + xb, r) for r in range(4)]
    cluster = [(f, s), (f, near[2]), (same[1], s), (same[1], near[2])]
    counter = [0, 0]
    pending = []

    def send(src, dst, group, seq):
        i = counter[0]
        counter[0] += 1
        copy = pltpu.make_async_remote_copy(
            src_ref=src,
            dst_ref=dst,
            send_sem=send_sem.at[i],
            recv_sem=recv_sem.at[i],
            device_id=(group, seq),
            device_id_type=MESH,
        )
        copy.start()
        pending.append(copy)
        return copy

    def done_sending(copy):
        pending[:] = [other_copy for other_copy in pending if other_copy is not copy]
        copy.wait_send()

    def local(src, dst):
        i = counter[1]
        counter[1] += 1
        copy = pltpu.make_async_copy(src, dst, local_sem.at[i])
        copy.start()
        return copy

    barrier = pltpu.get_barrier_semaphore()
    for g in same[1:] + other:
        pl.semaphore_signal(barrier, inc=1, device_id=(g, s), device_id_type=MESH)
    for q in near[1:]:
        pl.semaphore_signal(barrier, inc=1, device_id=(f, q), device_id_type=MESH)
    pl.semaphore_signal(barrier, inc=1, device_id=cluster[3], device_id_type=MESH)
    pl.semaphore_wait(barrier, 11)

    vec_copies = [send(vec_in, vec_all.at[f], g, s) for g in same[1:] + other]
    vec_all[f] = vec_in[...]

    def rows_at(n, g):
        return pl.ds(pl.multiple_of(g * n, n), n)

    def lanes_at(n, half):
        return pl.ds(pl.multiple_of(half * n, n), n)

    def qkv_spot(g):
        return qkv_w.at[rows_at(in_rows, g), :]

    def out_spot(g):
        return out_w.at[rows_at(in_rows, g), lanes_at(half_cols, core)]

    def up_spot(g):
        return up_w.at[rows_at(in_rows, g), lanes_at(half_ffn, core)]

    def down_spot(g):
        return down_w.at[rows_at(out_rows, g), lanes_at(half_cols, core)]

    class Flow:
        def __init__(self, own, odd, spot, shared):
            self.own, self.spot, self.shared = own, spot, shared
            self.z = [None] + [send(odd if k % 2 else own, spot(f), same[k], s) for k in (1, 2, 3)]
            self.y, self.core, self.local = [], [], None

        def start(self):
            self.y.append(send(self.own, self.spot(f), other[0], s))
            if self.shared:
                self.core.append(send(self.own, self.spot(f), f, near[1]))

        def keep(self):
            self.local = local(self.own, self.spot(f))

        def forward(self, k):
            self.z[k].wait_recv()
            ref = self.spot(same[k])
            self.y.append(send(ref, ref, other[0], s))
            if self.shared:
                self.core.append(send(ref, ref, f, near[1]))

        def end(self):
            for k in range(4):
                self.y[k].wait_recv()
                if self.shared:
                    ref = self.spot(other[k])
                    self.core.append(send(ref, ref, f, near[1]))
            for copy in self.core:
                copy.wait_recv()
            if self.local is not None:
                self.local.wait()

        def sent(self):
            for copy in self.z[1:] + self.y + self.core:
                done_sending(copy)

    for kind in range(3):
        part = jnp.zeros((in_rows, cols), BF16)
        for j in range(4):
            at = kind * features + j * cols
            part = jnp.where(s == j, qkv_in[:, at : at + cols], part)
        qkv_w[rows_at(in_rows, f), kind * cols : (kind + 1) * cols] = part
    out_w[rows_at(in_rows, f), lanes_at(half_cols, core)] = out_in[:, lanes_at(half_cols, core)]
    qkv_flow = Flow(qkv_spot(f), qkv_spot(f), qkv_spot, False)
    qkv_flow.start()
    out_flow = Flow(out_spot(f), out_spot(f), out_spot, True)
    up_flow = Flow(up_in.at[zb], up_in.at[1 - zb], up_spot, True)
    down_flow = Flow(down_in.at[zb], down_in.at[1 - zb], down_spot, True)
    up_flow.keep()
    down_flow.keep()

    def near_of(shape, axis):
        at = lax.broadcasted_iota(jnp.int32, shape, axis)
        named = jnp.full(shape, -1, jnp.int32)
        for r in range(4):
            named = jnp.where(at == r, named_by[r], named)
        return named

    own_len = SEQ_LEN // 4 + jnp.where(s < SEQ_LEN % 4, 1, 0)
    at_piece = lax.broadcasted_iota(jnp.int32, (1, piece), 1)
    route_rows = jnp.zeros((rows, LANES), F32)
    route_cols = jnp.zeros((LANES, rows), F32)
    for i in range(images):
        ok = jnp.where((at_piece < own_len) & (i < counts[f]), 1.0, 0.0)
        facts = jnp.concatenate(
            [
                ids_in[i].astype(F32),
                jnp.where(keep_in[i] == 1, 1.0, 0.0) * ok,
                ok,
                jnp.zeros((LANES - 5, piece), F32),
            ],
            axis=0,
        ).astype(BF16)
        spread = jnp.where(
            lax.broadcasted_iota(jnp.int32, (piece, rows), 0) + i * padded
            == lax.broadcasted_iota(jnp.int32, (piece, rows), 1),
            1.0,
            0.0,
        ).astype(BF16)
        route_cols = route_cols + dot32(facts, spread, ((1,), (0,)))
        route_rows = route_rows + dot32(spread, facts, ((0,), (1,)))
    token_ok = route_rows[:, 4:5]
    hits[:, LANES:] = token_ok
    route_rows = route_rows.astype(jnp.int32)
    route_cols = route_cols.astype(jnp.int32)
    named = near_of((rows, LANES), 1)
    hit = ((route_rows[:, 0:1] == named) & (route_rows[:, 2:3] == 1)) | (
        (route_rows[:, 1:2] == named) & (route_rows[:, 3:4] == 1)
    )
    hit_f = jnp.where(hit, 1.0, 0.0)
    before = (
        lax.broadcasted_iota(jnp.int32, (rows, rows), 0) > lax.broadcasted_iota(jnp.int32, (rows, rows), 1)
    )
    before = jnp.where(before, 1.0, 0.0).astype(BF16)
    place = dot32(before, hit_f.astype(BF16), ((1,), (0,)))
    place = jnp.where(hit, place, -1.0)
    hits[:, 0:LANES] = hit_f
    named_t = near_of((LANES, rows), 0)
    hit_t = ((route_cols[0:1, :] == named_t) & (route_cols[2:3, :] == 1)) | (
        (route_cols[1:2, :] == named_t) & (route_cols[3:4, :] == 1)
    )
    hit_tf = jnp.where(hit_t, 1.0, 0.0).astype(BF16)
    place_t = dot32(hit_tf, before, ((1,), (1,)))
    place_t = jnp.where(hit_t, place_t, -1.0)
    slot_down = lax.broadcasted_iota(jnp.int32, (cap, rows), 0).astype(F32)
    slot_along = lax.broadcasted_iota(jnp.int32, (rows, cap), 1).astype(F32)
    for r in range(4):
        select[r] = jnp.where(place_t[r : r + 1, :] == slot_down, 1.0, 0.0).astype(BF16)
        select_t[r] = jnp.where(place[:, r : r + 1] == slot_along, 1.0, 0.0).astype(BF16)

    for copy in vec_copies:
        copy.wait_recv()
    at_row = lax.broadcasted_iota(jnp.int32, (128, features), 0)
    at_col = lax.broadcasted_iota(jnp.int32, (128, features), 1)
    total = jnp.zeros((STATS, features), F32)
    for g in range(8):
        spread = jnp.where((at_col - g * in_rows == at_row) & (at_row < in_rows), 1.0, 0.0).astype(BF16)
        total = total + dot32(vec_all[g], spread, ((1,), (0,)))
    vecs[...] = total

    low_all[s] = jnp.zeros((rows, features), BF16)
    low_x, low_c, low_d = [], [], []

    def image_of(j, i):
        return low_all.at[j, pl.ds(i * padded, padded), :]

    for i in range(images):
        unit, _ = unit_rows(x_in[:, i, :])
        low_all[s, i * padded : i * padded + piece, :] = (
            unit * vecs[GAIN_ONE : GAIN_ONE + 1, :] + vecs[BIAS_ONE : BIAS_ONE + 1, :]
        ).astype(BF16)
        low_x.append(send(image_of(s, i), image_of(s, i), f, near[2]))
        low_c.append(send(image_of(s, i), image_of(s, i), f, near[1]))

    for k in (1, 2, 3):
        qkv_flow.forward(k)
    for flow in (out_flow, up_flow, down_flow):
        flow.start()
    for i in range(images):
        low_x[i].wait_recv()
        low_d.append(send(image_of(near[2], i), image_of(near[2], i), f, near[1]))
    qkv_flow.end()

    def project(j):
        found = dot32(low_all[j], qkv_w[...], ((1,), (0,))).astype(BF16)
        for i in range(images):
            qkv_s[i, pl.ds(pl.multiple_of(j * padded, padded), padded), :] = found[
                i * padded : (i + 1) * padded, :
            ]

    project(s)
    for copy in low_c:
        copy.wait_recv()
    project(near[1])
    project(near[2])
    for k in (1, 2, 3):
        out_flow.forward(k)
    for copy in low_d:
        copy.wait_recv()
    project(near[3])

    key_at = lax.broadcasted_iota(jnp.int32, (slots, 1), 0)
    key_piece = jnp.zeros((slots, 1), jnp.int32)
    for j in range(1, 4):
        key_piece = key_piece + jnp.where(key_at >= j * padded, 1, 0)
    key_len = SEQ_LEN // 4 + jnp.where(key_piece < SEQ_LEN % 4, 1, 0)
    key_ok = key_at - key_piece * padded < key_len

    def heads_of(ref, i, kind, h):
        return ref[i, :, kind * cols + h * HD : kind * cols + (h + 1) * HD]

    def scores_of(i, h):
        found = dot32(heads_of(qkv_s, i, 1, h), heads_of(qkv_s, i, 0, h), ((1,), (1,))) * inv_root
        return jnp.where(key_ok, found, -1e30)

    def piece_rows(ref, j):
        return ref.at[:, pl.ds(pl.multiple_of(j * padded, padded), padded), :]

    @pl.loop(0, images)
    def _(i):
        found = []
        for h in range(cols // HD):
            scores = scores_of(i, h)
            highest = jnp.max(scores, axis=0, keepdims=True)
            raised = jnp.exp(scores - highest)
            total = jnp.sum(raised, axis=0, keepdims=True)
            shares = (raised * (1.0 / total)).astype(BF16)
            lse_s[i, h : h + 1, :] = highest + jnp.log(total)
            found.append(dot32(heads_of(qkv_s, i, 2, h), shares, ((0,), (0,))))
        ctx_s[i] = jnp.concatenate(found, axis=0).T.astype(BF16)

    ctx_copies = [send(piece_rows(ctx_s, near[r]), ctx_rows.at[s], f, near[r]) for r in (2, 3, 1)]
    ctx_rows[s] = ctx_s[:, pl.ds(pl.multiple_of(s * padded, padded), padded), :]
    out_flow.end()
    up_flow.forward(1)
    for copy in ctx_copies:
        copy.wait_recv()
        done_sending(copy)

    attended = jnp.zeros((rows, features), F32)
    for j in range(4):
        attended = attended + dot32(
            ctx_rows[j].reshape(rows, cols), out_w[j * cols : (j + 1) * cols, :], ((1,), (0,))
        )
    middle[...] = attended
    for i in range(images):
        at = slice(i * padded, i * padded + piece)
        middle[at, :] = middle[at, :] + x_in[:, i, :]
    unit, _ = unit_rows(middle[...])
    low_two[...] = (unit * vecs[GAIN_TWO : GAIN_TWO + 1, :] + vecs[BIAS_TWO : BIAS_TWO + 1, :]).astype(BF16)
    router = vecs[...].astype(BF16)

    def probs_of():
        logits = dot32(low_two[...], router, ((1,), (1,)))
        real = lax.broadcasted_iota(jnp.int32, (rows, LANES), 1) < EXPERTS
        logits = jnp.where(real, logits, -1e30)
        raised = jnp.exp(logits - jnp.max(logits, axis=1, keepdims=True))
        return raised / jnp.sum(raised, axis=1, keepdims=True)

    disp_copies = []
    for r in (1, 2, 3, 0):
        found = dot32(select[r], low_two[...], ((1,), (0,))).astype(BF16)
        if r:
            send_s[r - 1] = found
            disp_copies.append(send(send_s.at[r - 1], arrived.at[r], *cluster[r]))
        else:
            arrived[0] = found
    probs = probs_of()
    lane = lax.broadcasted_iota(jnp.int32, (rows, LANES), 1)
    chosen = jnp.zeros((rows, LANES), F32)
    for r in range(4):
        value = jnp.sum(jnp.where(lane == named_by[r], probs, 0.0), axis=1, keepdims=True)
        chosen = jnp.where(lane == r, value, chosen)
    weights[...] = chosen * hits[:, 0:LANES]

    up_flow.forward(2)
    up_flow.forward(3)
    down_flow.forward(1)
    up_flow.end()

    def expert_up(half):
        given = arrived[2 * half : 2 * half + 2].reshape(2 * cap, features)

        @pl.loop(0, 6)
        def _(t):
            tile = pl.ds(pl.multiple_of(t * wide, wide), wide)
            hidden = dot32(given, up_w[:, tile], ((1,), (0,)))
            phi = 0.5 * (1.0 + lax.erf(hidden * (2.0**-0.5)))
            at = slice(2 * half * cap, 2 * (half + 1) * cap)
            act[at, tile] = (hidden * phi).astype(BF16)
            slope[at, tile] = (phi + hidden * jnp.exp(-0.5 * hidden * hidden) * 0.3989422804014327).astype(BF16)

    disp_copies[0].wait_recv()
    expert_up(0)
    down_flow.forward(2)
    disp_copies[1].wait_recv()
    disp_copies[2].wait_recv()
    expert_up(1)
    down_flow.forward(3)
    for copy in disp_copies:
        done_sending(copy)
    down_flow.end()

    def to_rows(left, right, dims, half, dst):
        at = slice(2 * half * cap, 2 * (half + 1) * cap)
        found = dot32(left[at, :], right[...], dims).astype(BF16)
        out = []
        for r in (2 * half + 1, 2 * half):
            part = found[(r - 2 * half) * cap : (r - 2 * half + 1) * cap, :]
            if r:
                send_s[r - 1] = part
                out.append(send(send_s.at[r - 1], dst.at[r], *cluster[r]))
            else:
                dst[0] = part
        return out

    ret_copies = to_rows(act, down_w, ((1,), (0,)), 1, ret_r)
    ret_copies += to_rows(act, down_w, ((1,), (0,)), 0, ret_r)
    for i in range(images):
        at = slice(i * padded, i * padded + piece)
        misfit[at, :] = teacher_in[:, i, :]
        misfit[i * padded + piece : (i + 1) * padded, :] = jnp.zeros((padded - piece, features), F32)

    found = middle[...]
    for r in (0, 1, 2, 3):
        if r:
            ret_copies[{3: 0, 2: 1, 1: 2}[r]].wait_recv()
        found = found + weights[:, r : r + 1] * dot32(select_t[r], ret_r[r], ((1,), (0,)))
    for i in range(images):
        block_out[:, i, :] = found[i * padded : i * padded + piece, :]
    wrong = (found - misfit[...]) * hits[:, LANES:]
    misfit[...] = wrong
    for copy in ret_copies:
        done_sending(copy)
    dret_copies = []
    for r in (3, 2, 1, 0):
        pair = (weights[:, r : r + 1] * misfit[...]).astype(BF16)
        part = dot32(select[r], pair, ((1,), (0,))).astype(BF16)
        if r:
            send_s[r - 1] = part
            dret_copies.append(send(send_s.at[r - 1], dret_r.at[r], *cluster[r]))
        else:
            dret_r[0] = part
    stats[...] = jnp.zeros_like(stats)
    stats[LOSS_ROW : LOSS_ROW + 1, :] = jnp.sum(wrong * wrong, axis=0, keepdims=True)
    probs = probs_of()
    prob_grad = jnp.zeros((rows, LANES), F32)
    for r in range(4):
        picked = dot32(select_t[r], ret_r[r], ((1,), (0,)))
        value = jnp.sum(picked * misfit[...], axis=1, keepdims=True) * hits[:, r : r + 1]
        prob_grad = jnp.where(lane == named_by[r], value, prob_grad)
    logit_grad = probs * (prob_grad - jnp.sum(probs * prob_grad, axis=1, keepdims=True))
    high, low = hi_lo(logit_grad)
    router_grad = dot32(high, low_two[...], ((0,), (0,))) + dot32(low, low_two[...], ((0,), (0,)))
    stats[0:EXPERTS, :] = router_grad[0:EXPERTS, :]

    def down_back(r):
        at = slice(r * cap, (r + 1) * cap)

        @pl.loop(0, 6)
        def _(t, r=r, at=at):
            tile = pl.ds(pl.multiple_of(t * wide, wide), wide)
            found = dot32(dret_r[r], down_w[tile, :], ((1,), (1,)))
            slope[at, tile] = (found * slope[at, tile].astype(F32)).astype(BF16)

    down_back(0)
    for r in (1, 2):
        dret_copies[3 - r].wait_recv()
        down_back(r)
    dret_copies[0].wait_recv()
    turned[...] = dret_r[...].reshape(4 * cap, features).T

    def down_grads(half):
        rows_here = lanes_at(half_cols, half)

        @pl.loop(0, 8)
        def _(g):
            grad_down[g, rows_here, :] = dot32(
                turned[rows_here, :], act[:, rows_at(out_rows, g)], ((1,), (0,))
            ).astype(BF16)

    down_grads(1 - core)

    def half_at(ref, half, n):
        return ref.at[:, pl.ds(pl.multiple_of(half * n, n), n), :]

    core_copy = send(half_at(grad_down, 1 - core, half_cols), core_down, f, near[1])

    def down_block(g):
        return grad_down.at[g, pl.ds(pl.multiple_of(core * half_cols, half_cols), half_cols), :]

    def down_core(g):
        return core_down[g].astype(F32)

    def up_core(g):
        at = pl.ds(pl.multiple_of(lax.rem(g, 4) * in_rows, in_rows), in_rows)
        return act[at, pl.ds(pl.multiple_of(g // 4 * half_ffn, half_ffn), half_ffn)].astype(F32)

    def sum_start(block, extra, yrecv):
        flow = {}
        for k in (3, 2, 1, 0):
            ref = block(other[k])
            if extra is not None:
                ref[...] = (ref[...].astype(F32) + extra(other[k])).astype(BF16)
            flow[k] = send(ref, yrecv.at[k], other[0], s)
        return flow

    def sum_pass(flow, block, extra, yrecv, zrecv, k):
        flow[k].wait_recv()
        ref = block(same[k])
        total = ref[...].astype(F32) + yrecv[k].astype(F32)
        if extra is not None:
            total = total + extra(same[k])
        ref[...] = total.astype(BF16)
        if k:
            flow["z%d" % k] = send(ref, zrecv.at[k - 1], same[k], s)

    def sum_end(flow, block, zrecv, dst):
        ref = block(f)
        for k in (1, 2, 3):
            flow["z%d" % k].wait_recv()
        total = ref[...].astype(F32)
        for k in (1, 2, 3):
            total = total + zrecv[k - 1].astype(F32)
        ref[...] = total.astype(BF16)
        return share(ref, dst.at[s], dst.at[near[2]])

    def share(ref, own, of_x):
        return send(ref, own, f, near[2]), send(ref, own, f, near[1]), local(ref, own), of_x

    def expert_sum_end(flow, block, yrecv, zrecv, own, of_x, turn):
        for k in (1, 2, 3):
            flow["z%d" % k].wait_recv()
        totals = (
            block(f)[...].astype(F32) + zrecv[1].astype(F32),
            zrecv[0].astype(F32) + zrecv[2].astype(F32),
        )
        for parity, total in zip((zb, 1 - zb), totals):
            yrecv[parity] = (total.T if turn else total).astype(BF16)
        return share(yrecv.at[pl.ds(0, 2)], own, of_x)

    def down_all_at(x):
        return down_all.at[:, x, :, pl.ds(pl.multiple_of(core * half_cols, half_cols), half_cols)]

    def up_all_at(x):
        return up_all.at[:, x, :, pl.ds(pl.multiple_of(core * half_ffn, half_ffn), half_ffn)]

    def share_pass(flow):
        flow[0].wait_recv()
        return send(flow[3], flow[3], f, near[1])

    for copy in dret_copies:
        done_sending(copy)
    down_back(3)
    down_grads(core)
    pl.semaphore_signal(free_sem, inc=1, device_id=(f, near[1]), device_id_type=MESH)
    core_copy.wait_recv()
    down_sum = sum_start(down_block, down_core, yrecv_down)
    back_copies = to_rows(slope, up_w, ((1,), (1,)), 1, back_r)
    back_copies += to_rows(slope, up_w, ((1,), (1,)), 0, back_r)
    up_flow.sent()
    turned[...] = arrived[...].reshape(4 * cap, features).T

    def up_grads(half):
        @pl.loop(0, 3)
        def _(t):
            tile = pl.ds(pl.multiple_of(half * half_ffn + t * wide, wide), wide)
            up_w[:, tile] = dot32(turned[...], slope[:, tile], ((1,), (0,))).astype(BF16)

    up_grads(1 - core)
    pl.semaphore_wait(free_sem, 1)
    up_copies = [
        send(
            up_w.at[pl.ds(h * 4 * in_rows, 4 * in_rows), lanes_at(half_ffn, 1 - core)],
            act.at[pl.ds(0, 4 * in_rows), pl.ds(h * half_ffn, half_ffn)],
            f,
            near[1],
        )
        for h in (0, 1)
    ]
    up_grads(core)
    sum_pass(down_sum, down_block, down_core, yrecv_down, zrecv_down, 3)
    for copy in up_copies:
        copy.wait_recv()
    up_sum = sum_start(up_spot, up_core, yrecv_up)
    for copy in up_copies:
        done_sending(copy)

    normed_grad = dot32(high, router, ((1,), (0,))) + dot32(low, router, ((1,), (0,)))
    for r in (0, 1, 2, 3):
        if r:
            back_copies[{3: 0, 2: 1, 1: 2}[r]].wait_recv()
        normed_grad = normed_grad + dot32(select_t[r], back_r[r], ((1,), (0,)))
    unit, root = unit_rows(middle[...])
    stats[GAIN_TWO : GAIN_TWO + 1, :] = jnp.sum(normed_grad * unit, axis=0, keepdims=True)
    stats[BIAS_TWO : BIAS_TWO + 1, :] = jnp.sum(normed_grad, axis=0, keepdims=True)
    middle_grad = misfit[...] + norm_back(normed_grad, unit, root, vecs[GAIN_TWO : GAIN_TWO + 1, :])
    middle[...] = middle_grad
    low_two[...] = middle_grad.astype(BF16)

    dctx_copies = []
    for r in (2, 3, 1, 0):
        block = out_w[pl.ds(pl.multiple_of(near[r] * cols, cols), cols), :]
        found = dot32(low_two[...], block, ((1,), (1,))).astype(BF16).reshape(images, padded, cols)
        if r:
            dctx_s[r - 1] = found
            dctx_copies.append(send(dctx_s.at[r - 1], piece_rows(ctx_s, s), f, near[r]))
        else:
            ctx_s[:, pl.ds(pl.multiple_of(s * padded, padded), padded), :] = found
    out_flow.sent()
    sum_pass(down_sum, down_block, down_core, yrecv_down, zrecv_down, 2)
    for j in range(4):
        out_w[j * cols : (j + 1) * cols, :] = dot32(
            ctx_rows[j].reshape(rows, cols), low_two[...], ((0,), (0,))
        ).astype(BF16)
    half_copy = send(out_w.at[:, lanes_at(half_cols, 1 - core)], half_recv, f, near[1])
    sum_pass(down_sum, down_block, down_core, yrecv_down, zrecv_down, 1)
    for copy in dctx_copies:
        copy.wait_recv()

    def heads_back(i):
        found = [[], [], []]
        for h in range(cols // HD):
            shares = jnp.exp(scores_of(i, h) - lse_s[i, h : h + 1, :])
            given = ctx_s[i, :, h * HD : (h + 1) * HD]
            found[2].append(dot32(shares.astype(BF16), given, ((1,), (0,))))
            share_grad = dot32(heads_of(qkv_s, i, 2, h), given, ((1,), (1,)))
            across = jnp.sum(shares * share_grad, axis=0, keepdims=True)
            score_grad = (shares * (share_grad - across)).astype(BF16)
            found[1].append(dot32(score_grad, heads_of(qkv_s, i, 0, h), ((1,), (0,))) * inv_root)
            query_t = dot32(heads_of(qkv_s, i, 1, h), score_grad, ((0,), (0,))) * inv_root
            found[0].append(query_t.T)
        qkv_s[i] = jnp.concatenate([head for kind in found for head in kind], axis=1).astype(BF16)

    heads_back(0)
    half_copy.wait_recv()

    def out_core(g):
        return half_recv[rows_at(in_rows, g), :].astype(F32)

    out_sum = sum_start(out_spot, out_core, yrecv_out)
    sum_pass(down_sum, down_block, down_core, yrecv_down, zrecv_down, 0)
    for i in range(1, images):
        heads_back(i)

    def dqkv_rows(j):
        return qkv_s[:, pl.ds(pl.multiple_of(j * padded, padded), padded), :].reshape(rows, 3 * cols)

    def low_part(j):
        return dot32(dqkv_rows(j), qkv_w[...], ((1,), (1,)))

    part_s[0] = low_part(near[3]).astype(BF16)
    part_c = send(part_s.at[0], part_r.at[0], f, near[1])
    part_s[1] = low_part(near[1]).astype(BF16)
    part_d = send(part_s.at[1], part_r.at[1], f, near[1])
    for_x = low_part(near[2])
    part_c.wait_recv()
    part_s[2] = (for_x + part_r[0].astype(F32)).astype(BF16)
    part_x = send(part_s.at[2], part_r.at[2], f, near[2])
    sum_pass(up_sum, up_spot, up_core, yrecv_up, zrecv_up, 3)
    down_share = expert_sum_end(
        down_sum, down_block, yrecv_down, zrecv_down, down_all_at(xb), down_all_at(1 - xb), True
    )

    misfit[...] = low_part(s)

    qkv_flow.sent()
    qkv_grad = jnp.zeros((features, 3 * cols), F32)
    for i in range(images):
        given = low_all[:, i * padded : (i + 1) * padded, :].reshape(4 * padded, features)
        qkv_grad = qkv_grad + dot32(given, qkv_s[i], ((0,), (0,)))
    qkv_w[...] = qkv_grad.astype(BF16)
    qkv_sum = sum_start(qkv_spot, None, yrecv_qkv)
    sum_pass(up_sum, up_spot, up_core, yrecv_up, zrecv_up, 2)

    part_d.wait_recv()
    low_grad = misfit[...] + part_r[1].astype(F32)
    part_x.wait_recv()
    low_grad = low_grad + part_r[2].astype(F32)
    misfit[...] = low_grad
    stats[BIAS_ONE : BIAS_ONE + 1, :] = jnp.sum(low_grad, axis=0, keepdims=True)
    gain_grad = jnp.zeros((1, features), F32)
    for i in range(images):
        at = slice(i * padded, i * padded + piece)
        unit, root = unit_rows(x_in[:, i, :])
        gain_grad = gain_grad + jnp.sum(misfit[at, :] * unit, axis=0, keepdims=True)
        input_grad[:, i, :] = middle[at, :] + norm_back(misfit[at, :], unit, root, vecs[GAIN_ONE : GAIN_ONE + 1, :])
    stats[GAIN_ONE : GAIN_ONE + 1, :] = gain_grad

    seq_copies = [send(stats, stats_r.at[r - 1], f, near[r]) for r in (1, 2, 3)]
    down_last = share_pass(down_share)
    sum_pass(up_sum, up_spot, up_core, yrecv_up, zrecv_up, 1)
    for copy in seq_copies:
        copy.wait_recv()
        done_sending(copy)
    stats[...] = stats[...] + stats_r[0] + stats_r[1] + stats_r[2]
    y_copy = send(stats, stats_r.at[3], other[0], s)
    sum_pass(up_sum, up_spot, up_core, yrecv_up, zrecv_up, 0)
    for k in (3, 2, 1, 0):
        sum_pass(out_sum, out_spot, out_core, yrecv_out, zrecv_out, k)
    up_share = expert_sum_end(up_sum, up_spot, yrecv_up, zrecv_up, up_all_at(xb), up_all_at(1 - xb), False)
    for k in (3, 2):
        sum_pass(qkv_sum, qkv_spot, None, yrecv_qkv, zrecv_qkv, k)
    out_share = sum_end(out_sum, out_spot, zrecv_out, out_all)
    for k in (1, 0):
        sum_pass(qkv_sum, qkv_spot, None, yrecv_qkv, zrecv_qkv, k)
    y_copy.wait_recv()
    done_sending(y_copy)
    stats[...] = stats[...] + stats_r[3]
    z_copies = [send(stats, stats_r.at[3 + k], same[k], s) for k in (1, 2, 3)]
    up_last = share_pass(up_share)
    out_last = share_pass(out_share)
    qkv_share = sum_end(qkv_sum, qkv_spot, zrecv_qkv, qkv_all)
    for copy in z_copies:
        copy.wait_recv()
    stats_out[...] = stats[...] + stats_r[4] + stats_r[5] + stats_r[6]
    qkv_last = share_pass(qkv_share)
    for shared, last in (
        (down_share, down_last),
        (up_share, up_last),
        (out_share, out_last),
        (qkv_share, qkv_last),
    ):
        shared[1].wait_recv()
        shared[2].wait()
        last.wait_recv()
    for copy in list(pending):
        done_sending(copy)


def run_block(sizes, operands):
    images, piece, padded, cap, features, cols, ffn, in_rows, out_rows = sizes
    rows = images * padded
    half_cols, half_ffn = features // 2, ffn // 2
    shape = jax.ShapeDtypeStruct
    vmem = pl.BlockSpec(memory_space=pltpu.VMEM)
    hbm = pl.BlockSpec(memory_space=pl.ANY)
    scratch = [
        pltpu.VMEM((8, STATS, 128), BF16),
        pltpu.VMEM((STATS, features), F32),
        pltpu.VMEM((8 * in_rows, 3 * cols), BF16),
        pltpu.VMEM((features, features), BF16),
        pltpu.VMEM((features, ffn), BF16),
        pltpu.VMEM((ffn, features), BF16),
        pltpu.VMEM((4, rows, features), BF16),
        pltpu.VMEM((images, 4 * padded, 3 * cols), BF16),
        pltpu.VMEM((images, 8, 4 * padded), F32),
        pltpu.VMEM((images, 4 * padded, cols), BF16),
        pltpu.VMEM((4, images, padded, cols), BF16),
        pltpu.VMEM((rows, features), F32),
        pltpu.VMEM((rows, features), F32),
        pltpu.VMEM((rows, features), BF16),
        pltpu.VMEM((4, cap, rows), BF16),
        pltpu.VMEM((4, rows, cap), BF16),
        pltpu.VMEM((rows, LANES + 1), F32),
        pltpu.VMEM((rows, LANES), F32),
        pltpu.VMEM((3, cap, features), BF16),
        pltpu.VMEM((4, cap, features), BF16),
        pltpu.VMEM((4, cap, features), BF16),
        pltpu.VMEM((4, cap, features), BF16),
        pltpu.VMEM((4, cap, features), BF16),
        pltpu.VMEM((features, 4 * cap), BF16),
        pltpu.VMEM((4 * cap, ffn), BF16),
        pltpu.VMEM((4 * cap, ffn), BF16),
        pltpu.VMEM((8, features, out_rows), BF16),
        pltpu.VMEM((8, half_cols, out_rows), BF16),
        pltpu.VMEM((4, half_cols, out_rows), BF16),
        pltpu.VMEM((4, in_rows, half_ffn), BF16),
        pltpu.VMEM((3, half_cols, out_rows), BF16),
        pltpu.VMEM((3, in_rows, half_ffn), BF16),
        pltpu.VMEM((3, images, padded, cols), BF16),
        pltpu.VMEM((features, half_cols), BF16),
        pltpu.VMEM((4, in_rows, 3 * cols), BF16),
        pltpu.VMEM((3, in_rows, 3 * cols), BF16),
        pltpu.VMEM((4, in_rows, half_cols), BF16),
        pltpu.VMEM((3, in_rows, half_cols), BF16),
        pltpu.VMEM((3, rows, features), BF16),
        pltpu.VMEM((3, rows, features), BF16),
        pltpu.VMEM((STATS, features), F32),
        pltpu.VMEM((7, STATS, features), F32),
        pltpu.SemaphoreType.DMA((168,)),
        pltpu.SemaphoreType.DMA((168,)),
        pltpu.SemaphoreType.DMA((16,)),
        pltpu.SemaphoreType.REGULAR,
    ]
    return pl.pallas_call(
        lambda *refs: block_kernel(sizes, *refs),
        out_shape=(
            shape((piece, images, features), F32),
            shape((piece, images, features), F32),
            shape((STATS, features), F32),
            shape((4, in_rows, 3 * cols), BF16),
            shape((4, in_rows, half_cols), BF16),
            shape((2, 2, in_rows, ffn), BF16),
            shape((2, 2, out_rows, features), BF16),
        ),
        in_specs=[vmem, vmem, pl.BlockSpec(memory_space=pltpu.SMEM), vmem, vmem, vmem, vmem, vmem, hbm, hbm],
        out_specs=(vmem, vmem, vmem, hbm, hbm, hbm, hbm),
        scratch_shapes=scratch,
        compiler_params=pltpu.CompilerParams(
            collective_id=0, has_side_effects=True, vmem_limit_bytes=64_500_000
        ),
        name="block",
    )(*operands)


def finish_kernel(
    sizes,
    counts,
    stats,
    qkv_all,
    out_all,
    up_all,
    down_all,
    loss,
    gain_one,
    bias_one,
    grad_qkv,
    grad_out,
    gain_two,
    bias_two,
    router,
    up,
    down,
):
    images, piece, padded, cap, features, cols, ffn, in_rows, out_rows = sizes
    half_cols = features // 2
    for e in range(EXPERTS):
        up[:, e, :] = up_all[e // 2, e % 2].astype(F32)
        down[:, e, :] = down_all[e // 2, e % 2].astype(F32)
    grad_out[:, 0:half_cols] = out_all[0].astype(F32) + out_all[2].astype(F32)
    grad_out[:, half_cols:] = out_all[1].astype(F32) + out_all[3].astype(F32)
    for kind in range(3):
        at = kind * cols
        grad_qkv[:, kind * features : (kind + 1) * features] = jnp.concatenate(
            [qkv_all[j, :, at : at + cols].astype(F32) for j in range(4)], axis=1
        )

    @pl.when(pl.program_id(0) == 0)
    def _():
        f = lax.axis_index("fsdp")
        own = jnp.zeros((STATS, in_rows), F32)
        for g in range(8):
            own = jnp.where(f == g, stats[:, g * in_rows : (g + 1) * in_rows], own)
        router[...] = own[0:EXPERTS, :]
        gain_one[...] = own[GAIN_ONE : GAIN_ONE + 1, :]
        bias_one[...] = own[BIAS_ONE : BIAS_ONE + 1, :]
        gain_two[...] = own[GAIN_TWO : GAIN_TWO + 1, :]
        bias_two[...] = own[BIAS_TWO : BIAS_TWO + 1, :]
        used = counts[0]
        for g in range(1, counts.shape[0]):
            used = used + counts[g]
        tokens = (used * SEQ_LEN).astype(F32) * features
        total = jnp.sum(stats[LOSS_ROW : LOSS_ROW + 1, :], axis=1, keepdims=True)
        loss[...] = total / tokens


def run_finish(sizes, image_counts, stats, qkv_all, out_all, up_all, down_all):
    images, piece, padded, cap, features, cols, ffn, in_rows, out_rows = sizes
    half_cols = features // 2
    steps = in_rows // 16
    tall = out_rows // steps
    shape = jax.ShapeDtypeStruct

    def whole(*dims):
        return pl.BlockSpec(dims, lambda i: (0,) * len(dims))

    row = whole(1, in_rows)
    return pl.pallas_call(
        lambda *refs: finish_kernel(sizes, *refs),
        grid=(steps,),
        out_shape=(
            shape((1, 1), F32),
            shape((1, in_rows), F32),
            shape((1, in_rows), F32),
            shape((in_rows, 3 * features), F32),
            shape((in_rows, features), F32),
            shape((1, in_rows), F32),
            shape((1, in_rows), F32),
            shape((EXPERTS, in_rows), F32),
            shape((in_rows, EXPERTS, ffn), F32),
            shape((out_rows, EXPERTS, features), F32),
        ),
        in_specs=[
            pl.BlockSpec(memory_space=pltpu.SMEM),
            whole(STATS, features),
            pl.BlockSpec((4, 16, 3 * cols), lambda i: (0, i, 0)),
            pl.BlockSpec((4, 16, half_cols), lambda i: (0, i, 0)),
            pl.BlockSpec((2, 2, 16, ffn), lambda i: (0, 0, i, 0)),
            pl.BlockSpec((2, 2, tall, features), lambda i: (0, 0, i, 0)),
        ],
        out_specs=(
            whole(1, 1),
            row,
            row,
            pl.BlockSpec((16, 3 * features), lambda i: (i, 0)),
            pl.BlockSpec((16, features), lambda i: (i, 0)),
            row,
            row,
            whole(EXPERTS, in_rows),
            pl.BlockSpec((16, EXPERTS, ffn), lambda i: (i, 0, 0)),
            pl.BlockSpec((tall, EXPERTS, features), lambda i: (i, 0, 0)),
        ),
        name="finish",
    )(image_counts, stats, qkv_all, out_all, up_all, down_all)


def on_device(
    block_in,
    teacher,
    image_counts,
    expert_ids,
    pair_keep,
    norm1_gain,
    norm1_bias,
    qkv_weight,
    out_weight,
    norm2_gain,
    norm2_bias,
    router_weight,
    expert_in,
    expert_out,
):
    arguments = (
        block_in, teacher, image_counts, expert_ids, pair_keep, norm1_gain, norm1_bias, qkv_weight,
        out_weight, norm2_gain, norm2_bias, router_weight, expert_in, expert_out,
    )
    images, piece_len, features = block_in.shape
    pieces = lax.axis_size("seq")
    groups = lax.axis_size("fsdp")
    in_rows, out_rows, ffn = expert_in.shape[0], expert_out.shape[0], expert_in.shape[2]
    if pieces != EXPERTS or groups != 8 or in_rows % 16 or in_rows > 128 or out_rows % 128:
        return on_device_plain(*arguments)
    s = lax.axis_index("seq")
    f = lax.axis_index("fsdp")
    rows = images * piece_len
    cols = HEADS // pieces * HD
    padded = round_up(piece_len, 16)
    cap = round_up(rows * TOPK * 9 // (EXPERTS * 8) + 1, 16)
    half_cols = features // 2

    vec = jnp.concatenate(
        [router_weight.T, jnp.stack([norm1_gain, norm1_bias, norm2_gain, norm2_bias], axis=0)], axis=0
    )
    vec = jnp.pad(vec, ((0, STATS - 8), (0, 128 - in_rows)))
    up_shard = lax.dynamic_slice(
        expert_in.reshape(in_rows, 2, 2, ffn), (0, 0, s // 2, lax.rem(s, 2) * (ffn // 2)), (in_rows, 2, 1, ffn // 2)
    ).transpose(1, 2, 0, 3).reshape(2, in_rows, ffn // 2)
    down_shard = lax.dynamic_slice(
        expert_out.reshape(out_rows, 2, 2, features),
        (0, 0, s // 2, lax.rem(s, 2) * half_cols),
        (out_rows, 2, 1, half_cols),
    ).transpose(1, 2, 0, 3).reshape(2, out_rows, half_cols)
    sizes = (images, piece_len, padded, cap, features, cols, ffn, in_rows, out_rows)
    block_out, input_grad, *sums = run_block(
        sizes,
        (
            block_in.transpose(1, 0, 2),
            teacher.transpose(1, 0, 2),
            image_counts,
            expert_ids[0].transpose(0, 2, 1),
            pair_keep[0].transpose(0, 2, 1),
            vec,
            qkv_weight,
            out_weight,
            up_shard,
            down_shard,
        ),
    )
    loss, gain_one, bias_one, grad_qkv, grad_out, gain_two, bias_two, router, up, down = run_finish(
        sizes, image_counts, *sums
    )
    return (
        block_out.transpose(1, 0, 2),
        loss.reshape(()),
        input_grad.transpose(1, 0, 2),
        gain_one.reshape(in_rows),
        bias_one.reshape(in_rows),
        grad_qkv,
        grad_out,
        gain_two.reshape(in_rows),
        bias_two.reshape(in_rows),
        router.T,
        up,
        down,
    )


def solution(mesh):
    return jax.shard_map(
        on_device,
        mesh=mesh,
        in_specs=(
            P("fsdp", "seq", None),
            P("fsdp", "seq", None),
            P(),
            P("seq", "fsdp", None, None),
            P("seq", "fsdp", None, None),
            P("fsdp"),
            P("fsdp"),
            P("fsdp", None),
            P("fsdp", None),
            P("fsdp"),
            P("fsdp"),
            P("fsdp", None),
            P("fsdp", None, None),
            P("fsdp", None, None),
        ),
        out_specs=(
            P("fsdp", "seq", None),
            P(),
            P("fsdp", "seq", None),
            P("fsdp"),
            P("fsdp"),
            P("fsdp", None),
            P("fsdp", None),
            P("fsdp"),
            P("fsdp"),
            P("fsdp", None),
            P("fsdp", None, None),
            P("fsdp", None, None),
        ),
        check_vma=False,
    )
```

```python
import jax
import jax.numpy as jnp
from jax import lax
from jax.experimental import pallas as pl
from jax.experimental.pallas import tpu as pltpu
from jax.sharding import PartitionSpec as P

HEADS = 12
HD = 64
SEQ_LEN = 577
EXPERTS = 4
TOPK = 2
NORM_EPS = 1e-06
PRECISE = lax.Precision.HIGHEST
F32 = jnp.float32
BF16 = jnp.bfloat16


def layer_norm(values_in, gain_vec, bias_vec):
    centered = values_in - jnp.mean(values_in, axis=-1, keepdims=True)
    variance = jnp.mean(centered * centered, axis=-1, keepdims=True)
    root = lax.rsqrt(variance + NORM_EPS)
    unit = centered * root
    return unit * gain_vec + bias_vec, unit, root


def layer_norm_back(grad_out, unit, root, gain_vec):
    scaled = grad_out * gain_vec
    return root * (
        scaled
        - jnp.mean(scaled, axis=-1, keepdims=True)
        - unit * jnp.mean(scaled * unit, axis=-1, keepdims=True)
    )


def slot_holds(piece_index, piece_len, seq_len, pieces):
    lengths = seq_len // pieces + (piece_index < seq_len % pieces).astype(jnp.int32)
    return jnp.arange(piece_len, dtype=jnp.int32)[None, :] < lengths[:, None]


def dot32(left, right, dims):
    return lax.dot_general(left, right, (dims, ((), ())), preferred_element_type=F32)


def on_device_plain(
    block_in,
    teacher,
    image_counts,
    expert_ids,
    pair_keep,
    norm1_gain,
    norm1_bias,
    qkv_weight,
    out_weight,
    norm2_gain,
    norm2_bias,
    router_weight,
    expert_in,
    expert_out,
):
    images, piece_len, features = block_in.shape
    pieces = lax.axis_size("seq")
    groups = lax.axis_size("fsdp")
    seq_place = lax.axis_index("seq")
    group_place = lax.axis_index("fsdp")
    rows = images * piece_len
    slots = pieces * piece_len
    heads_here = HEADS // pieces
    cols = heads_here * HD
    hidden_size = expert_in.shape[2]
    capacity = rows * TOPK * 9 // (EXPERTS * 8) + 1
    inv_root = HD ** (-0.5)
    in_rows = expert_in.shape[0]
    out_rows = expert_out.shape[0]

    small = jnp.concatenate(
        [
            jnp.stack([norm1_gain, norm1_bias, norm2_gain, norm2_bias], axis=1),
            router_weight,
            out_weight,
            lax.dynamic_index_in_dim(
                qkv_weight.reshape(-1, 3, pieces, cols), seq_place, 2, keepdims=False
            ).reshape(-1, 3 * cols),
        ],
        axis=1,
    )
    small_full = lax.all_gather(small, "fsdp", axis=0, tiled=True)
    gain_one, bias_one, gain_two, bias_two = [small_full[:, i].astype(F32) for i in range(4)]
    router_full = small_full[:, 4 : 4 + EXPERTS]
    out_full = small_full[:, 4 + EXPERTS : 4 + EXPERTS + features]
    qkv_here = small_full[:, 4 + EXPERTS + features :]
    up_here = lax.all_gather(
        lax.dynamic_index_in_dim(expert_in, seq_place, 1, keepdims=False), "fsdp", axis=0, tiled=True
    )
    down_here = lax.all_gather(
        lax.dynamic_index_in_dim(expert_out, seq_place, 1, keepdims=False), "fsdp", axis=0, tiled=True
    )

    own_slots = slot_holds(jnp.reshape(seq_place, (1,)), piece_len, SEQ_LEN, pieces).reshape(piece_len)
    key_ok = slot_holds(jnp.arange(pieces, dtype=jnp.int32), piece_len, SEQ_LEN, pieces).reshape(slots)
    group_count = jnp.sum(
        jnp.where(jnp.arange(image_counts.shape[0], dtype=jnp.int32) == group_place, image_counts, 0)
    )
    token_ok = (
        (jnp.arange(images, dtype=jnp.int32) < group_count)[:, None] & own_slots[None, :]
    ).reshape(rows)

    flat_in = block_in.reshape(rows, features)
    normed_one, unit_one, root_one = layer_norm(flat_in, gain_one, bias_one)
    low_one = normed_one.astype(BF16)
    low_all = lax.all_gather(low_one.reshape(images, piece_len, features), "seq", axis=1, tiled=True)
    projected = dot32(low_all, qkv_here, ((2,), (0,))).astype(BF16)
    by_heads = projected.reshape(images, slots, 3, heads_here, HD).transpose(2, 0, 3, 1, 4)
    queries, key_rows, value_rows = by_heads[0], by_heads[1], by_heads[2]
    scores = jnp.einsum("ihqd,ihkd->ihqk", queries, key_rows, preferred_element_type=F32) * inv_root
    scores = jnp.where(key_ok[None, None, None, :], scores, -1e30)
    raised = jnp.exp(scores - jnp.max(scores, axis=-1, keepdims=True))
    attn = raised / jnp.sum(raised, axis=-1, keepdims=True)
    attn_low = attn.astype(BF16)
    context = jnp.einsum("ihqk,ihkd->iqhd", attn_low, value_rows, preferred_element_type=F32).astype(BF16)
    context_rows = lax.all_to_all(
        context.reshape(images, slots, 1, cols), "seq", split_axis=1, concat_axis=2, tiled=True
    ).reshape(rows, features)
    middle = flat_in + dot32(context_rows, out_full, ((1,), (0,)))
    normed_two, unit_two, root_two = layer_norm(middle, gain_two, bias_two)
    low_two = normed_two.astype(BF16)
    probs = jax.nn.softmax(dot32(low_two, router_full, ((1,), (0,))), axis=-1)

    expert_rows = expert_ids.reshape(rows, TOPK)
    usable = (pair_keep.reshape(rows, TOPK) == 1) & token_ok[:, None]
    hit = jnp.any(
        (expert_rows[:, :, None] == jnp.arange(EXPERTS, dtype=jnp.int32)) & usable[:, :, None], axis=1
    )
    earlier = (jnp.arange(rows)[:, None] > jnp.arange(rows)[None, :]).astype(BF16)
    place = dot32(earlier, hit.astype(BF16), ((1,), (0,))).astype(jnp.int32)
    place = jnp.where(hit, place, -1)
    select = (place.T[:, None, :] == jnp.arange(capacity, dtype=jnp.int32)[None, :, None]).astype(BF16)
    weight = jnp.where(hit, probs, 0.0)

    dispatched = dot32(select, low_two, ((2,), (0,))).astype(BF16)
    arrived = lax.all_to_all(dispatched, "seq", split_axis=0, concat_axis=0, tiled=True)
    arrived = arrived.reshape(pieces * capacity, features)
    hidden = dot32(arrived, up_here, ((1,), (0,)))
    activated, gelu_back = jax.vjp(lambda u: jax.nn.gelu(u, approximate=False), hidden)
    low_act = activated.astype(BF16)
    returned = dot32(low_act, down_here, ((1,), (0,))).astype(BF16)
    returned = lax.all_to_all(
        returned.reshape(pieces, capacity, features), "seq", split_axis=0, concat_axis=0, tiled=True
    )
    picked = jnp.einsum("est,esd->etd", select, returned, preferred_element_type=F32)
    block_out = middle + jnp.sum(weight.T[:, :, None] * picked, axis=0)
    misfit = (block_out - teacher.reshape(rows, features)) * token_ok.astype(F32)[:, None]
    loss_here = jnp.sum(misfit * misfit)

    pair_grad = (weight.T[:, :, None] * misfit[None]).astype(BF16)
    returned_grad = jnp.einsum("est,etd->esd", select, pair_grad, preferred_element_type=F32).astype(BF16)
    prob_grad = jnp.where(hit, jnp.sum(picked * misfit[None], axis=2).T, 0.0)
    grad_arrived = lax.all_to_all(returned_grad, "seq", split_axis=0, concat_axis=0, tiled=True).reshape(
        pieces * capacity, features
    )
    hidden_grad = gelu_back(dot32(grad_arrived, down_here, ((1,), (1,))))[0].astype(BF16)
    grad_down = dot32(low_act, grad_arrived, ((0,), (0,))).astype(BF16)
    grad_up = dot32(arrived, hidden_grad, ((0,), (0,))).astype(BF16)
    dispatch_grad = dot32(hidden_grad, up_here, ((1,), (1,))).astype(BF16)
    dispatch_grad = lax.all_to_all(
        dispatch_grad.reshape(pieces, capacity, features), "seq", split_axis=0, concat_axis=0, tiled=True
    )
    owned_down = lax.psum_scatter(grad_down, "fsdp", scatter_dimension=0, tiled=True)
    owned_up = lax.psum_scatter(grad_up, "fsdp", scatter_dimension=0, tiled=True)

    logit_grad = probs * (prob_grad - jnp.sum(probs * prob_grad, axis=1, keepdims=True))
    grad_router = lax.dot_general(
        low_two.astype(F32), logit_grad, (((0,), (0,)), ((), ())), precision=PRECISE
    )
    normed_two_grad = jnp.einsum("est,esd->td", select, dispatch_grad, preferred_element_type=F32)
    normed_two_grad = normed_two_grad + lax.dot_general(
        logit_grad, router_full.astype(F32), (((1,), (1,)), ((), ())), precision=PRECISE
    )
    grad_gain_two = jnp.sum(normed_two_grad * unit_two, axis=0)
    grad_bias_two = jnp.sum(normed_two_grad, axis=0)
    middle_grad = misfit + layer_norm_back(normed_two_grad, unit_two, root_two, gain_two)
    attended_grad = middle_grad.astype(BF16)
    grad_out_w = dot32(context_rows, attended_grad, ((0,), (0,))).astype(BF16)
    context_grad = dot32(attended_grad, out_full, ((1,), (1,))).astype(BF16)
    heads_grad = lax.all_to_all(
        context_grad.reshape(images, piece_len, pieces, cols), "seq", split_axis=2, concat_axis=1, tiled=True
    ).reshape(images, slots, heads_here, HD)
    value_grad = jnp.einsum("ihqk,iqhd->ikhd", attn_low, heads_grad, preferred_element_type=F32)
    share_grad = jnp.einsum("iqhd,ihkd->ihqk", heads_grad, value_rows, preferred_element_type=F32)
    score_grad = (attn * (share_grad - jnp.sum(attn * share_grad, axis=-1, keepdims=True))).astype(BF16)
    query_grad = jnp.einsum("ihqk,ihkd->iqhd", score_grad, key_rows, preferred_element_type=F32) * inv_root
    key_grad = jnp.einsum("ihqk,ihqd->ikhd", score_grad, queries, preferred_element_type=F32) * inv_root
    heads_back = jnp.stack([query_grad, key_grad, value_grad], axis=2).astype(BF16)
    heads_back = heads_back.reshape(images * slots, 3 * cols)
    grad_qkv = dot32(low_all.reshape(images * slots, features), heads_back, ((0,), (0,))).astype(BF16)
    normed_one_part = dot32(heads_back, qkv_here, ((1,), (1,))).astype(BF16)
    normed_one_grad = lax.psum_scatter(
        normed_one_part.reshape(images, slots, features), "seq", scatter_dimension=1, tiled=True
    ).astype(F32).reshape(rows, features)
    grad_gain_one = jnp.sum(normed_one_grad * unit_one, axis=0)
    grad_bias_one = jnp.sum(normed_one_grad, axis=0)
    input_grad = middle_grad + layer_norm_back(normed_one_grad, unit_one, root_one, gain_one)

    out_share = lax.psum_scatter(grad_out_w, "seq", scatter_dimension=1, tiled=True)
    attn_owned = lax.psum_scatter(
        jnp.concatenate([grad_qkv, out_share], axis=1), "fsdp", scatter_dimension=0, tiled=True
    )
    loss_row = jnp.zeros((features,), F32).at[0].set(loss_here)
    vectors = jnp.concatenate(
        [jnp.stack([grad_gain_one, grad_bias_one, grad_gain_two, grad_bias_two, loss_row]), grad_router.T], axis=0
    )
    vectors = lax.psum(vectors, ("fsdp", "seq"))
    mean_loss = vectors[4, 0] / (
        (jnp.sum(image_counts, dtype=jnp.int32) * SEQ_LEN).astype(F32) * features
    )
    owned_vectors = lax.dynamic_slice_in_dim(vectors, group_place * in_rows, in_rows, axis=1)
    attn_whole = lax.all_gather(attn_owned, "seq", axis=0)
    grad_qkv_w = (
        attn_whole[:, :, : 3 * cols].reshape(pieces, in_rows, 3, cols).transpose(1, 2, 0, 3)
        .reshape(in_rows, 3 * features).astype(F32)
    )
    grad_out_whole = attn_whole[:, :, 3 * cols :].transpose(1, 0, 2).reshape(in_rows, features).astype(F32)
    grad_up_w = lax.all_gather(owned_up, "seq", axis=0).transpose(1, 0, 2).astype(F32)
    grad_down_w = lax.all_gather(owned_down, "seq", axis=0).transpose(1, 0, 2).astype(F32)
    return (
        block_out.reshape(images, piece_len, features),
        mean_loss,
        input_grad.reshape(images, piece_len, features),
        owned_vectors[0],
        owned_vectors[1],
        grad_qkv_w,
        grad_out_whole,
        owned_vectors[2],
        owned_vectors[3],
        owned_vectors[5:].T,
        grad_up_w,
        grad_down_w,
    )


MESH = pl.DeviceIdType.MESH
LANES = 16
STATS = 16
GAIN_ONE, BIAS_ONE, GAIN_TWO, BIAS_TWO = 4, 5, 6, 7
LOSS_ROW = 8


def round_up(value, step):
    return (value + step - 1) // step * step


def flipped(place, bits):
    low, high = lax.rem(place, 2), place // 2
    if bits % 2:
        low = 1 - low
    if bits // 2:
        high = 1 - high
    return high * 2 + low


def unit_rows(values_in):
    centered = values_in - jnp.mean(values_in, axis=1, keepdims=True)
    variance = jnp.mean(centered * centered, axis=1, keepdims=True)
    root = lax.rsqrt(variance + NORM_EPS)
    return centered * root, root


def norm_back(grad_out, unit, root, gain_row):
    scaled = grad_out * gain_row
    return root * (
        scaled
        - jnp.mean(scaled, axis=1, keepdims=True)
        - unit * jnp.mean(scaled * unit, axis=1, keepdims=True)
    )


def hi_lo(values_in):
    high = values_in.astype(BF16)
    return high, (values_in - high.astype(F32)).astype(BF16)


def block_kernel(
    sizes,
    x_in,
    teacher_in,
    counts,
    ids_in,
    keep_in,
    vec_in,
    qkv_in,
    out_in,
    up_own,
    up_odd,
    down_in,
    block_out,
    input_grad,
    stats_out,
    qkv_all,
    out_all,
    up_all,
    down_all,
    vec_all,
    vecs,
    qkv_w,
    out_w,
    up_w,
    down_w,
    low_all,
    qkv_s,
    lse_s,
    ctx_s,
    ctx_rows,
    middle,
    misfit,
    low_two,
    select,
    select_t,
    hits,
    weights,
    send_s,
    arrived,
    ret_r,
    back_r,
    dret_r,
    turned,
    act,
    slope,
    grad_down,
    core_down,
    yrecv_down,
    yrecv_up,
    zrecv_down,
    zrecv_up,
    dctx_s,
    half_recv,
    yrecv_qkv,
    zrecv_qkv,
    yrecv_out,
    zrecv_out,
    part_s,
    part_r,
    stats,
    stats_r,
    send_sem,
    recv_sem,
    local_sem,
    free_sem,
):
    images, piece, padded, cap, features, cols, ffn, in_rows, out_rows = sizes
    rows = images * padded
    slots = 4 * padded
    half_cols, half_ffn = features // 2, ffn // 2
    wide = ffn // 6
    f = lax.axis_index("fsdp")
    s = lax.axis_index("seq")
    z, y = f // 2, lax.rem(f, 2)
    inv_root = HD ** (-0.5)
    same = [flipped(z, k) * 2 + y for k in range(4)]
    other = [flipped(z, k) * 2 + (1 - y) for k in range(4)]
    near = [flipped(s, r) for r in range(4)]
    zb, xb, core = lax.rem(z, 2), s // 2, lax.rem(s, 2)
    named_by = [flipped(zb * 2 + xb, r) for r in range(4)]
    cluster = [(f, s), (f, near[2]), (same[1], s), (same[1], near[2])]
    counter = [0, 0]
    pending = []

    def send(src, dst, group, seq):
        i = counter[0]
        counter[0] += 1
        copy = pltpu.make_async_remote_copy(
            src_ref=src,
            dst_ref=dst,
            send_sem=send_sem.at[i],
            recv_sem=recv_sem.at[i],
            device_id=(group, seq),
            device_id_type=MESH,
        )
        copy.start()
        pending.append(copy)
        return copy

    def done_sending(copy):
        pending[:] = [other_copy for other_copy in pending if other_copy is not copy]
        copy.wait_send()

    def local(src, dst):
        i = counter[1]
        counter[1] += 1
        copy = pltpu.make_async_copy(src, dst, local_sem.at[i])
        copy.start()
        return copy

    barrier = pltpu.get_barrier_semaphore()
    for g in same[1:] + other:
        pl.semaphore_signal(barrier, inc=1, device_id=(g, s), device_id_type=MESH)
    for q in near[1:]:
        pl.semaphore_signal(barrier, inc=1, device_id=(f, q), device_id_type=MESH)
    pl.semaphore_signal(barrier, inc=1, device_id=cluster[3], device_id_type=MESH)
    pl.semaphore_wait(barrier, 11)

    vec_copies = [send(vec_in, vec_all.at[f], g, s) for g in same[1:] + other]
    vec_all[f] = vec_in[...]

    def rows_at(n, g):
        return pl.ds(pl.multiple_of(g * n, n), n)

    def lanes_at(n, half):
        return pl.ds(pl.multiple_of(half * n, n), n)

    def qkv_spot(g):
        return qkv_w.at[rows_at(in_rows, g), :]

    def out_spot(g):
        return out_w.at[rows_at(in_rows, g), lanes_at(half_cols, core)]

    def up_spot(g):
        return up_w.at[rows_at(in_rows, g), lanes_at(half_ffn, core)]

    def down_spot(g):
        return down_w.at[rows_at(out_rows, g), lanes_at(half_cols, core)]

    class Flow:
        def __init__(self, own, odd, spot, shared):
            self.own, self.spot, self.shared = own, spot, shared
            self.z = [None] + [send(odd if k % 2 else own, spot(f), same[k], s) for k in (1, 2, 3)]
            self.y, self.core, self.local = [], [], None

        def start(self):
            self.y.append(send(self.own, self.spot(f), other[0], s))
            if self.shared:
                self.core.append(send(self.own, self.spot(f), f, near[1]))

        def keep(self):
            self.local = local(self.own, self.spot(f))

        def forward(self, k):
            self.z[k].wait_recv()
            ref = self.spot(same[k])
            self.y.append(send(ref, ref, other[0], s))
            if self.shared:
                self.core.append(send(ref, ref, f, near[1]))

        def end(self):
            for k in range(4):
                self.y[k].wait_recv()
                if self.shared:
                    ref = self.spot(other[k])
                    self.core.append(send(ref, ref, f, near[1]))
            for copy in self.core:
                copy.wait_recv()
            if self.local is not None:
                self.local.wait()

        def sent(self):
            for copy in self.z[1:] + self.y + self.core:
                done_sending(copy)

    for kind in range(3):
        part = jnp.zeros((in_rows, cols), BF16)
        for j in range(4):
            at = kind * features + j * cols
            part = jnp.where(s == j, qkv_in[:, at : at + cols], part)
        qkv_w[rows_at(in_rows, f), kind * cols : (kind + 1) * cols] = part
    out_w[rows_at(in_rows, f), lanes_at(half_cols, core)] = out_in[:, lanes_at(half_cols, core)]
    qkv_flow = Flow(qkv_spot(f), qkv_spot(f), qkv_spot, False)
    qkv_flow.start()
    out_flow = Flow(out_spot(f), out_spot(f), out_spot, True)
    up_flow = Flow(up_own, up_odd, up_spot, True)
    down_flow = Flow(down_in.at[zb], down_in.at[1 - zb], down_spot, True)
    up_flow.keep()
    down_flow.keep()

    def near_of(shape, axis):
        at = lax.broadcasted_iota(jnp.int32, shape, axis)
        named = jnp.full(shape, -1, jnp.int32)
        for r in range(4):
            named = jnp.where(at == r, named_by[r], named)
        return named

    own_len = SEQ_LEN // 4 + jnp.where(s < SEQ_LEN % 4, 1, 0)
    at_piece = lax.broadcasted_iota(jnp.int32, (1, piece), 1)
    route_rows = jnp.zeros((rows, LANES), F32)
    route_cols = jnp.zeros((LANES, rows), F32)
    for i in range(images):
        ok = jnp.where((at_piece < own_len) & (i < counts[f]), 1.0, 0.0)
        facts = jnp.concatenate(
            [
                ids_in[i].astype(F32),
                jnp.where(keep_in[i] == 1, 1.0, 0.0) * ok,
                ok,
                jnp.zeros((LANES - 5, piece), F32),
            ],
            axis=0,
        ).astype(BF16)
        spread = jnp.where(
            lax.broadcasted_iota(jnp.int32, (piece, rows), 0) + i * padded
            == lax.broadcasted_iota(jnp.int32, (piece, rows), 1),
            1.0,
            0.0,
        ).astype(BF16)
        route_cols = route_cols + dot32(facts, spread, ((1,), (0,)))
        route_rows = route_rows + dot32(spread, facts, ((0,), (1,)))
    token_ok = route_rows[:, 4:5]
    hits[:, LANES:] = token_ok
    route_rows = route_rows.astype(jnp.int32)
    route_cols = route_cols.astype(jnp.int32)
    named = near_of((rows, LANES), 1)
    hit = ((route_rows[:, 0:1] == named) & (route_rows[:, 2:3] == 1)) | (
        (route_rows[:, 1:2] == named) & (route_rows[:, 3:4] == 1)
    )
    hit_f = jnp.where(hit, 1.0, 0.0)
    before = (
        lax.broadcasted_iota(jnp.int32, (rows, rows), 0) > lax.broadcasted_iota(jnp.int32, (rows, rows), 1)
    )
    before = jnp.where(before, 1.0, 0.0).astype(BF16)
    place = dot32(before, hit_f.astype(BF16), ((1,), (0,)))
    place = jnp.where(hit, place, -1.0)
    hits[:, 0:LANES] = hit_f
    named_t = near_of((LANES, rows), 0)
    hit_t = ((route_cols[0:1, :] == named_t) & (route_cols[2:3, :] == 1)) | (
        (route_cols[1:2, :] == named_t) & (route_cols[3:4, :] == 1)
    )
    hit_tf = jnp.where(hit_t, 1.0, 0.0).astype(BF16)
    place_t = dot32(hit_tf, before, ((1,), (1,)))
    place_t = jnp.where(hit_t, place_t, -1.0)
    slot_down = lax.broadcasted_iota(jnp.int32, (cap, rows), 0).astype(F32)
    slot_along = lax.broadcasted_iota(jnp.int32, (rows, cap), 1).astype(F32)
    for r in range(4):
        select[r] = jnp.where(place_t[r : r + 1, :] == slot_down, 1.0, 0.0).astype(BF16)
        select_t[r] = jnp.where(place[:, r : r + 1] == slot_along, 1.0, 0.0).astype(BF16)

    for copy in vec_copies:
        copy.wait_recv()
    at_row = lax.broadcasted_iota(jnp.int32, (128, features), 0)
    at_col = lax.broadcasted_iota(jnp.int32, (128, features), 1)
    total = jnp.zeros((STATS, features), F32)
    for g in range(8):
        spread = jnp.where((at_col - g * in_rows == at_row) & (at_row < in_rows), 1.0, 0.0).astype(BF16)
        total = total + dot32(vec_all[g], spread, ((1,), (0,)))
    vecs[...] = total

    low_all[s] = jnp.zeros((rows, features), BF16)
    low_x, low_c, low_d = [], [], []

    def image_of(j, i):
        return low_all.at[j, pl.ds(i * padded, padded), :]

    for i in range(images):
        unit, _ = unit_rows(x_in[:, i, :])
        low_all[s, i * padded : i * padded + piece, :] = (
            unit * vecs[GAIN_ONE : GAIN_ONE + 1, :] + vecs[BIAS_ONE : BIAS_ONE + 1, :]
        ).astype(BF16)
        low_x.append(send(image_of(s, i), image_of(s, i), f, near[2]))
        low_c.append(send(image_of(s, i), image_of(s, i), f, near[1]))

    for k in (1, 2, 3):
        qkv_flow.forward(k)
    for flow in (out_flow, up_flow, down_flow):
        flow.start()
    for i in range(images):
        low_x[i].wait_recv()
        low_d.append(send(image_of(near[2], i), image_of(near[2], i), f, near[1]))
    qkv_flow.end()

    def project(j):
        found = dot32(low_all[j], qkv_w[...], ((1,), (0,))).astype(BF16)
        for i in range(images):
            qkv_s[i, pl.ds(pl.multiple_of(j * padded, padded), padded), :] = found[
                i * padded : (i + 1) * padded, :
            ]

    project(s)
    for copy in low_c:
        copy.wait_recv()
    project(near[1])
    project(near[2])
    for k in (1, 2, 3):
        out_flow.forward(k)
    for copy in low_d:
        copy.wait_recv()
    project(near[3])

    key_at = lax.broadcasted_iota(jnp.int32, (slots, 1), 0)
    key_piece = jnp.zeros((slots, 1), jnp.int32)
    for j in range(1, 4):
        key_piece = key_piece + jnp.where(key_at >= j * padded, 1, 0)
    key_len = SEQ_LEN // 4 + jnp.where(key_piece < SEQ_LEN % 4, 1, 0)
    key_ok = key_at - key_piece * padded < key_len

    def heads_of(ref, i, kind, h):
        return ref[i, :, kind * cols + h * HD : kind * cols + (h + 1) * HD]

    def scores_of(i, h):
        found = dot32(heads_of(qkv_s, i, 1, h), heads_of(qkv_s, i, 0, h), ((1,), (1,))) * inv_root
        return jnp.where(key_ok, found, -1e30)

    def piece_rows(ref, j):
        return ref.at[:, pl.ds(pl.multiple_of(j * padded, padded), padded), :]

    @pl.loop(0, images)
    def _(i):
        found = []
        for h in range(cols // HD):
            scores = scores_of(i, h)
            highest = jnp.max(scores, axis=0, keepdims=True)
            raised = jnp.exp(scores - highest)
            total = jnp.sum(raised, axis=0, keepdims=True)
            shares = (raised * (1.0 / total)).astype(BF16)
            lse_s[i, h : h + 1, :] = highest + jnp.log(total)
            found.append(dot32(heads_of(qkv_s, i, 2, h), shares, ((0,), (0,))))
        ctx_s[i] = jnp.concatenate(found, axis=0).T.astype(BF16)

    ctx_copies = [send(piece_rows(ctx_s, near[r]), ctx_rows.at[s], f, near[r]) for r in (2, 3, 1)]
    ctx_rows[s] = ctx_s[:, pl.ds(pl.multiple_of(s * padded, padded), padded), :]
    out_flow.end()
    up_flow.forward(1)
    for copy in ctx_copies:
        copy.wait_recv()
        done_sending(copy)

    attended = jnp.zeros((rows, features), F32)
    for j in range(4):
        attended = attended + dot32(
            ctx_rows[j].reshape(rows, cols), out_w[j * cols : (j + 1) * cols, :], ((1,), (0,))
        )
    middle[...] = attended
    for i in range(images):
        at = slice(i * padded, i * padded + piece)
        middle[at, :] = middle[at, :] + x_in[:, i, :]
    unit, _ = unit_rows(middle[...])
    low_two[...] = (unit * vecs[GAIN_TWO : GAIN_TWO + 1, :] + vecs[BIAS_TWO : BIAS_TWO + 1, :]).astype(BF16)
    router = vecs[...].astype(BF16)

    def probs_of():
        logits = dot32(low_two[...], router, ((1,), (1,)))
        real = lax.broadcasted_iota(jnp.int32, (rows, LANES), 1) < EXPERTS
        logits = jnp.where(real, logits, -1e30)
        raised = jnp.exp(logits - jnp.max(logits, axis=1, keepdims=True))
        return raised / jnp.sum(raised, axis=1, keepdims=True)

    disp_copies = []
    for r in (1, 2, 3, 0):
        found = dot32(select[r], low_two[...], ((1,), (0,))).astype(BF16)
        if r:
            send_s[r - 1] = found
            disp_copies.append(send(send_s.at[r - 1], arrived.at[r], *cluster[r]))
        else:
            arrived[0] = found
    probs = probs_of()
    lane = lax.broadcasted_iota(jnp.int32, (rows, LANES), 1)
    chosen = jnp.zeros((rows, LANES), F32)
    for r in range(4):
        value = jnp.sum(jnp.where(lane == named_by[r], probs, 0.0), axis=1, keepdims=True)
        chosen = jnp.where(lane == r, value, chosen)
    weights[...] = chosen * hits[:, 0:LANES]

    up_flow.forward(2)
    up_flow.forward(3)
    down_flow.forward(1)
    up_flow.end()

    def expert_up(half):
        given = arrived[2 * half : 2 * half + 2].reshape(2 * cap, features)

        @pl.loop(0, 6)
        def _(t):
            tile = pl.ds(pl.multiple_of(t * wide, wide), wide)
            hidden = dot32(given, up_w[:, tile], ((1,), (0,)))
            phi = 0.5 * (1.0 + lax.erf(hidden * (2.0**-0.5)))
            at = slice(2 * half * cap, 2 * (half + 1) * cap)
            act[at, tile] = (hidden * phi).astype(BF16)
            slope[at, tile] = (phi + hidden * jnp.exp(-0.5 * hidden * hidden) * 0.3989422804014327).astype(BF16)

    disp_copies[0].wait_recv()
    expert_up(0)
    down_flow.forward(2)
    disp_copies[1].wait_recv()
    disp_copies[2].wait_recv()
    expert_up(1)
    down_flow.forward(3)
    for copy in disp_copies:
        done_sending(copy)
    down_flow.end()

    def to_rows(left, right, dims, half, dst):
        at = slice(2 * half * cap, 2 * (half + 1) * cap)
        found = dot32(left[at, :], right[...], dims).astype(BF16)
        out = []
        for r in (2 * half + 1, 2 * half):
            part = found[(r - 2 * half) * cap : (r - 2 * half + 1) * cap, :]
            if r:
                send_s[r - 1] = part
                out.append(send(send_s.at[r - 1], dst.at[r], *cluster[r]))
            else:
                dst[0] = part
        return out

    ret_copies = to_rows(act, down_w, ((1,), (0,)), 1, ret_r)
    ret_copies += to_rows(act, down_w, ((1,), (0,)), 0, ret_r)
    for i in range(images):
        at = slice(i * padded, i * padded + piece)
        misfit[at, :] = teacher_in[:, i, :]
        misfit[i * padded + piece : (i + 1) * padded, :] = jnp.zeros((padded - piece, features), F32)

    found = middle[...]
    for r in (0, 1, 2, 3):
        if r:
            ret_copies[{3: 0, 2: 1, 1: 2}[r]].wait_recv()
        found = found + weights[:, r : r + 1] * dot32(select_t[r], ret_r[r], ((1,), (0,)))
    for i in range(images):
        block_out[:, i, :] = found[i * padded : i * padded + piece, :]
    wrong = (found - misfit[...]) * hits[:, LANES:]
    misfit[...] = wrong
    for copy in ret_copies:
        done_sending(copy)
    dret_copies = []
    for r in (3, 2, 1, 0):
        pair = (weights[:, r : r + 1] * misfit[...]).astype(BF16)
        part = dot32(select[r], pair, ((1,), (0,))).astype(BF16)
        if r:
            send_s[r - 1] = part
            dret_copies.append(send(send_s.at[r - 1], dret_r.at[r], *cluster[r]))
        else:
            dret_r[0] = part
    stats[...] = jnp.zeros_like(stats)
    stats[LOSS_ROW : LOSS_ROW + 1, :] = jnp.sum(wrong * wrong, axis=0, keepdims=True)
    probs = probs_of()
    prob_grad = jnp.zeros((rows, LANES), F32)
    for r in range(4):
        picked = dot32(select_t[r], ret_r[r], ((1,), (0,)))
        value = jnp.sum(picked * misfit[...], axis=1, keepdims=True) * hits[:, r : r + 1]
        prob_grad = jnp.where(lane == named_by[r], value, prob_grad)
    logit_grad = probs * (prob_grad - jnp.sum(probs * prob_grad, axis=1, keepdims=True))
    high, low = hi_lo(logit_grad)
    router_grad = dot32(high, low_two[...], ((0,), (0,))) + dot32(low, low_two[...], ((0,), (0,)))
    stats[0:EXPERTS, :] = router_grad[0:EXPERTS, :]

    def down_back(r):
        at = slice(r * cap, (r + 1) * cap)

        @pl.loop(0, 6)
        def _(t, r=r, at=at):
            tile = pl.ds(pl.multiple_of(t * wide, wide), wide)
            found = dot32(dret_r[r], down_w[tile, :], ((1,), (1,)))
            slope[at, tile] = (found * slope[at, tile].astype(F32)).astype(BF16)

    down_back(0)
    for r in (1, 2):
        dret_copies[3 - r].wait_recv()
        down_back(r)
    dret_copies[0].wait_recv()
    turned[...] = dret_r[...].reshape(4 * cap, features).T

    def down_grads(half):
        rows_here = lanes_at(half_cols, half)

        @pl.loop(0, 8)
        def _(g):
            grad_down[g, rows_here, :] = dot32(
                turned[rows_here, :], act[:, rows_at(out_rows, g)], ((1,), (0,))
            ).astype(BF16)

    down_grads(1 - core)

    def half_at(ref, half, n):
        return ref.at[:, pl.ds(pl.multiple_of(half * n, n), n), :]

    core_copy = send(half_at(grad_down, 1 - core, half_cols), core_down, f, near[1])

    def down_block(g):
        return grad_down.at[g, pl.ds(pl.multiple_of(core * half_cols, half_cols), half_cols), :]

    def down_core(g):
        return core_down[g].astype(F32)

    def up_core(g):
        at = pl.ds(pl.multiple_of(lax.rem(g, 4) * in_rows, in_rows), in_rows)
        return act[at, pl.ds(pl.multiple_of(g // 4 * half_ffn, half_ffn), half_ffn)].astype(F32)

    def sum_start(block, extra, yrecv):
        flow = {}
        for k in (3, 2, 1, 0):
            ref = block(other[k])
            if extra is not None:
                ref[...] = (ref[...].astype(F32) + extra(other[k])).astype(BF16)
            flow[k] = send(ref, yrecv.at[k], other[0], s)
        return flow

    def sum_pass(flow, block, extra, yrecv, zrecv, k):
        flow[k].wait_recv()
        ref = block(same[k])
        total = ref[...].astype(F32) + yrecv[k].astype(F32)
        if extra is not None:
            total = total + extra(same[k])
        ref[...] = total.astype(BF16)
        if k:
            flow["z%d" % k] = send(ref, zrecv.at[k - 1], same[k], s)

    def sum_end(flow, block, zrecv, dst):
        ref = block(f)
        for k in (1, 2, 3):
            flow["z%d" % k].wait_recv()
        total = ref[...].astype(F32)
        for k in (1, 2, 3):
            total = total + zrecv[k - 1].astype(F32)
        ref[...] = total.astype(BF16)
        return share(ref, dst.at[s], dst.at[near[2]])

    def share(ref, own, of_x):
        return send(ref, own, f, near[2]), send(ref, own, f, near[1]), local(ref, own), of_x

    def expert_sum_end(flow, block, yrecv, zrecv, own, of_x, turn):
        for k in (1, 2, 3):
            flow["z%d" % k].wait_recv()
        totals = (
            block(f)[...].astype(F32) + zrecv[1].astype(F32),
            zrecv[0].astype(F32) + zrecv[2].astype(F32),
        )
        for parity, total in zip((zb, 1 - zb), totals):
            yrecv[parity] = (total.T if turn else total).astype(BF16)
        return share(yrecv.at[pl.ds(0, 2)], own, of_x)

    def down_all_at(x):
        return down_all.at[:, x, :, pl.ds(pl.multiple_of(core * half_cols, half_cols), half_cols)]

    def up_all_at(x):
        return up_all.at[:, x, :, pl.ds(pl.multiple_of(core * half_ffn, half_ffn), half_ffn)]

    def share_pass(flow):
        flow[0].wait_recv()
        return send(flow[3], flow[3], f, near[1])

    for copy in dret_copies:
        done_sending(copy)
    down_back(3)
    down_grads(core)
    pl.semaphore_signal(free_sem, inc=1, device_id=(f, near[1]), device_id_type=MESH)
    core_copy.wait_recv()
    down_sum = sum_start(down_block, down_core, yrecv_down)
    back_copies = to_rows(slope, up_w, ((1,), (1,)), 1, back_r)
    back_copies += to_rows(slope, up_w, ((1,), (1,)), 0, back_r)
    up_flow.sent()
    turned[...] = arrived[...].reshape(4 * cap, features).T

    def up_grads(half):
        @pl.loop(0, 3)
        def _(t):
            tile = pl.ds(pl.multiple_of(half * half_ffn + t * wide, wide), wide)
            up_w[:, tile] = dot32(turned[...], slope[:, tile], ((1,), (0,))).astype(BF16)

    up_grads(1 - core)
    pl.semaphore_wait(free_sem, 1)
    up_copies = [
        send(
            up_w.at[pl.ds(h * 4 * in_rows, 4 * in_rows), lanes_at(half_ffn, 1 - core)],
            act.at[pl.ds(0, 4 * in_rows), pl.ds(h * half_ffn, half_ffn)],
            f,
            near[1],
        )
        for h in (0, 1)
    ]
    up_grads(core)
    sum_pass(down_sum, down_block, down_core, yrecv_down, zrecv_down, 3)
    for copy in up_copies:
        copy.wait_recv()
    up_sum = sum_start(up_spot, up_core, yrecv_up)
    for copy in up_copies:
        done_sending(copy)

    normed_grad = dot32(high, router, ((1,), (0,))) + dot32(low, router, ((1,), (0,)))
    for r in (0, 1, 2, 3):
        if r:
            back_copies[{3: 0, 2: 1, 1: 2}[r]].wait_recv()
        normed_grad = normed_grad + dot32(select_t[r], back_r[r], ((1,), (0,)))
    unit, root = unit_rows(middle[...])
    stats[GAIN_TWO : GAIN_TWO + 1, :] = jnp.sum(normed_grad * unit, axis=0, keepdims=True)
    stats[BIAS_TWO : BIAS_TWO + 1, :] = jnp.sum(normed_grad, axis=0, keepdims=True)
    middle_grad = misfit[...] + norm_back(normed_grad, unit, root, vecs[GAIN_TWO : GAIN_TWO + 1, :])
    middle[...] = middle_grad
    low_two[...] = middle_grad.astype(BF16)

    dctx_copies = []
    for r in (2, 3, 1, 0):
        block = out_w[pl.ds(pl.multiple_of(near[r] * cols, cols), cols), :]
        found = dot32(low_two[...], block, ((1,), (1,))).astype(BF16).reshape(images, padded, cols)
        if r:
            dctx_s[r - 1] = found
            dctx_copies.append(send(dctx_s.at[r - 1], piece_rows(ctx_s, s), f, near[r]))
        else:
            ctx_s[:, pl.ds(pl.multiple_of(s * padded, padded), padded), :] = found
    out_flow.sent()
    sum_pass(down_sum, down_block, down_core, yrecv_down, zrecv_down, 2)
    for j in range(4):
        out_w[j * cols : (j + 1) * cols, :] = dot32(
            ctx_rows[j].reshape(rows, cols), low_two[...], ((0,), (0,))
        ).astype(BF16)
    half_copy = send(out_w.at[:, lanes_at(half_cols, 1 - core)], half_recv, f, near[1])
    sum_pass(down_sum, down_block, down_core, yrecv_down, zrecv_down, 1)
    for copy in dctx_copies:
        copy.wait_recv()

    def heads_back(i):
        found = [[], [], []]
        for h in range(cols // HD):
            shares = jnp.exp(scores_of(i, h) - lse_s[i, h : h + 1, :])
            given = ctx_s[i, :, h * HD : (h + 1) * HD]
            found[2].append(dot32(shares.astype(BF16), given, ((1,), (0,))))
            share_grad = dot32(heads_of(qkv_s, i, 2, h), given, ((1,), (1,)))
            across = jnp.sum(shares * share_grad, axis=0, keepdims=True)
            score_grad = (shares * (share_grad - across)).astype(BF16)
            found[1].append(dot32(score_grad, heads_of(qkv_s, i, 0, h), ((1,), (0,))) * inv_root)
            query_t = dot32(heads_of(qkv_s, i, 1, h), score_grad, ((0,), (0,))) * inv_root
            found[0].append(query_t.T)
        qkv_s[i] = jnp.concatenate([head for kind in found for head in kind], axis=1).astype(BF16)

    heads_back(0)
    half_copy.wait_recv()

    def out_core(g):
        return half_recv[rows_at(in_rows, g), :].astype(F32)

    out_sum = sum_start(out_spot, out_core, yrecv_out)
    sum_pass(down_sum, down_block, down_core, yrecv_down, zrecv_down, 0)
    for i in range(1, images):
        heads_back(i)

    def dqkv_rows(j):
        return qkv_s[:, pl.ds(pl.multiple_of(j * padded, padded), padded), :].reshape(rows, 3 * cols)

    def low_part(j):
        return dot32(dqkv_rows(j), qkv_w[...], ((1,), (1,)))

    part_s[0] = low_part(near[3]).astype(BF16)
    part_c = send(part_s.at[0], part_r.at[0], f, near[1])
    part_s[1] = low_part(near[1]).astype(BF16)
    part_d = send(part_s.at[1], part_r.at[1], f, near[1])
    for_x = low_part(near[2])
    part_c.wait_recv()
    part_s[2] = (for_x + part_r[0].astype(F32)).astype(BF16)
    part_x = send(part_s.at[2], part_r.at[2], f, near[2])
    sum_pass(up_sum, up_spot, up_core, yrecv_up, zrecv_up, 3)
    down_share = expert_sum_end(
        down_sum, down_block, yrecv_down, zrecv_down, down_all_at(xb), down_all_at(1 - xb), True
    )

    misfit[...] = low_part(s)

    qkv_flow.sent()
    qkv_grad = jnp.zeros((features, 3 * cols), F32)
    for i in range(images):
        given = low_all[:, i * padded : (i + 1) * padded, :].reshape(4 * padded, features)
        qkv_grad = qkv_grad + dot32(given, qkv_s[i], ((0,), (0,)))
    qkv_w[...] = qkv_grad.astype(BF16)
    qkv_sum = sum_start(qkv_spot, None, yrecv_qkv)
    sum_pass(up_sum, up_spot, up_core, yrecv_up, zrecv_up, 2)

    part_d.wait_recv()
    low_grad = misfit[...] + part_r[1].astype(F32)
    part_x.wait_recv()
    low_grad = low_grad + part_r[2].astype(F32)
    misfit[...] = low_grad
    stats[BIAS_ONE : BIAS_ONE + 1, :] = jnp.sum(low_grad, axis=0, keepdims=True)
    gain_grad = jnp.zeros((1, features), F32)
    for i in range(images):
        at = slice(i * padded, i * padded + piece)
        unit, root = unit_rows(x_in[:, i, :])
        gain_grad = gain_grad + jnp.sum(misfit[at, :] * unit, axis=0, keepdims=True)
        input_grad[:, i, :] = middle[at, :] + norm_back(misfit[at, :], unit, root, vecs[GAIN_ONE : GAIN_ONE + 1, :])
    stats[GAIN_ONE : GAIN_ONE + 1, :] = gain_grad

    seq_copies = [send(stats, stats_r.at[r - 1], f, near[r]) for r in (1, 2, 3)]
    down_last = share_pass(down_share)
    sum_pass(up_sum, up_spot, up_core, yrecv_up, zrecv_up, 1)
    for copy in seq_copies:
        copy.wait_recv()
        done_sending(copy)
    stats[...] = stats[...] + stats_r[0] + stats_r[1] + stats_r[2]
    y_copy = send(stats, stats_r.at[3], other[0], s)
    sum_pass(up_sum, up_spot, up_core, yrecv_up, zrecv_up, 0)
    for k in (3, 2, 1, 0):
        sum_pass(out_sum, out_spot, out_core, yrecv_out, zrecv_out, k)
    up_share = expert_sum_end(up_sum, up_spot, yrecv_up, zrecv_up, up_all_at(xb), up_all_at(1 - xb), False)
    for k in (3, 2):
        sum_pass(qkv_sum, qkv_spot, None, yrecv_qkv, zrecv_qkv, k)
    out_share = sum_end(out_sum, out_spot, zrecv_out, out_all)
    for k in (1, 0):
        sum_pass(qkv_sum, qkv_spot, None, yrecv_qkv, zrecv_qkv, k)
    y_copy.wait_recv()
    done_sending(y_copy)
    stats[...] = stats[...] + stats_r[3]
    z_copies = [send(stats, stats_r.at[3 + k], same[k], s) for k in (1, 2, 3)]
    up_last = share_pass(up_share)
    out_last = share_pass(out_share)
    qkv_share = sum_end(qkv_sum, qkv_spot, zrecv_qkv, qkv_all)
    for copy in z_copies:
        copy.wait_recv()
    stats_out[...] = stats[...] + stats_r[4] + stats_r[5] + stats_r[6]
    qkv_last = share_pass(qkv_share)
    for shared, last in (
        (down_share, down_last),
        (up_share, up_last),
        (out_share, out_last),
        (qkv_share, qkv_last),
    ):
        shared[1].wait_recv()
        shared[2].wait()
        last.wait_recv()
    for copy in list(pending):
        done_sending(copy)


def run_block(sizes, operands):
    images, piece, padded, cap, features, cols, ffn, in_rows, out_rows = sizes
    rows = images * padded
    half_cols, half_ffn = features // 2, ffn // 2
    shape = jax.ShapeDtypeStruct
    vmem = pl.BlockSpec(memory_space=pltpu.VMEM)
    hbm = pl.BlockSpec(memory_space=pl.ANY)
    scratch = [
        pltpu.VMEM((8, STATS, 128), BF16),
        pltpu.VMEM((STATS, features), F32),
        pltpu.VMEM((8 * in_rows, 3 * cols), BF16),
        pltpu.VMEM((features, features), BF16),
        pltpu.VMEM((features, ffn), BF16),
        pltpu.VMEM((ffn, features), BF16),
        pltpu.VMEM((4, rows, features), BF16),
        pltpu.VMEM((images, 4 * padded, 3 * cols), BF16),
        pltpu.VMEM((images, 8, 4 * padded), F32),
        pltpu.VMEM((images, 4 * padded, cols), BF16),
        pltpu.VMEM((4, images, padded, cols), BF16),
        pltpu.VMEM((rows, features), F32),
        pltpu.VMEM((rows, features), F32),
        pltpu.VMEM((rows, features), BF16),
        pltpu.VMEM((4, cap, rows), BF16),
        pltpu.VMEM((4, rows, cap), BF16),
        pltpu.VMEM((rows, LANES + 1), F32),
        pltpu.VMEM((rows, LANES), F32),
        pltpu.VMEM((3, cap, features), BF16),
        pltpu.VMEM((4, cap, features), BF16),
        pltpu.VMEM((4, cap, features), BF16),
        pltpu.VMEM((4, cap, features), BF16),
        pltpu.VMEM((4, cap, features), BF16),
        pltpu.VMEM((features, 4 * cap), BF16),
        pltpu.VMEM((4 * cap, ffn), BF16),
        pltpu.VMEM((4 * cap, ffn), BF16),
        pltpu.VMEM((8, features, out_rows), BF16),
        pltpu.VMEM((8, half_cols, out_rows), BF16),
        pltpu.VMEM((4, half_cols, out_rows), BF16),
        pltpu.VMEM((4, in_rows, half_ffn), BF16),
        pltpu.VMEM((3, half_cols, out_rows), BF16),
        pltpu.VMEM((3, in_rows, half_ffn), BF16),
        pltpu.VMEM((3, images, padded, cols), BF16),
        pltpu.VMEM((features, half_cols), BF16),
        pltpu.VMEM((4, in_rows, 3 * cols), BF16),
        pltpu.VMEM((3, in_rows, 3 * cols), BF16),
        pltpu.VMEM((4, in_rows, half_cols), BF16),
        pltpu.VMEM((3, in_rows, half_cols), BF16),
        pltpu.VMEM((3, rows, features), BF16),
        pltpu.VMEM((3, rows, features), BF16),
        pltpu.VMEM((STATS, features), F32),
        pltpu.VMEM((7, STATS, features), F32),
        pltpu.SemaphoreType.DMA((168,)),
        pltpu.SemaphoreType.DMA((168,)),
        pltpu.SemaphoreType.DMA((16,)),
        pltpu.SemaphoreType.REGULAR,
    ]
    return pl.pallas_call(
        lambda *refs: block_kernel(sizes, *refs),
        out_shape=(
            shape((piece, images, features), F32),
            shape((piece, images, features), F32),
            shape((STATS, features), F32),
            shape((4, in_rows, 3 * cols), BF16),
            shape((4, in_rows, half_cols), BF16),
            shape((2, 2, in_rows, ffn), BF16),
            shape((2, 2, out_rows, features), BF16),
        ),
        in_specs=[vmem, vmem, pl.BlockSpec(memory_space=pltpu.SMEM), vmem, vmem, vmem, vmem, vmem, hbm, hbm, hbm],
        out_specs=(vmem, vmem, vmem, hbm, hbm, hbm, hbm),
        scratch_shapes=scratch,
        compiler_params=pltpu.CompilerParams(
            collective_id=0, has_side_effects=True, vmem_limit_bytes=64_500_000
        ),
        name="block",
    )(*operands)


def finish_kernel(
    sizes,
    counts,
    stats,
    qkv_all,
    out_all,
    up_all,
    down_all,
    loss,
    gain_one,
    bias_one,
    grad_qkv,
    grad_out,
    gain_two,
    bias_two,
    router,
    up,
    down,
):
    images, piece, padded, cap, features, cols, ffn, in_rows, out_rows = sizes
    half_cols = features // 2
    for e in range(EXPERTS):
        up[:, e, :] = up_all[e // 2, e % 2].astype(F32)
        down[:, e, :] = down_all[e // 2, e % 2].astype(F32)
    grad_out[:, 0:half_cols] = out_all[0].astype(F32) + out_all[2].astype(F32)
    grad_out[:, half_cols:] = out_all[1].astype(F32) + out_all[3].astype(F32)
    for kind in range(3):
        at = kind * cols
        grad_qkv[:, kind * features : (kind + 1) * features] = jnp.concatenate(
            [qkv_all[j, :, at : at + cols].astype(F32) for j in range(4)], axis=1
        )

    @pl.when(pl.program_id(0) == 0)
    def _():
        f = lax.axis_index("fsdp")
        own = jnp.zeros((STATS, in_rows), F32)
        for g in range(8):
            own = jnp.where(f == g, stats[:, g * in_rows : (g + 1) * in_rows], own)
        router[...] = own[0:EXPERTS, :]
        gain_one[...] = own[GAIN_ONE : GAIN_ONE + 1, :]
        bias_one[...] = own[BIAS_ONE : BIAS_ONE + 1, :]
        gain_two[...] = own[GAIN_TWO : GAIN_TWO + 1, :]
        bias_two[...] = own[BIAS_TWO : BIAS_TWO + 1, :]
        used = counts[0]
        for g in range(1, counts.shape[0]):
            used = used + counts[g]
        tokens = (used * SEQ_LEN).astype(F32) * features
        total = jnp.sum(stats[LOSS_ROW : LOSS_ROW + 1, :], axis=1, keepdims=True)
        loss[...] = total / tokens


def run_finish(sizes, image_counts, stats, qkv_all, out_all, up_all, down_all):
    images, piece, padded, cap, features, cols, ffn, in_rows, out_rows = sizes
    half_cols = features // 2
    steps = in_rows // 16
    tall = out_rows // steps
    shape = jax.ShapeDtypeStruct

    def whole(*dims):
        return pl.BlockSpec(dims, lambda i: (0,) * len(dims))

    row = whole(1, in_rows)
    return pl.pallas_call(
        lambda *refs: finish_kernel(sizes, *refs),
        grid=(steps,),
        out_shape=(
            shape((1, 1), F32),
            shape((1, in_rows), F32),
            shape((1, in_rows), F32),
            shape((in_rows, 3 * features), F32),
            shape((in_rows, features), F32),
            shape((1, in_rows), F32),
            shape((1, in_rows), F32),
            shape((EXPERTS, in_rows), F32),
            shape((in_rows, EXPERTS, ffn), F32),
            shape((out_rows, EXPERTS, features), F32),
        ),
        in_specs=[
            pl.BlockSpec(memory_space=pltpu.SMEM),
            whole(STATS, features),
            pl.BlockSpec((4, 16, 3 * cols), lambda i: (0, i, 0)),
            pl.BlockSpec((4, 16, half_cols), lambda i: (0, i, 0)),
            pl.BlockSpec((2, 2, 16, ffn), lambda i: (0, 0, i, 0)),
            pl.BlockSpec((2, 2, tall, features), lambda i: (0, 0, i, 0)),
        ],
        out_specs=(
            whole(1, 1),
            row,
            row,
            pl.BlockSpec((16, 3 * features), lambda i: (i, 0)),
            pl.BlockSpec((16, features), lambda i: (i, 0)),
            row,
            row,
            whole(EXPERTS, in_rows),
            pl.BlockSpec((16, EXPERTS, ffn), lambda i: (i, 0, 0)),
            pl.BlockSpec((tall, EXPERTS, features), lambda i: (i, 0, 0)),
        ),
        name="finish",
    )(image_counts, stats, qkv_all, out_all, up_all, down_all)


def on_device(
    block_in,
    teacher,
    image_counts,
    expert_ids,
    pair_keep,
    norm1_gain,
    norm1_bias,
    qkv_weight,
    out_weight,
    norm2_gain,
    norm2_bias,
    router_weight,
    expert_in,
    expert_out,
):
    arguments = (
        block_in, teacher, image_counts, expert_ids, pair_keep, norm1_gain, norm1_bias, qkv_weight,
        out_weight, norm2_gain, norm2_bias, router_weight, expert_in, expert_out,
    )
    images, piece_len, features = block_in.shape
    pieces = lax.axis_size("seq")
    groups = lax.axis_size("fsdp")
    in_rows, out_rows, ffn = expert_in.shape[0], expert_out.shape[0], expert_in.shape[2]
    if pieces != EXPERTS or groups != 8 or in_rows % 16 or in_rows > 128 or out_rows % 128:
        return on_device_plain(*arguments)
    s = lax.axis_index("seq")
    f = lax.axis_index("fsdp")
    rows = images * piece_len
    cols = HEADS // pieces * HD
    padded = round_up(piece_len, 16)
    cap = round_up(rows * TOPK * 9 // (EXPERTS * 8) + 1, 16)
    half_cols = features // 2

    vec = jnp.pad(router_weight.T, ((0, STATS - EXPERTS), (0, 128 - in_rows)))
    for at, row in (
        (GAIN_ONE, norm1_gain),
        (BIAS_ONE, norm1_bias),
        (GAIN_TWO, norm2_gain),
        (BIAS_TWO, norm2_bias),
    ):
        vec = vec + jnp.pad(row[None, :], ((at, STATS - 1 - at), (0, 128 - in_rows)))
    parity, chip, core = lax.rem(f // 2, 2), s // 2, lax.rem(s, 2)

    def up_of(expert):
        at = (0, expert, core * (ffn // 2))
        return lax.dynamic_slice(expert_in, at, (in_rows, 1, ffn // 2)).reshape(in_rows, ffn // 2)

    up_own, up_odd = up_of(parity * 2 + chip), up_of((1 - parity) * 2 + chip)
    down_shard = lax.dynamic_slice(
        expert_out.reshape(out_rows, 2, 2, features),
        (0, 0, s // 2, lax.rem(s, 2) * half_cols),
        (out_rows, 2, 1, half_cols),
    ).transpose(1, 2, 0, 3).reshape(2, out_rows, half_cols)
    sizes = (images, piece_len, padded, cap, features, cols, ffn, in_rows, out_rows)
    block_out, input_grad, *sums = run_block(
        sizes,
        (
            block_in.transpose(1, 0, 2),
            teacher.transpose(1, 0, 2),
            image_counts,
            expert_ids[0].transpose(0, 2, 1),
            pair_keep[0].transpose(0, 2, 1),
            vec,
            qkv_weight,
            out_weight,
            up_own,
            up_odd,
            down_shard,
        ),
    )
    loss, gain_one, bias_one, grad_qkv, grad_out, gain_two, bias_two, router, up, down = run_finish(
        sizes, image_counts, *sums
    )
    return (
        block_out.transpose(1, 0, 2),
        loss.reshape(()),
        input_grad.transpose(1, 0, 2),
        gain_one.reshape(in_rows),
        bias_one.reshape(in_rows),
        grad_qkv,
        grad_out,
        gain_two.reshape(in_rows),
        bias_two.reshape(in_rows),
        router.T,
        up,
        down,
    )


def solution(mesh):
    return jax.shard_map(
        on_device,
        mesh=mesh,
        in_specs=(
            P("fsdp", "seq", None),
            P("fsdp", "seq", None),
            P(),
            P("seq", "fsdp", None, None),
            P("seq", "fsdp", None, None),
            P("fsdp"),
            P("fsdp"),
            P("fsdp", None),
            P("fsdp", None),
            P("fsdp"),
            P("fsdp"),
            P("fsdp", None),
            P("fsdp", None, None),
            P("fsdp", None, None),
        ),
        out_specs=(
            P("fsdp", "seq", None),
            P(),
            P("fsdp", "seq", None),
            P("fsdp"),
            P("fsdp"),
            P("fsdp", None),
            P("fsdp", None),
            P("fsdp"),
            P("fsdp"),
            P("fsdp", None),
            P("fsdp", None, None),
            P("fsdp", None, None),
        ),
        check_vma=False,
    )
```
